32 devices in a mesh: ctx: 8 (over z, y), tp: 4 (over x, core).
Axes of the slice: x: 2, y: 2, z: 4, core: 2. Of those that a mesh axis runs over, the one named last changes fastest.
Arguments:
- streams: bfloat16 [3, 8192, 1024], P(None, 'tp', 'ctx'), may hold values from -6 to 6
- short_weight: float32 [3, 3, 8192], P(None, None, 'tp')
- filters: float32 [512, 1024], P('tp', 'ctx'), may hold values from -0.1875 to 0.1875
- skip_gain: float32 [8192], P('tp'), may hold values from -4 to 4
- norm_gain: float32 [8192], P('tp'), may hold values from 0.5 to 1.5
Outputs:
- block_out: bfloat16 [8192, 1024], P('tp', 'ctx')
The draws below stay inside these ranges and needn't reach their ends.
All inputs are finite; a program needn't handle non-finite values.
Results may differ from the reference program's by a relative error of at most 0.0064.
Values may be sent and summed in bfloat16 or wider, within the bound.
A program may use at most 64 MiB of HBM per device.

```python
import math
import jax
import jax.numpy as jnp
from jax import lax

GROUPS = 512
C = 8192
SHORT = 3
SEQ = 1024


def draw_short_weight(key, part):
    base = jax.random.normal(key, (SHORT, 3, C), jnp.float32) / math.sqrt(SHORT)
    span = math.log(3.0)
    place = jnp.arange(C).astype(jnp.float32) / (C - 1)
    ramp = jnp.exp(span * place - 0.5 * span)
    scale = jnp.concatenate([ramp[None, :], jnp.ones((2, C), jnp.float32)], axis=0)
    return base * scale[None, :, :]


def level_of(own_key, shape, cuts, smallest, top_value):
    loudness, own = 1.0, jax.random.fold_in(own_key, 6)
    for position, shards_of in cuts:
        heights = jnp.exp(jax.random.uniform(jax.random.fold_in(own, position), (shards_of,), jnp.float32, smallest / len(cuts), top_value / len(cuts)))
        loudness = loudness * jnp.repeat(heights, shape[position] // shards_of).reshape([-1 if axis == position else 1 for axis in range(len(shape))])
    return loudness


def gaussian(stream_key, shape, spread, limit, split=(), kind=jnp.bfloat16):
    level = level_of(stream_key, shape, split, -0.22, 0.18) if split else 1.0
    values = jax.random.normal(stream_key, shape, jnp.float32) * spread * level
    return jnp.minimum(jnp.maximum(values, -limit), limit).astype(kind)


def setup_inputs(seed: int = 0) -> dict:
    splits = jax.random.split(jax.random.key(seed), 6)
    streams = gaussian(splits[0], (3, C, SEQ), 1.0, 6.0, ((1, 4), (2, 8)))
    short_weight = draw_short_weight(jax.random.fold_in(splits[5], 71), 0)
    filters = gaussian(splits[2], (GROUPS, SEQ), SEQ ** -0.5, 0.1875, ((0, 4), (1, 8)), jnp.float32)
    skip_gain = gaussian(splits[3], (C,), 1.0, 4.0, ((0, 4),), jnp.float32)
    norm_gain = jnp.clip(1.0 + 0.1 * jax.random.normal(splits[4], (C,), jnp.float32), 0.5, 1.5)
    return {"streams": streams, "short_weight": short_weight, "filters": filters, "skip_gain": skip_gain, "norm_gain": norm_gain}


def reference(streams, short_weight, filters, skip_gain, norm_gain):
    values = streams.astype(jnp.float32)
    taps = short_weight.shape[0]
    length = values.shape[2]
    padded = jnp.pad(values, ((0, 0), (0, 0), (taps - 1, 0)))
    conv_streams = jnp.zeros(values.shape, jnp.float32)
    for offset in range(taps):
        start = taps - 1 - offset
        conv_streams = conv_streams + short_weight[offset][:, :, None] * padded[:, :, start:start + length]
    query = lax.optimization_barrier(conv_streams[0].astype(jnp.bfloat16)).astype(jnp.float32)
    product = lax.optimization_barrier((conv_streams[1] * conv_streams[2]).astype(jnp.bfloat16)).astype(jnp.float32)
    group_count = filters.shape[0]
    channel_count = product.shape[0]
    grouped = product.reshape(group_count, channel_count // group_count, length)

    def one_group(pair):
        block, taps_row = pair
        spectrum = jnp.fft.rfft(block, n=2 * length, axis=1) * jnp.fft.rfft(taps_row, n=2 * length)[None, :]
        return jnp.fft.irfft(spectrum, n=2 * length, axis=1)[:, :length]
    long_conv = lax.map(one_group, (grouped, filters)).reshape(channel_count, length)
    gated = (query * (long_conv + skip_gain[:, None] * product)).astype(jnp.bfloat16)
    gated_wide = lax.optimization_barrier(gated).astype(jnp.float32)
    rms = jnp.sqrt(lax.optimization_barrier(jnp.mean(gated_wide * gated_wide, axis=0)) + 1e-05)
    return (gated_wide * norm_gain[:, None] / rms[None, :]).astype(jnp.bfloat16)
```

```python
import functools
import math

import jax
import jax.numpy as jnp
from jax import lax
from jax.experimental import pallas as pl
from jax.experimental.pallas import tpu as pltpu
from jax.sharding import PartitionSpec as P

highest = lax.Precision.HIGHEST
MESH = pl.DeviceIdType.MESH


def causal_short(padded, weights, length):
    taps = weights.shape[0]
    total = jnp.zeros(padded.shape[:2] + (length,), jnp.float32)
    for offset in range(taps):
        start = taps - 1 - offset
        total = total + weights[offset][:, :, None] * padded[:, :, start : start + length]
    return total


def trig_tables(half_count, row_count):
    periods = 2 * half_count
    total_len = periods * row_count
    freq = lax.iota(jnp.int32, periods)[:, None]
    place = lax.iota(jnp.int32, half_count)[None, :]
    angle_one = (freq * place % periods).astype(jnp.float32) * (2.0 * math.pi / periods)
    cols = lax.iota(jnp.int32, row_count)
    angle_two = (cols[:, None] * cols[None, :] % row_count).astype(jnp.float32) * (
        2.0 * math.pi / row_count
    )
    angle_twist = (freq * cols[None, :] % total_len).astype(jnp.float32) * (
        2.0 * math.pi / total_len
    )
    return (
        jnp.cos(angle_one),
        jnp.sin(angle_one),
        jnp.cos(angle_two),
        jnp.sin(angle_two),
        jnp.cos(angle_twist),
        jnp.sin(angle_twist),
    )


def forward_dft(signal, tables):
    cos_one, sin_one, cos_two, sin_two, cos_tw, sin_tw = tables
    first_re = jnp.einsum("ka,cab->ckb", cos_one, signal, precision=highest)
    first_im = -jnp.einsum("ka,cab->ckb", sin_one, signal, precision=highest)
    turned_re = first_re * cos_tw + first_im * sin_tw
    turned_im = first_im * cos_tw - first_re * sin_tw
    out_re = jnp.einsum("ckb,bq->ckq", turned_re, cos_two, precision=highest) + jnp.einsum(
        "ckb,bq->ckq", turned_im, sin_two, precision=highest
    )
    out_im = jnp.einsum("ckb,bq->ckq", turned_im, cos_two, precision=highest) - jnp.einsum(
        "ckb,bq->ckq", turned_re, sin_two, precision=highest
    )
    return (out_re, out_im)


def inverse_dft(spec_re, spec_im, tables):
    cos_one, sin_one, cos_two, sin_two, cos_tw, sin_tw = tables
    back_re = jnp.einsum("ckq,qb->ckb", spec_re, cos_two, precision=highest) - jnp.einsum(
        "ckq,qb->ckb", spec_im, sin_two, precision=highest
    )
    back_im = jnp.einsum("ckq,qb->ckb", spec_re, sin_two, precision=highest) + jnp.einsum(
        "ckq,qb->ckb", spec_im, cos_two, precision=highest
    )
    turned_re = back_re * cos_tw - back_im * sin_tw
    turned_im = back_re * sin_tw + back_im * cos_tw
    result = jnp.einsum("ka,ckb->cab", cos_one, turned_re, precision=highest) - jnp.einsum(
        "ka,ckb->cab", sin_one, turned_im, precision=highest
    )
    total_len = 2 * cos_one.shape[1] * cos_two.shape[0]
    return result / total_len


def shards(streams, short_weight, filters, skip_gain, norm_gain):
    n_ctx = lax.axis_size("ctx")
    n_width = lax.axis_size("tp")
    tok_rows = streams.shape[2]
    local_chan = streams.shape[1]
    owned = local_chan // n_ctx
    owned_groups = filters.shape[0] // n_ctx
    per_group = owned // owned_groups
    seq_len = tok_rows * n_ctx
    taps = short_weight.shape[0]
    owner_start = lax.axis_index("ctx") * owned
    skip_own = lax.dynamic_slice_in_dim(skip_gain, owner_start, owned, 0)
    filter_own = lax.all_to_all(filters, "ctx", split_axis=0, concat_axis=1, tiled=True)
    raw_own = lax.all_to_all(streams, "ctx", split_axis=1, concat_axis=2, tiled=True)
    weight_own = lax.dynamic_slice_in_dim(short_weight, owner_start, owned, 2)
    padded = jnp.pad(raw_own.astype(jnp.float32), ((0, 0), (0, 0), (taps - 1, 0)))
    conv_own = causal_short(padded, weight_own, seq_len)
    query_own = lax.optimization_barrier(conv_own[0].astype(jnp.bfloat16)).astype(jnp.float32)
    value_own = lax.optimization_barrier((conv_own[1] * conv_own[2]).astype(jnp.bfloat16)).astype(
        jnp.float32
    )
    tables = trig_tables(n_ctx, tok_rows)
    value_re, value_im = forward_dft(value_own.reshape(owned, n_ctx, tok_rows), tables)
    filt_re, filt_im = forward_dft(filter_own.reshape(owned_groups, n_ctx, tok_rows), tables)
    spec_shape = (owned_groups, per_group) + value_re.shape[1:]
    value_re = value_re.reshape(spec_shape)
    value_im = value_im.reshape(spec_shape)
    filt_re = filt_re[:, None]
    filt_im = filt_im[:, None]
    spec_re = (value_re * filt_re - value_im * filt_im).reshape((owned,) + spec_shape[2:])
    spec_im = (value_re * filt_im + value_im * filt_re).reshape((owned,) + spec_shape[2:])
    long_conv = inverse_dft(spec_re, spec_im, tables).reshape(owned, seq_len)
    gated = (query_own * (long_conv + skip_own[:, None] * value_own)).astype(jnp.bfloat16)
    gated_rows = lax.all_to_all(gated, "ctx", split_axis=1, concat_axis=0, tiled=True)
    gated_wide = gated_rows.astype(jnp.float32)
    squares = lax.psum(jnp.sum(gated_wide * gated_wide, axis=0), "tp")
    rms = jnp.sqrt(squares / (local_chan * n_width) + 1e-05)
    return (gated_wide * norm_gain[:, None] / rms[None, :]).astype(jnp.bfloat16)


def rolled_order(n):
    return sorted(range(1, n), key=lambda r: (abs(2 * r - n), r))


def kernel(
    n,
    nt,
    n_chunks,
    st_hbm,
    sw_ref,
    filt_ref,
    skip_ref,
    gated_ref,
    rms_ref,
    st,
    halo_out,
    halo_in,
    halo_col,
    coef_row,
    coef_col,
    filt_out,
    filt_in,
    filt_f32,
    toep,
    prod,
    query,
    recv,
    res,
    back,
    sq_out,
    sq_in,
    load_sem,
    halo_send,
    halo_recv,
    filt_send,
    filt_recv,
    prod_send,
    prod_recv,
    res_send,
    res_recv,
    sq_send,
    sq_recv,
):
    bf16, f32 = jnp.bfloat16, jnp.float32
    me = lax.axis_index("ctx")
    tp = lax.axis_index("tp")
    taps = sw_ref.shape[0]
    own, width = st.shape[2], st.shape[3]
    chan = n * own
    owned_groups = filt_in.shape[1]
    per_group = own // owned_groups
    rows = own // n_chunks
    order = rolled_order(n)

    loads = [pltpu.make_async_copy(st_hbm.at[s], st.at[s], load_sem.at[s]) for s in range(3)]
    for load in loads:
        load.start()

    barrier = pltpu.get_barrier_semaphore()
    for r in range(1, n):
        pl.semaphore_signal(
            barrier, inc=1, device_id=(lax.rem(me + r, n), tp), device_id_type=MESH
        )
    for r in range(1, nt):
        pl.semaphore_signal(
            barrier, inc=1, device_id=(me, lax.rem(tp + r, nt)), device_id_type=MESH
        )
    filt_out[...] = filt_ref[...].astype(bf16)
    coef_row[...] = jnp.zeros_like(coef_row)
    for j in range(taps):
        for s in range(3):
            coef_row[3 * j + s : 3 * j + s + 1, :] = sw_ref[j, s : s + 1, :]
    coef_row[3 * taps : 3 * taps + 1, :] = skip_ref[...]
    coef_col[...] = coef_row[...].T.reshape(coef_col.shape)
    for load in loads:
        load.wait()
    halo = jnp.zeros((16, chan), f32)
    row_id = lax.broadcasted_iota(jnp.int32, (16, width), 0)
    lane_id = lax.broadcasted_iota(jnp.int32, (16, width), 1)
    for s in range(3):
        pick = (lane_id >= width - 2) & (row_id == 2 * s + lane_id - (width - 2))
        halo = halo + lax.dot_general(
            pick.astype(f32).astype(bf16),
            st[s].reshape(chan, width),
            (((1,), (1,)), ((), ())),
            preferred_element_type=f32,
        )
    halo_out[...] = halo.astype(bf16)

    pl.semaphore_wait(barrier, n - 1 + nt - 1)

    halo_copy = pltpu.make_async_remote_copy(
        src_ref=halo_out,
        dst_ref=halo_in,
        send_sem=halo_send,
        recv_sem=halo_recv,
        device_id=(lax.rem(me + 1, n), tp),
        device_id_type=MESH,
    )

    @pl.when(me < n - 1)
    def _():
        halo_copy.start()

    def filt_copy(r):
        to = lax.rem(me + r, n)
        return pltpu.make_async_remote_copy(
            src_ref=filt_out.at[pl.ds(pl.multiple_of(to * owned_groups, owned_groups), owned_groups)],
            dst_ref=filt_in.at[me],
            send_sem=filt_send.at[r],
            recv_sem=filt_recv.at[r],
            device_id=(to, tp),
            device_id_type=MESH,
        )

    for r in order:
        filt_copy(r).start()
    filt_in[me] = filt_out[pl.ds(pl.multiple_of(me * owned_groups, owned_groups), owned_groups), :]

    @pl.when(me == 0)
    def _():
        halo_in[...] = jnp.zeros_like(halo_in)

    @pl.when(me > 0)
    def _():
        halo_copy.wait_recv()

    wide = jnp.concatenate([halo_in[...].astype(f32), jnp.zeros((width - 16, chan), f32)], axis=0)
    halo_col[...] = wide.T.astype(bf16).reshape(halo_col.shape)

    def prod_copy(q, r):
        to = lax.rem(me + r, n)
        part = pl.ds(q * rows, rows)
        return pltpu.make_async_remote_copy(
            src_ref=prod.at[to, part],
            dst_ref=recv.at[me, part],
            send_sem=prod_send.at[q, r],
            recv_sem=prod_recv.at[q, r],
            device_id=(to, tp),
            device_id_type=MESH,
        )

    def res_copy(q, r):
        to = lax.rem(me + r, n)
        part = pl.ds(q * rows, rows)
        return pltpu.make_async_remote_copy(
            src_ref=res.at[to, part],
            dst_ref=back.at[me, part],
            send_sem=res_send.at[q, r],
            recv_sem=res_recv.at[q, r],
            device_id=(to, tp),
            device_id_type=MESH,
        )

    k_id = lax.broadcasted_iota(jnp.int32, (2 * width, 2 * width), 0)
    m_id = lax.broadcasted_iota(jnp.int32, (2 * width, 2 * width), 1)
    shift = jnp.where(m_id < width, 1, 2)
    m_in = jnp.where(m_id < width, m_id, m_id - width)
    for q in range(n_chunks):
        part = slice(q * rows, (q + 1) * rows)
        coef = coef_col[:, part, :].reshape(n * rows, coef_col.shape[2])
        conv = []
        for s in range(3):
            inner = (k_id < width) & (k_id == m_in - shift)
            outer = (k_id >= width) & (m_in < shift) & (k_id - width == 2 * s + 2 + m_in - shift)
            mover = (inner | outer).astype(f32).astype(bf16)
            now = st[s, :, part, :].reshape(n * rows, width)
            both = jnp.concatenate(
                [now, halo_col[:, part, :].reshape(n * rows, width)], axis=1
            )
            moved = jnp.dot(both, mover, preferred_element_type=f32)
            conv.append(
                coef[:, s : s + 1] * now.astype(f32)
                + coef[:, 3 + s : 4 + s] * moved[:, :width]
                + coef[:, 6 + s : 7 + s] * moved[:, width:]
            )
        query[:, part, :] = conv[0].astype(bf16).reshape(n, rows, width)
        prod[:, part, :] = (conv[1] * conv[2]).astype(bf16).reshape(n, rows, width)
        for r in order:
            prod_copy(q, r).start()
        recv[me, part, :] = prod[me, part, :]

    for r in order:
        filt_copy(r).wait_recv()
    filt_f32[...] = filt_in[...].astype(f32)
    t_id = lax.broadcasted_iota(jnp.int32, (width, width), 1)
    s_id = lax.broadcasted_iota(jnp.int32, (width, width), 0)

    @pl.loop(0, owned_groups)
    def _(g):
        line = jnp.concatenate([filt_f32[j, pl.ds(g, 1), :] for j in range(n)], axis=1)
        line = jnp.broadcast_to(line, (width, n * width))
        turned = pltpu.roll(line, 0, 1, stride=1, stride_axis=0)
        toep[g, :, width:] = turned[:, width:].astype(bf16)
        toep[g, :, :width] = jnp.where(t_id >= s_id, turned[:, :width], 0.0).astype(bf16)

    for q in range(n_chunks):
        for r in order:
            prod_copy(q, r).wait_recv()
        per_chunk = rows // per_group

        @pl.loop(0, per_chunk)
        def _(k):
            place = pl.ds(pl.multiple_of(q * rows + k * per_group, per_group), per_group)
            block = recv[:, place, :].reshape(n * per_group, width)
            full = jnp.dot(block, toep[q * per_chunk + k], preferred_element_type=f32)
            for i in range(n):
                total = full[:per_group, i * width : (i + 1) * width]
                for j in range(1, i + 1):
                    total = total + full[
                        j * per_group : (j + 1) * per_group, (i - j) * width : (i - j + 1) * width
                    ]
                res[i, place, :] = total.astype(bf16)

        for r in order:
            res_copy(q, r).start()
        part = slice(q * rows, (q + 1) * rows)
        back[me, part, :] = res[me, part, :]

    squares = jnp.zeros((8, width), f32)
    for q in range(n_chunks):
        part = slice(q * rows, (q + 1) * rows)
        for r in order:
            res_copy(q, r).wait_recv()
        skip = coef_col[:, part, :].reshape(n * rows, coef_col.shape[2])[:, 3 * taps : 3 * taps + 1]
        direct = skip * prod[:, part, :].reshape(n * rows, width).astype(f32)
        far = back[:, part, :].reshape(n * rows, width).astype(f32)
        gated = (query[:, part, :].reshape(n * rows, width).astype(f32) * (far + direct)).astype(bf16)
        gated_ref[:, part, :] = gated.reshape(n, rows, width)
        gated = gated.astype(f32)
        squares = squares + jnp.sum((gated * gated).reshape(n * rows // 8, 8, width), axis=0)
    sq_out[...] = squares

    def sq_copy(r):
        return pltpu.make_async_remote_copy(
            src_ref=sq_out,
            dst_ref=sq_in.at[tp],
            send_sem=sq_send.at[r],
            recv_sem=sq_recv.at[r],
            device_id=(me, lax.rem(tp + r, nt)),
            device_id_type=MESH,
        )

    for r in range(1, nt):
        sq_copy(r).start()
    sq_in[tp] = squares
    for r in order:
        filt_copy(r).wait_send()
        for q in range(n_chunks):
            prod_copy(q, r).wait_send()
            res_copy(q, r).wait_send()

    @pl.when(me < n - 1)
    def _():
        halo_copy.wait_send()

    for r in range(1, nt):
        sq_copy(r).wait_recv()
    total = jnp.sum(jnp.sum(sq_in[...], axis=0), axis=0, keepdims=True)
    rms_ref[...] = jnp.sqrt(total / (chan * nt) + 1e-05)
    for r in range(1, nt):
        sq_copy(r).wait_send()


def fused_shards(streams, short_weight, filters, skip_gain, norm_gain):
    n = lax.axis_size("ctx")
    nt = lax.axis_size("tp")
    chan, width = streams.shape[1:]
    own = chan // n
    owned_groups = filters.shape[0] // n
    n_chunks = 4
    bf16, f32 = jnp.bfloat16, jnp.float32
    vmem = pl.BlockSpec(memory_space=pltpu.VMEM)
    dma = pltpu.SemaphoreType.DMA
    slab = pltpu.VMEM((n, own, width), bf16)
    gated, rms = pl.pallas_call(
        functools.partial(kernel, n, nt, n_chunks),
        out_shape=(
            jax.ShapeDtypeStruct((n, own, width), bf16),
            jax.ShapeDtypeStruct((1, width), f32),
        ),
        in_specs=[pl.BlockSpec(memory_space=pl.ANY), vmem, vmem, vmem],
        out_specs=(vmem, vmem),
        scratch_shapes=[
            pltpu.VMEM((3, n, own, width), bf16),
            pltpu.VMEM((16, chan), bf16),
            pltpu.VMEM((16, chan), bf16),
            slab,
            pltpu.VMEM((128, chan), f32),
            pltpu.VMEM((n, own, 128), f32),
            pltpu.VMEM((filters.shape[0], width), bf16),
            pltpu.VMEM((n, owned_groups, width), bf16),
            pltpu.VMEM((n, owned_groups, width), f32),
            pltpu.VMEM((owned_groups, width, n * width), bf16),
            slab,
            slab,
            slab,
            slab,
            slab,
            pltpu.VMEM((8, width), f32),
            pltpu.VMEM((nt, 8, width), f32),
            dma((3,)),
            dma,
            dma,
            dma((n,)),
            dma((n,)),
            dma((n_chunks, n)),
            dma((n_chunks, n)),
            dma((n_chunks, n)),
            dma((n_chunks, n)),
            dma((nt,)),
            dma((nt,)),
        ],
        compiler_params=pltpu.CompilerParams(
            collective_id=0, has_side_effects=True, vmem_limit_bytes=40 * 1024 * 1024
        ),
        name="hyena",
    )(
        streams.reshape(3, n, own, width),
        short_weight,
        filters,
        skip_gain.reshape(1, chan),
    )
    wide = gated.reshape(chan, width).astype(f32)
    return (wide * norm_gain[:, None] / rms).astype(bf16)


def solution(mesh):
    in_specs = (P(None, "tp", "ctx"), P(None, None, "tp"), P("tp", "ctx"), P("tp"), P("tp"))
    out_specs = P("tp", "ctx")
    body = fused_shards if mesh.shape["ctx"] <= 16 else shards
    return jax.shard_map(body, mesh=mesh, in_specs=in_specs, out_specs=out_specs, check_vma=False)
```

```python
import functools
import math

import jax
import jax.numpy as jnp
from jax import lax
from jax.experimental import pallas as pl
from jax.experimental.pallas import tpu as pltpu
from jax.sharding import PartitionSpec as P

highest = lax.Precision.HIGHEST
MESH = pl.DeviceIdType.MESH


def causal_short(padded, weights, length):
    taps = weights.shape[0]
    total = jnp.zeros(padded.shape[:2] + (length,), jnp.float32)
    for offset in range(taps):
        start = taps - 1 - offset
        total = total + weights[offset][:, :, None] * padded[:, :, start : start + length]
    return total


def trig_tables(half_count, row_count):
    periods = 2 * half_count
    total_len = periods * row_count
    freq = lax.iota(jnp.int32, periods)[:, None]
    place = lax.iota(jnp.int32, half_count)[None, :]
    angle_one = (freq * place % periods).astype(jnp.float32) * (2.0 * math.pi / periods)
    cols = lax.iota(jnp.int32, row_count)
    angle_two = (cols[:, None] * cols[None, :] % row_count).astype(jnp.float32) * (
        2.0 * math.pi / row_count
    )
    angle_twist = (freq * cols[None, :] % total_len).astype(jnp.float32) * (
        2.0 * math.pi / total_len
    )
    return (
        jnp.cos(angle_one),
        jnp.sin(angle_one),
        jnp.cos(angle_two),
        jnp.sin(angle_two),
        jnp.cos(angle_twist),
        jnp.sin(angle_twist),
    )


def forward_dft(signal, tables):
    cos_one, sin_one, cos_two, sin_two, cos_tw, sin_tw = tables
    first_re = jnp.einsum("ka,cab->ckb", cos_one, signal, precision=highest)
    first_im = -jnp.einsum("ka,cab->ckb", sin_one, signal, precision=highest)
    turned_re = first_re * cos_tw + first_im * sin_tw
    turned_im = first_im * cos_tw - first_re * sin_tw
    out_re = jnp.einsum("ckb,bq->ckq", turned_re, cos_two, precision=highest) + jnp.einsum(
        "ckb,bq->ckq", turned_im, sin_two, precision=highest
    )
    out_im = jnp.einsum("ckb,bq->ckq", turned_im, cos_two, precision=highest) - jnp.einsum(
        "ckb,bq->ckq", turned_re, sin_two, precision=highest
    )
    return (out_re, out_im)


def inverse_dft(spec_re, spec_im, tables):
    cos_one, sin_one, cos_two, sin_two, cos_tw, sin_tw = tables
    back_re = jnp.einsum("ckq,qb->ckb", spec_re, cos_two, precision=highest) - jnp.einsum(
        "ckq,qb->ckb", spec_im, sin_two, precision=highest
    )
    back_im = jnp.einsum("ckq,qb->ckb", spec_re, sin_two, precision=highest) + jnp.einsum(
        "ckq,qb->ckb", spec_im, cos_two, precision=highest
    )
    turned_re = back_re * cos_tw - back_im * sin_tw
    turned_im = back_re * sin_tw + back_im * cos_tw
    result = jnp.einsum("ka,ckb->cab", cos_one, turned_re, precision=highest) - jnp.einsum(
        "ka,ckb->cab", sin_one, turned_im, precision=highest
    )
    total_len = 2 * cos_one.shape[1] * cos_two.shape[0]
    return result / total_len


def shards(streams, short_weight, filters, skip_gain, norm_gain):
    n_ctx = lax.axis_size("ctx")
    n_width = lax.axis_size("tp")
    tok_rows = streams.shape[2]
    local_chan = streams.shape[1]
    owned = local_chan // n_ctx
    owned_groups = filters.shape[0] // n_ctx
    per_group = owned // owned_groups
    seq_len = tok_rows * n_ctx
    taps = short_weight.shape[0]
    owner_start = lax.axis_index("ctx") * owned
    skip_own = lax.dynamic_slice_in_dim(skip_gain, owner_start, owned, 0)
    filter_own = lax.all_to_all(filters, "ctx", split_axis=0, concat_axis=1, tiled=True)
    raw_own = lax.all_to_all(streams, "ctx", split_axis=1, concat_axis=2, tiled=True)
    weight_own = lax.dynamic_slice_in_dim(short_weight, owner_start, owned, 2)
    padded = jnp.pad(raw_own.astype(jnp.float32), ((0, 0), (0, 0), (taps - 1, 0)))
    conv_own = causal_short(padded, weight_own, seq_len)
    query_own = lax.optimization_barrier(conv_own[0].astype(jnp.bfloat16)).astype(jnp.float32)
    value_own = lax.optimization_barrier((conv_own[1] * conv_own[2]).astype(jnp.bfloat16)).astype(
        jnp.float32
    )
    tables = trig_tables(n_ctx, tok_rows)
    value_re, value_im = forward_dft(value_own.reshape(owned, n_ctx, tok_rows), tables)
    filt_re, filt_im = forward_dft(filter_own.reshape(owned_groups, n_ctx, tok_rows), tables)
    spec_shape = (owned_groups, per_group) + value_re.shape[1:]
    value_re = value_re.reshape(spec_shape)
    value_im = value_im.reshape(spec_shape)
    filt_re = filt_re[:, None]
    filt_im = filt_im[:, None]
    spec_re = (value_re * filt_re - value_im * filt_im).reshape((owned,) + spec_shape[2:])
    spec_im = (value_re * filt_im + value_im * filt_re).reshape((owned,) + spec_shape[2:])
    long_conv = inverse_dft(spec_re, spec_im, tables).reshape(owned, seq_len)
    gated = (query_own * (long_conv + skip_own[:, None] * value_own)).astype(jnp.bfloat16)
    gated_rows = lax.all_to_all(gated, "ctx", split_axis=1, concat_axis=0, tiled=True)
    gated_wide = gated_rows.astype(jnp.float32)
    squares = lax.psum(jnp.sum(gated_wide * gated_wide, axis=0), "tp")
    rms = jnp.sqrt(squares / (local_chan * n_width) + 1e-05)
    return (gated_wide * norm_gain[:, None] / rms[None, :]).astype(jnp.bfloat16)


def rolled_order(n):
    return sorted(range(1, n), key=lambda r: (abs(2 * r - n), r))


def kernel(
    n,
    nt,
    n_chunks,
    st_hbm,
    sw_hbm,
    filt_hbm,
    skip_hbm,
    gated_ref,
    rms_ref,
    st,
    sw_ref,
    filt_ref,
    skip_ref,
    halo_out,
    halo_in,
    halo_col,
    coef_row,
    coef_col,
    filt_out,
    filt_in,
    filt_f32,
    toep,
    prod,
    query,
    recv,
    res,
    back,
    sq_out,
    sq_in,
    load_sem,
    halo_send,
    halo_recv,
    filt_send,
    filt_recv,
    prod_send,
    prod_recv,
    res_send,
    res_recv,
    sq_send,
    sq_recv,
):
    bf16, f32 = jnp.bfloat16, jnp.float32
    me = lax.axis_index("ctx")
    tp = lax.axis_index("tp")
    taps = sw_ref.shape[0]
    own, width = st.shape[2], st.shape[3]
    chan = n * own
    owned_groups = filt_in.shape[1]
    per_group = own // owned_groups
    rows = own // n_chunks
    order = rolled_order(n)

    loads = [pltpu.make_async_copy(st_hbm.at[s], st.at[s], load_sem.at[s]) for s in range(3)]
    small = [
        pltpu.make_async_copy(filt_hbm, filt_ref, load_sem.at[3]),
        pltpu.make_async_copy(sw_hbm, sw_ref, load_sem.at[4]),
        pltpu.make_async_copy(skip_hbm, skip_ref, load_sem.at[5]),
    ]
    for load in loads + small:
        load.start()

    barrier = pltpu.get_barrier_semaphore()
    for r in range(1, n):
        pl.semaphore_signal(
            barrier, inc=1, device_id=(lax.rem(me + r, n), tp), device_id_type=MESH
        )
    for r in range(1, nt):
        pl.semaphore_signal(
            barrier, inc=1, device_id=(me, lax.rem(tp + r, nt)), device_id_type=MESH
        )
    for load in small:
        load.wait()
    filt_out[...] = filt_ref[...].astype(bf16)
    coef_row[...] = jnp.zeros_like(coef_row)
    for j in range(taps):
        for s in range(3):
            coef_row[3 * j + s : 3 * j + s + 1, :] = sw_ref[j, s : s + 1, :]
    coef_row[3 * taps : 3 * taps + 1, :] = skip_ref[...]
    coef_col[...] = coef_row[...].T.reshape(coef_col.shape)
    for load in loads:
        load.wait()
    halo = jnp.zeros((16, chan), f32)
    row_id = lax.broadcasted_iota(jnp.int32, (16, width), 0)
    lane_id = lax.broadcasted_iota(jnp.int32, (16, width), 1)
    for s in range(3):
        pick = (lane_id >= width - 2) & (row_id == 2 * s + lane_id - (width - 2))
        halo = halo + lax.dot_general(
            pick.astype(f32).astype(bf16),
            st[s].reshape(chan, width),
            (((1,), (1,)), ((), ())),
            preferred_element_type=f32,
        )
    halo_out[...] = halo.astype(bf16)

    pl.semaphore_wait(barrier, n - 1 + nt - 1)

    halo_copy = pltpu.make_async_remote_copy(
        src_ref=halo_out,
        dst_ref=halo_in,
        send_sem=halo_send,
        recv_sem=halo_recv,
        device_id=(lax.rem(me + 1, n), tp),
        device_id_type=MESH,
    )

    @pl.when(me < n - 1)
    def _():
        halo_copy.start()

    def filt_copy(r):
        to = lax.rem(me + r, n)
        return pltpu.make_async_remote_copy(
            src_ref=filt_out.at[pl.ds(pl.multiple_of(to * owned_groups, owned_groups), owned_groups)],
            dst_ref=filt_in.at[me],
            send_sem=filt_send.at[r],
            recv_sem=filt_recv.at[r],
            device_id=(to, tp),
            device_id_type=MESH,
        )

    for r in order:
        filt_copy(r).start()
    filt_in[me] = filt_out[pl.ds(pl.multiple_of(me * owned_groups, owned_groups), owned_groups), :]

    @pl.when(me == 0)
    def _():
        halo_in[...] = jnp.zeros_like(halo_in)

    @pl.when(me > 0)
    def _():
        halo_copy.wait_recv()

    wide = jnp.concatenate([halo_in[...].astype(f32), jnp.zeros((width - 16, chan), f32)], axis=0)
    halo_col[...] = wide.T.astype(bf16).reshape(halo_col.shape)

    def prod_copy(q, r):
        to = lax.rem(me + r, n)
        part = pl.ds(q * rows, rows)
        return pltpu.make_async_remote_copy(
            src_ref=prod.at[to, part],
            dst_ref=recv.at[me, part],
            send_sem=prod_send.at[q, r],
            recv_sem=prod_recv.at[q, r],
            device_id=(to, tp),
            device_id_type=MESH,
        )

    def res_copy(q, r):
        to = lax.rem(me + r, n)
        part = pl.ds(q * rows, rows)
        return pltpu.make_async_remote_copy(
            src_ref=res.at[to, part],
            dst_ref=back.at[me, part],
            send_sem=res_send.at[q, r],
            recv_sem=res_recv.at[q, r],
            device_id=(to, tp),
            device_id_type=MESH,
        )

    k_id = lax.broadcasted_iota(jnp.int32, (2 * width, 2 * width), 0)
    m_id = lax.broadcasted_iota(jnp.int32, (2 * width, 2 * width), 1)
    shift = jnp.where(m_id < width, 1, 2)
    m_in = jnp.where(m_id < width, m_id, m_id - width)
    for q in range(n_chunks):
        part = slice(q * rows, (q + 1) * rows)
        coef = coef_col[:, part, :].reshape(n * rows, coef_col.shape[2])
        conv = []
        for s in range(3):
            inner = (k_id < width) & (k_id == m_in - shift)
            outer = (k_id >= width) & (m_in < shift) & (k_id - width == 2 * s + 2 + m_in - shift)
            mover = (inner | outer).astype(f32).astype(bf16)
            now = st[s, :, part, :].reshape(n * rows, width)
            both = jnp.concatenate(
                [now, halo_col[:, part, :].reshape(n * rows, width)], axis=1
            )
            moved = jnp.dot(both, mover, preferred_element_type=f32)
            conv.append(
                coef[:, s : s + 1] * now.astype(f32)
                + coef[:, 3 + s : 4 + s] * moved[:, :width]
                + coef[:, 6 + s : 7 + s] * moved[:, width:]
            )
        query[:, part, :] = conv[0].astype(bf16).reshape(n, rows, width)
        prod[:, part, :] = (conv[1] * conv[2]).astype(bf16).reshape(n, rows, width)
        for r in order:
            prod_copy(q, r).start()
        recv[me, part, :] = prod[me, part, :]

    for r in order:
        filt_copy(r).wait_recv()
    filt_f32[...] = filt_in[...].astype(f32)
    t_id = lax.broadcasted_iota(jnp.int32, (width, width), 1)
    s_id = lax.broadcasted_iota(jnp.int32, (width, width), 0)

    @pl.loop(0, owned_groups)
    def _(g):
        line = jnp.concatenate([filt_f32[j, pl.ds(g, 1), :] for j in range(n)], axis=1)
        line = jnp.broadcast_to(line, (width, n * width))
        turned = pltpu.roll(line, 0, 1, stride=1, stride_axis=0)
        toep[g, :, width:] = turned[:, width:].astype(bf16)
        toep[g, :, :width] = jnp.where(t_id >= s_id, turned[:, :width], 0.0).astype(bf16)

    for q in range(n_chunks):
        for r in order:
            prod_copy(q, r).wait_recv()
        per_chunk = rows // per_group

        @pl.loop(0, per_chunk)
        def _(k):
            place = pl.ds(pl.multiple_of(q * rows + k * per_group, per_group), per_group)
            block = recv[:, place, :].reshape(n * per_group, width)
            full = jnp.dot(block, toep[q * per_chunk + k], preferred_element_type=f32)
            for i in range(n):
                total = full[:per_group, i * width : (i + 1) * width]
                for j in range(1, i + 1):
                    total = total + full[
                        j * per_group : (j + 1) * per_group, (i - j) * width : (i - j + 1) * width
                    ]
                res[i, place, :] = total.astype(bf16)

        for r in order:
            res_copy(q, r).start()
        part = slice(q * rows, (q + 1) * rows)
        back[me, part, :] = res[me, part, :]

    squares = jnp.zeros((8, width), f32)
    for q in range(n_chunks):
        part = slice(q * rows, (q + 1) * rows)
        for r in order:
            res_copy(q, r).wait_recv()
        skip = coef_col[:, part, :].reshape(n * rows, coef_col.shape[2])[:, 3 * taps : 3 * taps + 1]
        direct = skip * prod[:, part, :].reshape(n * rows, width).astype(f32)
        far = back[:, part, :].reshape(n * rows, width).astype(f32)
        gated = (query[:, part, :].reshape(n * rows, width).astype(f32) * (far + direct)).astype(bf16)
        gated_ref[:, part, :] = gated.reshape(n, rows, width)
        gated = gated.astype(f32)
        squares = squares + jnp.sum((gated * gated).reshape(n * rows // 8, 8, width), axis=0)
    sq_out[...] = squares

    def sq_copy(r):
        return pltpu.make_async_remote_copy(
            src_ref=sq_out,
            dst_ref=sq_in.at[tp],
            send_sem=sq_send.at[r],
            recv_sem=sq_recv.at[r],
            device_id=(me, lax.rem(tp + r, nt)),
            device_id_type=MESH,
        )

    for r in range(1, nt):
        sq_copy(r).start()
    sq_in[tp] = squares
    for r in order:
        filt_copy(r).wait_send()
        for q in range(n_chunks):
            prod_copy(q, r).wait_send()
            res_copy(q, r).wait_send()

    @pl.when(me < n - 1)
    def _():
        halo_copy.wait_send()

    for r in range(1, nt):
        sq_copy(r).wait_recv()
    total = jnp.sum(jnp.sum(sq_in[...], axis=0), axis=0, keepdims=True)
    rms_ref[...] = jnp.sqrt(total / (chan * nt) + 1e-05)
    for r in range(1, nt):
        sq_copy(r).wait_send()


def fused_shards(streams, short_weight, filters, skip_gain, norm_gain):
    n = lax.axis_size("ctx")
    nt = lax.axis_size("tp")
    chan, width = streams.shape[1:]
    own = chan // n
    owned_groups = filters.shape[0] // n
    n_chunks = 4
    bf16, f32 = jnp.bfloat16, jnp.float32
    vmem = pl.BlockSpec(memory_space=pltpu.VMEM)
    dma = pltpu.SemaphoreType.DMA
    slab = pltpu.VMEM((n, own, width), bf16)
    gated, rms = pl.pallas_call(
        functools.partial(kernel, n, nt, n_chunks),
        out_shape=(
            jax.ShapeDtypeStruct((n, own, width), bf16),
            jax.ShapeDtypeStruct((1, width), f32),
        ),
        in_specs=[pl.BlockSpec(memory_space=pltpu.HBM)] * 4,
        out_specs=(vmem, vmem),
        scratch_shapes=[
            pltpu.VMEM((3, n, own, width), bf16),
            pltpu.VMEM(short_weight.shape, f32),
            pltpu.VMEM(filters.shape, f32),
            pltpu.VMEM((1, chan), f32),
            pltpu.VMEM((16, chan), bf16),
            pltpu.VMEM((16, chan), bf16),
            slab,
            pltpu.VMEM((128, chan), f32),
            pltpu.VMEM((n, own, 128), f32),
            pltpu.VMEM((filters.shape[0], width), bf16),
            pltpu.VMEM((n, owned_groups, width), bf16),
            pltpu.VMEM((n, owned_groups, width), f32),
            pltpu.VMEM((owned_groups, width, n * width), bf16),
            slab,
            slab,
            slab,
            slab,
            slab,
            pltpu.VMEM((8, width), f32),
            pltpu.VMEM((nt, 8, width), f32),
            dma((6,)),
            dma,
            dma,
            dma((n,)),
            dma((n,)),
            dma((n_chunks, n)),
            dma((n_chunks, n)),
            dma((n_chunks, n)),
            dma((n_chunks, n)),
            dma((nt,)),
            dma((nt,)),
        ],
        compiler_params=pltpu.CompilerParams(
            collective_id=0, has_side_effects=True, vmem_limit_bytes=63 * 1024 * 1024
        ),
        name="hyena",
    )(
        streams.reshape(3, n, own, width),
        short_weight,
        filters,
        skip_gain.reshape(1, chan),
    )
    wide = gated.reshape(chan, width).astype(f32)
    return (wide * norm_gain[:, None] / rms).astype(bf16)


def solution(mesh):
    in_specs = (P(None, "tp", "ctx"), P(None, None, "tp"), P("tp", "ctx"), P("tp"), P("tp"))
    out_specs = P("tp", "ctx")
    body = fused_shards if mesh.shape["ctx"] <= 16 else shards
    return jax.shard_map(body, mesh=mesh, in_specs=in_specs, out_specs=out_specs, check_vma=False)
```

```python
import functools
import math

import jax
import jax.numpy as jnp
from jax import lax
from jax.experimental import pallas as pl
from jax.experimental.pallas import tpu as pltpu
from jax.sharding import PartitionSpec as P

highest = lax.Precision.HIGHEST
MESH = pl.DeviceIdType.MESH


def causal_short(padded, weights, length):
    taps = weights.shape[0]
    total = jnp.zeros(padded.shape[:2] + (length,), jnp.float32)
    for offset in range(taps):
        start = taps - 1 - offset
        total = total + weights[offset][:, :, None] * padded[:, :, start : start + length]
    return total


def trig_tables(half_count, row_count):
    periods = 2 * half_count
    total_len = periods * row_count
    freq = lax.iota(jnp.int32, periods)[:, None]
    place = lax.iota(jnp.int32, half_count)[None, :]
    angle_one = (freq * place % periods).astype(jnp.float32) * (2.0 * math.pi / periods)
    cols = lax.iota(jnp.int32, row_count)
    angle_two = (cols[:, None] * cols[None, :] % row_count).astype(jnp.float32) * (
        2.0 * math.pi / row_count
    )
    angle_twist = (freq * cols[None, :] % total_len).astype(jnp.float32) * (
        2.0 * math.pi / total_len
    )
    return (
        jnp.cos(angle_one),
        jnp.sin(angle_one),
        jnp.cos(angle_two),
        jnp.sin(angle_two),
        jnp.cos(angle_twist),
        jnp.sin(angle_twist),
    )


def forward_dft(signal, tables):
    cos_one, sin_one, cos_two, sin_two, cos_tw, sin_tw = tables
    first_re = jnp.einsum("ka,cab->ckb", cos_one, signal, precision=highest)
    first_im = -jnp.einsum("ka,cab->ckb", sin_one, signal, precision=highest)
    turned_re = first_re * cos_tw + first_im * sin_tw
    turned_im = first_im * cos_tw - first_re * sin_tw
    out_re = jnp.einsum("ckb,bq->ckq", turned_re, cos_two, precision=highest) + jnp.einsum(
        "ckb,bq->ckq", turned_im, sin_two, precision=highest
    )
    out_im = jnp.einsum("ckb,bq->ckq", turned_im, cos_two, precision=highest) - jnp.einsum(
        "ckb,bq->ckq", turned_re, sin_two, precision=highest
    )
    return (out_re, out_im)


def inverse_dft(spec_re, spec_im, tables):
    cos_one, sin_one, cos_two, sin_two, cos_tw, sin_tw = tables
    back_re = jnp.einsum("ckq,qb->ckb", spec_re, cos_two, precision=highest) - jnp.einsum(
        "ckq,qb->ckb", spec_im, sin_two, precision=highest
    )
    back_im = jnp.einsum("ckq,qb->ckb", spec_re, sin_two, precision=highest) + jnp.einsum(
        "ckq,qb->ckb", spec_im, cos_two, precision=highest
    )
    turned_re = back_re * cos_tw - back_im * sin_tw
    turned_im = back_re * sin_tw + back_im * cos_tw
    result = jnp.einsum("ka,ckb->cab", cos_one, turned_re, precision=highest) - jnp.einsum(
        "ka,ckb->cab", sin_one, turned_im, precision=highest
    )
    total_len = 2 * cos_one.shape[1] * cos_two.shape[0]
    return result / total_len


def shards(streams, short_weight, filters, skip_gain, norm_gain):
    n_ctx = lax.axis_size("ctx")
    n_width = lax.axis_size("tp")
    tok_rows = streams.shape[2]
    local_chan = streams.shape[1]
    owned = local_chan // n_ctx
    owned_groups = filters.shape[0] // n_ctx
    per_group = owned // owned_groups
    seq_len = tok_rows * n_ctx
    taps = short_weight.shape[0]
    owner_start = lax.axis_index("ctx") * owned
    skip_own = lax.dynamic_slice_in_dim(skip_gain, owner_start, owned, 0)
    filter_own = lax.all_to_all(filters, "ctx", split_axis=0, concat_axis=1, tiled=True)
    raw_own = lax.all_to_all(streams, "ctx", split_axis=1, concat_axis=2, tiled=True)
    weight_own = lax.dynamic_slice_in_dim(short_weight, owner_start, owned, 2)
    padded = jnp.pad(raw_own.astype(jnp.float32), ((0, 0), (0, 0), (taps - 1, 0)))
    conv_own = causal_short(padded, weight_own, seq_len)
    query_own = lax.optimization_barrier(conv_own[0].astype(jnp.bfloat16)).astype(jnp.float32)
    value_own = lax.optimization_barrier((conv_own[1] * conv_own[2]).astype(jnp.bfloat16)).astype(
        jnp.float32
    )
    tables = trig_tables(n_ctx, tok_rows)
    value_re, value_im = forward_dft(value_own.reshape(owned, n_ctx, tok_rows), tables)
    filt_re, filt_im = forward_dft(filter_own.reshape(owned_groups, n_ctx, tok_rows), tables)
    spec_shape = (owned_groups, per_group) + value_re.shape[1:]
    value_re = value_re.reshape(spec_shape)
    value_im = value_im.reshape(spec_shape)
    filt_re = filt_re[:, None]
    filt_im = filt_im[:, None]
    spec_re = (value_re * filt_re - value_im * filt_im).reshape((owned,) + spec_shape[2:])
    spec_im = (value_re * filt_im + value_im * filt_re).reshape((owned,) + spec_shape[2:])
    long_conv = inverse_dft(spec_re, spec_im, tables).reshape(owned, seq_len)
    gated = (query_own * (long_conv + skip_own[:, None] * value_own)).astype(jnp.bfloat16)
    gated_rows = lax.all_to_all(gated, "ctx", split_axis=1, concat_axis=0, tiled=True)
    gated_wide = gated_rows.astype(jnp.float32)
    squares = lax.psum(jnp.sum(gated_wide * gated_wide, axis=0), "tp")
    rms = jnp.sqrt(squares / (local_chan * n_width) + 1e-05)
    return (gated_wide * norm_gain[:, None] / rms[None, :]).astype(jnp.bfloat16)


def rolled_order(n):
    return sorted(range(1, n), key=lambda r: (abs(2 * r - n), r))


def kernel(
    n,
    nt,
    n_chunks,
    st_hbm,
    sw_hbm,
    filt_hbm,
    skip_hbm,
    gated_ref,
    rms_ref,
    st,
    sw_ref,
    filt_ref,
    skip_ref,
    edge_out,
    edge_in,
    fix_out,
    fix_in,
    fix_row,
    fix_col,
    local_col,
    direct,
    gated_vmem,
    coef_row,
    coef_col,
    filt_out,
    filt_in,
    filt_f32,
    toep,
    prod,
    query,
    recv,
    res,
    back,
    sq_out,
    sq_in,
    load_sem,
    edge_send,
    edge_recv,
    fix_send,
    fix_recv,
    filt_send,
    filt_recv,
    prod_send,
    prod_recv,
    res_send,
    res_recv,
    sq_send,
    sq_recv,
):
    bf16, f32 = jnp.bfloat16, jnp.float32
    me = lax.axis_index("ctx")
    tp = lax.axis_index("tp")
    taps = sw_ref.shape[0]
    own, width = st.shape[2], st.shape[3]
    chan = n * own
    owned_groups = filt_in.shape[1]
    per_group = own // owned_groups
    rows = own // n_chunks
    order = rolled_order(n)

    loads = [pltpu.make_async_copy(st_hbm.at[s], st.at[s], load_sem.at[s]) for s in range(3)]
    small = [
        pltpu.make_async_copy(filt_hbm, filt_ref, load_sem.at[3]),
        pltpu.make_async_copy(sw_hbm, sw_ref, load_sem.at[4]),
        pltpu.make_async_copy(skip_hbm, skip_ref, load_sem.at[5]),
    ]
    for load in loads + small:
        load.start()

    barrier = pltpu.get_barrier_semaphore()
    for r in range(1, n):
        pl.semaphore_signal(
            barrier, inc=1, device_id=(lax.rem(me + r, n), tp), device_id_type=MESH
        )
    for r in range(1, nt):
        pl.semaphore_signal(
            barrier, inc=1, device_id=(me, lax.rem(tp + r, nt)), device_id_type=MESH
        )
    for load in small:
        load.wait()
    filt_out[...] = filt_ref[...].astype(bf16)
    coef_row[...] = jnp.zeros_like(coef_row)
    fix_row[...] = jnp.zeros_like(fix_row)
    fix_out[...] = jnp.zeros_like(fix_out)
    for j in range(taps):
        for s in range(3):
            coef_row[3 * j + s : 3 * j + s + 1, :] = sw_ref[j, s : s + 1, :]
    coef_row[3 * taps : 3 * taps + 1, :] = skip_ref[...]
    coef_col[...] = coef_row[...].T.reshape(coef_col.shape)
    for load in loads:
        load.wait()
    edge = jnp.zeros((16, chan), f32)
    row_id = lax.broadcasted_iota(jnp.int32, (16, width), 0)
    lane_id = lax.broadcasted_iota(jnp.int32, (16, width), 1)
    slot = jnp.where(lane_id < 2, lane_id, lane_id - width + 4)
    at_edge = (lane_id < 2) | (lane_id >= width - 2)
    for s in range(3):
        pick = at_edge & (row_id == 4 * s + slot)
        edge = edge + lax.dot_general(
            pick.astype(f32).astype(bf16),
            st[s].reshape(chan, width),
            (((1,), (1,)), ((), ())),
            preferred_element_type=f32,
        )
    edge_out[...] = edge.astype(bf16)

    pl.semaphore_wait(barrier, n - 1 + nt - 1)

    edge_copy = pltpu.make_async_remote_copy(
        src_ref=edge_out,
        dst_ref=edge_in,
        send_sem=edge_send,
        recv_sem=edge_recv,
        device_id=(lax.rem(me + 1, n), tp),
        device_id_type=MESH,
    )

    @pl.when(me < n - 1)
    def _():
        edge_copy.start()

    def filt_copy(r):
        to = lax.rem(me + r, n)
        return pltpu.make_async_remote_copy(
            src_ref=filt_out.at[pl.ds(pl.multiple_of(to * owned_groups, owned_groups), owned_groups)],
            dst_ref=filt_in.at[me],
            send_sem=filt_send.at[r],
            recv_sem=filt_recv.at[r],
            device_id=(to, tp),
            device_id_type=MESH,
        )

    for r in order:
        filt_copy(r).start()
    filt_in[me] = filt_out[pl.ds(pl.multiple_of(me * owned_groups, owned_groups), owned_groups), :]

    def prod_copy(q, r):
        to = lax.rem(me + r, n)
        part = pl.ds(q * rows, rows)
        return pltpu.make_async_remote_copy(
            src_ref=prod.at[to, part],
            dst_ref=recv.at[me, part],
            send_sem=prod_send.at[q, r],
            recv_sem=prod_recv.at[q, r],
            device_id=(to, tp),
            device_id_type=MESH,
        )

    def res_copy(q, r):
        to = lax.rem(me + r, n)
        part = pl.ds(q * rows, rows)
        return pltpu.make_async_remote_copy(
            src_ref=res.at[to, part],
            dst_ref=back.at[me, part],
            send_sem=res_send.at[q, r],
            recv_sem=res_recv.at[q, r],
            device_id=(to, tp),
            device_id_type=MESH,
        )

    def fix_copy(r):
        to = lax.rem(me + r, n)
        return pltpu.make_async_remote_copy(
            src_ref=fix_out.at[to],
            dst_ref=fix_in.at[me],
            send_sem=fix_send.at[r],
            recv_sem=fix_recv.at[r],
            device_id=(to, tp),
            device_id_type=MESH,
        )

    def fix_edges():
        @pl.when(me == 0)
        def _():
            edge_in[...] = jnp.zeros_like(edge_in)

        @pl.when(me > 0)
        def _():
            edge_copy.wait_recv()

        here = edge_out[...].astype(f32)
        left = edge_in[...].astype(f32)
        coef = coef_row[...]
        first, second = [], []
        for s in range(3):
            now, later = here[4 * s : 4 * s + 1], here[4 * s + 1 : 4 * s + 2]
            two, one = left[4 * s + 2 : 4 * s + 3], left[4 * s + 3 : 4 * s + 4]
            w0, w1, w2 = (coef[3 * j + s : 3 * j + s + 1] for j in range(3))
            first.append(w0 * now + w1 * one + w2 * two)
            second.append(w0 * later + w1 * now + w2 * one)
        lines = [
            first[1] * first[2],
            second[1] * second[2],
            first[0],
            second[0],
        ]
        lines = [line.astype(bf16).astype(f32) for line in lines]
        for o in range(n):
            for h in range(own // 128):
                at = o * own + h * 128
                for p in range(2):
                    fix_out[o, 2 * h + p : 2 * h + p + 1, :] = lines[p][:, at : at + 128]
        for i in range(4):
            fix_row[i : i + 1, :] = lines[i]

    k_id = lax.broadcasted_iota(jnp.int32, (width, 2 * width), 0)
    m_id = lax.broadcasted_iota(jnp.int32, (width, 2 * width), 1)
    source = jnp.where(m_id < width, m_id - 1, m_id - width - 2)
    mover = (k_id == source).astype(f32).astype(bf16)
    for q in range(n_chunks):
        part = slice(q * rows, (q + 1) * rows)
        coef = coef_col[:, part, :].reshape(n * rows, coef_col.shape[2])
        conv = []
        for s in range(3):
            now = st[s, :, part, :].reshape(n * rows, width)
            moved = jnp.dot(now, mover, preferred_element_type=f32)
            conv.append(
                coef[:, s : s + 1] * now.astype(f32)
                + coef[:, 3 + s : 4 + s] * moved[:, :width]
                + coef[:, 6 + s : 7 + s] * moved[:, width:]
            )
        query[:, part, :] = conv[0].astype(bf16).reshape(n, rows, width)
        prod[:, part, :] = (conv[1] * conv[2]).astype(bf16).reshape(n, rows, width)
        for r in order:
            prod_copy(q, r).start()
        recv[me, part, :] = prod[me, part, :]
        if q == n_chunks // 2 - 1:
            fix_edges()
            for r in order:
                fix_copy(r).start()
            fix_in[me] = fix_out[me]

    for r in order:
        filt_copy(r).wait_recv()
    filt_f32[...] = filt_in[...].astype(f32)
    t_id = lax.broadcasted_iota(jnp.int32, (width, width), 1)
    s_id = lax.broadcasted_iota(jnp.int32, (width, width), 0)

    @pl.loop(0, owned_groups)
    def _(g):
        line = jnp.concatenate([filt_f32[j, pl.ds(g, 1), :] for j in range(n)], axis=1)
        line = jnp.broadcast_to(line, (width, n * width))
        turned = pltpu.roll(line, 0, 1, stride=1, stride_axis=0)
        toep[g, :, width:] = turned[:, width:].astype(bf16)
        toep[g, :, :width] = jnp.where(t_id >= s_id, turned[:, :width], 0.0).astype(bf16)

    for r in order:
        fix_copy(r).wait_recv()
    for h in range(own // 128):
        gathered = jnp.concatenate([fix_in[j, 2 * h : 2 * h + 2, :] for j in range(n)], axis=0)
        gathered = jnp.concatenate([gathered, jnp.zeros((width - 2 * n, 128), f32)], axis=0).T
        for j in range(n):
            near = gathered if j == 0 else pltpu.roll(gathered, width - 2 * j, 1)
            fix_col[j, h * 128 : (h + 1) * 128, :] = near
    head = lax.broadcasted_iota(jnp.int32, (n * per_group, width), 1) < 2

    for q in range(n_chunks):
        for r in order:
            prod_copy(q, r).wait_recv()
        per_chunk = rows // per_group

        @pl.loop(0, per_chunk)
        def _(k):
            place = pl.ds(pl.multiple_of(q * rows + k * per_group, per_group), per_group)
            block = recv[:, place, :].reshape(n * per_group, width).astype(f32)
            fixed = fix_col[:, place, :].reshape(n * per_group, width)
            block = jnp.where(head, fixed, block).astype(bf16)
            full = jnp.dot(block, toep[q * per_chunk + k], preferred_element_type=f32)
            for i in range(n):
                total = full[:per_group, i * width : (i + 1) * width]
                for j in range(1, i + 1):
                    total = total + full[
                        j * per_group : (j + 1) * per_group, (i - j) * width : (i - j + 1) * width
                    ]
                res[i, place, :] = total.astype(bf16)

        for r in order:
            res_copy(q, r).start()
        part = slice(q * rows, (q + 1) * rows)
        back[me, part, :] = res[me, part, :]

    local_col[...] = fix_row[...].T.reshape(local_col.shape)
    head = lax.broadcasted_iota(jnp.int32, (n * rows, width), 1) < 2
    for q in range(n_chunks):
        part = slice(q * rows, (q + 1) * rows)
        skip = coef_col[:, part, :].reshape(n * rows, coef_col.shape[2])[:, 3 * taps : 3 * taps + 1]
        fixed = local_col[:, part, :].reshape(n * rows, width)
        value = prod[:, part, :].reshape(n * rows, width).astype(f32)
        direct[:, part, :] = (skip * jnp.where(head, fixed, value)).reshape(n, rows, width)
        fixed = pltpu.roll(fixed, width - 2, 1)
        value = query[:, part, :].reshape(n * rows, width).astype(f32)
        query[:, part, :] = jnp.where(head, fixed, value).astype(bf16).reshape(n, rows, width)

    squares = jnp.zeros((8, width), f32)
    for q in range(n_chunks):
        part = slice(q * rows, (q + 1) * rows)
        for r in order:
            res_copy(q, r).wait_recv()
        far = back[:, part, :].astype(f32)
        gated = (query[:, part, :].astype(f32) * (far + direct[:, part, :])).astype(bf16)
        gated_vmem[:, part, :] = gated
        gated = gated.astype(f32)
        squares = squares + jnp.sum((gated * gated).reshape(n * rows // 8, 8, width), axis=0)
    sq_out[...] = squares

    def sq_copy(r):
        return pltpu.make_async_remote_copy(
            src_ref=sq_out,
            dst_ref=sq_in.at[tp],
            send_sem=sq_send.at[r],
            recv_sem=sq_recv.at[r],
            device_id=(me, lax.rem(tp + r, nt)),
            device_id_type=MESH,
        )

    for r in range(1, nt):
        sq_copy(r).start()
    gated_copy = pltpu.make_async_copy(gated_vmem, gated_ref, load_sem.at[6])
    gated_copy.start()
    sq_in[tp] = squares
    for r in order:
        filt_copy(r).wait_send()
        fix_copy(r).wait_send()
        for q in range(n_chunks):
            prod_copy(q, r).wait_send()
            res_copy(q, r).wait_send()

    @pl.when(me < n - 1)
    def _():
        edge_copy.wait_send()

    for r in range(1, nt):
        sq_copy(r).wait_recv()
    total = jnp.sum(jnp.sum(sq_in[...], axis=0), axis=0, keepdims=True)
    rms_ref[...] = jnp.sqrt(total / (chan * nt) + 1e-05)
    gated_copy.wait()
    for r in range(1, nt):
        sq_copy(r).wait_send()


def fused_shards(streams, short_weight, filters, skip_gain, norm_gain):
    n = lax.axis_size("ctx")
    nt = lax.axis_size("tp")
    chan, width = streams.shape[1:]
    own = chan // n
    owned_groups = filters.shape[0] // n
    n_chunks = 4
    bf16, f32 = jnp.bfloat16, jnp.float32
    vmem = pl.BlockSpec(memory_space=pltpu.VMEM)
    dma = pltpu.SemaphoreType.DMA
    slab = pltpu.VMEM((n, own, width), bf16)
    wide_slab = pltpu.VMEM((n, own, width), f32)
    gated, rms = pl.pallas_call(
        functools.partial(kernel, n, nt, n_chunks),
        out_shape=(
            jax.ShapeDtypeStruct((n, own, width), bf16),
            jax.ShapeDtypeStruct((1, width), f32),
        ),
        in_specs=[pl.BlockSpec(memory_space=pltpu.HBM)] * 4,
        out_specs=(pl.BlockSpec(memory_space=pltpu.HBM), vmem),
        scratch_shapes=[
            pltpu.VMEM((3, n, own, width), bf16),
            pltpu.VMEM(short_weight.shape, f32),
            pltpu.VMEM(filters.shape, f32),
            pltpu.VMEM((1, chan), f32),
            pltpu.VMEM((16, chan), bf16),
            pltpu.VMEM((16, chan), bf16),
            pltpu.VMEM((n, 8, 128), f32),
            pltpu.VMEM((n, 8, 128), f32),
            pltpu.VMEM((128, chan), f32),
            wide_slab,
            wide_slab,
            wide_slab,
            slab,
            pltpu.VMEM((128, chan), f32),
            pltpu.VMEM((n, own, 128), f32),
            pltpu.VMEM((filters.shape[0], width), bf16),
            pltpu.VMEM((n, owned_groups, width), bf16),
            pltpu.VMEM((n, owned_groups, width), f32),
            pltpu.VMEM((owned_groups, width, n * width), bf16),
            slab,
            slab,
            slab,
            slab,
            slab,
            pltpu.VMEM((8, width), f32),
            pltpu.VMEM((nt, 8, width), f32),
            dma((7,)),
            dma,
            dma,
            dma((n,)),
            dma((n,)),
            dma((n,)),
            dma((n,)),
            dma((n_chunks, n)),
            dma((n_chunks, n)),
            dma((n_chunks, n)),
            dma((n_chunks, n)),
            dma((nt,)),
            dma((nt,)),
        ],
        compiler_params=pltpu.CompilerParams(
            collective_id=0, has_side_effects=True, vmem_limit_bytes=63 * 1024 * 1024
        ),
        name="hyena",
    )(
        streams.reshape(3, n, own, width),
        short_weight,
        filters,
        skip_gain.reshape(1, chan),
    )
    wide = gated.reshape(chan, width).astype(f32)
    return (wide * norm_gain[:, None] / rms).astype(bf16)


def solution(mesh):
    in_specs = (P(None, "tp", "ctx"), P(None, None, "tp"), P("tp", "ctx"), P("tp"), P("tp"))
    out_specs = P("tp", "ctx")
    body = fused_shards if mesh.shape["ctx"] <= 16 else shards
    return jax.shard_map(body, mesh=mesh, in_specs=in_specs, out_specs=out_specs, check_vma=False)
```

```python
import functools
import math

import jax
import jax.numpy as jnp
from jax import lax
from jax.experimental import pallas as pl
from jax.experimental.pallas import tpu as pltpu
from jax.sharding import PartitionSpec as P

highest = lax.Precision.HIGHEST
MESH = pl.DeviceIdType.MESH


def causal_short(padded, weights, length):
    taps = weights.shape[0]
    total = jnp.zeros(padded.shape[:2] + (length,), jnp.float32)
    for offset in range(taps):
        start = taps - 1 - offset
        total = total + weights[offset][:, :, None] * padded[:, :, start : start + length]
    return total


def trig_tables(half_count, row_count):
    periods = 2 * half_count
    total_len = periods * row_count
    freq = lax.iota(jnp.int32, periods)[:, None]
    place = lax.iota(jnp.int32, half_count)[None, :]
    angle_one = (freq * place % periods).astype(jnp.float32) * (2.0 * math.pi / periods)
    cols = lax.iota(jnp.int32, row_count)
    angle_two = (cols[:, None] * cols[None, :] % row_count).astype(jnp.float32) * (
        2.0 * math.pi / row_count
    )
    angle_twist = (freq * cols[None, :] % total_len).astype(jnp.float32) * (
        2.0 * math.pi / total_len
    )
    return (
        jnp.cos(angle_one),
        jnp.sin(angle_one),
        jnp.cos(angle_two),
        jnp.sin(angle_two),
        jnp.cos(angle_twist),
        jnp.sin(angle_twist),
    )


def forward_dft(signal, tables):
    cos_one, sin_one, cos_two, sin_two, cos_tw, sin_tw = tables
    first_re = jnp.einsum("ka,cab->ckb", cos_one, signal, precision=highest)
    first_im = -jnp.einsum("ka,cab->ckb", sin_one, signal, precision=highest)
    turned_re = first_re * cos_tw + first_im * sin_tw
    turned_im = first_im * cos_tw - first_re * sin_tw
    out_re = jnp.einsum("ckb,bq->ckq", turned_re, cos_two, precision=highest) + jnp.einsum(
        "ckb,bq->ckq", turned_im, sin_two, precision=highest
    )
    out_im = jnp.einsum("ckb,bq->ckq", turned_im, cos_two, precision=highest) - jnp.einsum(
        "ckb,bq->ckq", turned_re, sin_two, precision=highest
    )
    return (out_re, out_im)


def inverse_dft(spec_re, spec_im, tables):
    cos_one, sin_one, cos_two, sin_two, cos_tw, sin_tw = tables
    back_re = jnp.einsum("ckq,qb->ckb", spec_re, cos_two, precision=highest) - jnp.einsum(
        "ckq,qb->ckb", spec_im, sin_two, precision=highest
    )
    back_im = jnp.einsum("ckq,qb->ckb", spec_re, sin_two, precision=highest) + jnp.einsum(
        "ckq,qb->ckb", spec_im, cos_two, precision=highest
    )
    turned_re = back_re * cos_tw - back_im * sin_tw
    turned_im = back_re * sin_tw + back_im * cos_tw
    result = jnp.einsum("ka,ckb->cab", cos_one, turned_re, precision=highest) - jnp.einsum(
        "ka,ckb->cab", sin_one, turned_im, precision=highest
    )
    total_len = 2 * cos_one.shape[1] * cos_two.shape[0]
    return result / total_len


def shards(streams, short_weight, filters, skip_gain, norm_gain):
    n_ctx = lax.axis_size("ctx")
    n_width = lax.axis_size("tp")
    tok_rows = streams.shape[2]
    local_chan = streams.shape[1]
    owned = local_chan // n_ctx
    owned_groups = filters.shape[0] // n_ctx
    per_group = owned // owned_groups
    seq_len = tok_rows * n_ctx
    taps = short_weight.shape[0]
    owner_start = lax.axis_index("ctx") * owned
    skip_own = lax.dynamic_slice_in_dim(skip_gain, owner_start, owned, 0)
    filter_own = lax.all_to_all(filters, "ctx", split_axis=0, concat_axis=1, tiled=True)
    raw_own = lax.all_to_all(streams, "ctx", split_axis=1, concat_axis=2, tiled=True)
    weight_own = lax.dynamic_slice_in_dim(short_weight, owner_start, owned, 2)
    padded = jnp.pad(raw_own.astype(jnp.float32), ((0, 0), (0, 0), (taps - 1, 0)))
    conv_own = causal_short(padded, weight_own, seq_len)
    query_own = lax.optimization_barrier(conv_own[0].astype(jnp.bfloat16)).astype(jnp.float32)
    value_own = lax.optimization_barrier((conv_own[1] * conv_own[2]).astype(jnp.bfloat16)).astype(
        jnp.float32
    )
    tables = trig_tables(n_ctx, tok_rows)
    value_re, value_im = forward_dft(value_own.reshape(owned, n_ctx, tok_rows), tables)
    filt_re, filt_im = forward_dft(filter_own.reshape(owned_groups, n_ctx, tok_rows), tables)
    spec_shape = (owned_groups, per_group) + value_re.shape[1:]
    value_re = value_re.reshape(spec_shape)
    value_im = value_im.reshape(spec_shape)
    filt_re = filt_re[:, None]
    filt_im = filt_im[:, None]
    spec_re = (value_re * filt_re - value_im * filt_im).reshape((owned,) + spec_shape[2:])
    spec_im = (value_re * filt_im + value_im * filt_re).reshape((owned,) + spec_shape[2:])
    long_conv = inverse_dft(spec_re, spec_im, tables).reshape(owned, seq_len)
    gated = (query_own * (long_conv + skip_own[:, None] * value_own)).astype(jnp.bfloat16)
    gated_rows = lax.all_to_all(gated, "ctx", split_axis=1, concat_axis=0, tiled=True)
    gated_wide = gated_rows.astype(jnp.float32)
    squares = lax.psum(jnp.sum(gated_wide * gated_wide, axis=0), "tp")
    rms = jnp.sqrt(squares / (local_chan * n_width) + 1e-05)
    return (gated_wide * norm_gain[:, None] / rms[None, :]).astype(jnp.bfloat16)


def rolled_order(n):
    return sorted(range(1, n), key=lambda r: (abs(2 * r - n), r))


def kernel(
    n,
    nt,
    n_chunks,
    st_hbm,
    sw_hbm,
    filt_hbm,
    skip_hbm,
    gated_ref,
    rms_ref,
    st,
    sw_ref,
    filt_ref,
    skip_ref,
    edge_out,
    edge_in,
    fix_out,
    fix_in,
    fix_row,
    fix_col,
    local_col,
    direct,
    gated_vmem,
    coef_row,
    coef_col,
    filt_out,
    filt_in,
    filt_f32,
    toep,
    prod,
    query,
    recv,
    res,
    back,
    sq_out,
    sq_in,
    load_sem,
    edge_send,
    edge_recv,
    fix_send,
    fix_recv,
    filt_send,
    filt_recv,
    prod_send,
    prod_recv,
    res_send,
    res_recv,
    sq_send,
    sq_recv,
):
    bf16, f32 = jnp.bfloat16, jnp.float32
    me = lax.axis_index("ctx")
    tp = lax.axis_index("tp")
    taps = sw_ref.shape[0]
    own, width = st.shape[2], st.shape[3]
    chan = n * own
    owned_groups = filt_in.shape[1]
    per_group = own // owned_groups
    rows = own // n_chunks
    order = rolled_order(n)

    small = [
        pltpu.make_async_copy(sw_hbm, sw_ref, load_sem.at[0]),
        pltpu.make_async_copy(skip_hbm, skip_ref, load_sem.at[1]),
        pltpu.make_async_copy(filt_hbm, filt_ref, load_sem.at[2]),
    ]
    loads = []
    for q in range(n_chunks):
        part = pl.ds(q * rows, rows)
        loads.append(
            pltpu.make_async_copy(
                st_hbm.at[:, :, part], st.at[:, :, part], load_sem.at[4 + q]
            )
        )
    for load in small + loads:
        load.start()

    barrier = pltpu.get_barrier_semaphore()
    for r in range(1, n):
        pl.semaphore_signal(
            barrier, inc=1, device_id=(lax.rem(me + r, n), tp), device_id_type=MESH
        )
    for r in range(1, nt):
        pl.semaphore_signal(
            barrier, inc=1, device_id=(me, lax.rem(tp + r, nt)), device_id_type=MESH
        )
    for load in small:
        load.wait()
    coef_row[...] = jnp.zeros_like(coef_row)
    fix_out[...] = jnp.zeros_like(fix_out)
    for j in range(taps):
        for s in range(3):
            coef_row[3 * j + s : 3 * j + s + 1, :] = sw_ref[j, s : s + 1, :]
    coef_row[3 * taps : 3 * taps + 1, :] = skip_ref[...]
    coef_col[...] = coef_row[...].T.reshape(coef_col.shape)
    filt_out[...] = filt_ref[...].astype(bf16)

    def filt_copy(r):
        to = lax.rem(me + r, n)
        return pltpu.make_async_remote_copy(
            src_ref=filt_out.at[pl.ds(pl.multiple_of(to * owned_groups, owned_groups), owned_groups)],
            dst_ref=filt_in.at[me],
            send_sem=filt_send.at[r],
            recv_sem=filt_recv.at[r],
            device_id=(to, tp),
            device_id_type=MESH,
        )

    def prod_copy(q, r):
        to = lax.rem(me + r, n)
        part = pl.ds(q * rows, rows)
        return pltpu.make_async_remote_copy(
            src_ref=prod.at[to, part],
            dst_ref=recv.at[me, part],
            send_sem=prod_send.at[q, r],
            recv_sem=prod_recv.at[q, r],
            device_id=(to, tp),
            device_id_type=MESH,
        )

    def res_copy(q, r):
        to = lax.rem(me + r, n)
        part = pl.ds(q * rows, rows)
        return pltpu.make_async_remote_copy(
            src_ref=res.at[to, part],
            dst_ref=back.at[me, part],
            send_sem=res_send.at[q, r],
            recv_sem=res_recv.at[q, r],
            device_id=(to, tp),
            device_id_type=MESH,
        )

    def fix_copy(r):
        to = lax.rem(me + r, n)
        return pltpu.make_async_remote_copy(
            src_ref=fix_out.at[to],
            dst_ref=fix_in.at[me],
            send_sem=fix_send.at[r],
            recv_sem=fix_recv.at[r],
            device_id=(to, tp),
            device_id_type=MESH,
        )

    edge_copy = pltpu.make_async_remote_copy(
        src_ref=edge_out,
        dst_ref=edge_in,
        send_sem=edge_send,
        recv_sem=edge_recv,
        device_id=(lax.rem(me + 1, n), tp),
        device_id_type=MESH,
    )

    def pick_edges():
        edge = jnp.zeros((16, chan), f32)
        row_id = lax.broadcasted_iota(jnp.int32, (16, width), 0)
        lane_id = lax.broadcasted_iota(jnp.int32, (16, width), 1)
        slot = jnp.where(lane_id < 2, lane_id, lane_id - width + 4)
        at_edge = (lane_id < 2) | (lane_id >= width - 2)
        for s in range(3):
            pick = at_edge & (row_id == 4 * s + slot)
            edge = edge + lax.dot_general(
                pick.astype(f32).astype(bf16),
                st[s].reshape(chan, width),
                (((1,), (1,)), ((), ())),
                preferred_element_type=f32,
            )
        edge_out[...] = edge.astype(bf16)

        @pl.when(me < n - 1)
        def _():
            edge_copy.start()

    def fix_edges():
        fix_row[...] = jnp.zeros_like(fix_row)

        @pl.when(me == 0)
        def _():
            edge_in[...] = jnp.zeros_like(edge_in)

        @pl.when(me > 0)
        def _():
            edge_copy.wait_recv()

        here = edge_out[...].astype(f32)
        left = edge_in[...].astype(f32)
        coef = coef_row[...]
        first, second = [], []
        for s in range(3):
            now, later = here[4 * s : 4 * s + 1], here[4 * s + 1 : 4 * s + 2]
            two, one = left[4 * s + 2 : 4 * s + 3], left[4 * s + 3 : 4 * s + 4]
            w0, w1, w2 = (coef[3 * j + s : 3 * j + s + 1] for j in range(3))
            first.append(w0 * now + w1 * one + w2 * two)
            second.append(w0 * later + w1 * now + w2 * one)
        lines = [
            first[1] * first[2],
            second[1] * second[2],
            first[0],
            second[0],
        ]
        lines = [line.astype(bf16).astype(f32) for line in lines]
        for o in range(n):
            for h in range(own // 128):
                at = o * own + h * 128
                for p in range(2):
                    fix_out[o, 2 * h + p : 2 * h + p + 1, :] = lines[p][:, at : at + 128]
        for i in range(4):
            fix_row[i : i + 1, :] = lines[i]

    k_id = lax.broadcasted_iota(jnp.int32, (width, 2 * width), 0)
    m_id = lax.broadcasted_iota(jnp.int32, (width, 2 * width), 1)
    source = jnp.where(m_id < width, m_id - 1, m_id - width - 2)
    mover = (k_id == source).astype(f32).astype(bf16)
    for q in range(n_chunks):
        if q == 0:
            loads[0].wait()
        part = slice(q * rows, (q + 1) * rows)
        coef = coef_col[:, part, :].reshape(n * rows, coef_col.shape[2])
        conv = []
        for s in range(3):
            now = st[s, :, part, :].reshape(n * rows, width)
            moved = jnp.dot(now, mover, preferred_element_type=f32)
            conv.append(
                coef[:, s : s + 1] * now.astype(f32)
                + coef[:, 3 + s : 4 + s] * moved[:, :width]
                + coef[:, 6 + s : 7 + s] * moved[:, width:]
            )
        query[:, part, :] = conv[0].astype(bf16).reshape(n, rows, width)
        prod[:, part, :] = (conv[1] * conv[2]).astype(bf16).reshape(n, rows, width)
        if q == 0:
            pl.semaphore_wait(barrier, n - 1 + nt - 1)
            for r in order:
                filt_copy(r).start()
        for r in order:
            prod_copy(q, r).start()
        if q == 0:
            filt_in[me] = filt_out[
                pl.ds(pl.multiple_of(me * owned_groups, owned_groups), owned_groups), :
            ]
            for load in loads[1:]:
                load.wait()
            pick_edges()
        recv[me, part, :] = prod[me, part, :]
        if q == n_chunks // 2 - 1:
            fix_edges()
            for r in order:
                fix_copy(r).start()
            fix_in[me] = fix_out[me]

    for r in order:
        filt_copy(r).wait_recv()
    filt_f32[...] = filt_in[...].astype(f32)
    t_id = lax.broadcasted_iota(jnp.int32, (width, width), 1)
    s_id = lax.broadcasted_iota(jnp.int32, (width, width), 0)

    @pl.loop(0, owned_groups)
    def _(g):
        line = jnp.concatenate([filt_f32[j, pl.ds(g, 1), :] for j in range(n)], axis=1)
        line = jnp.broadcast_to(line, (width, n * width))
        turned = pltpu.roll(line, 0, 1, stride=1, stride_axis=0)
        toep[g, :, width:] = turned[:, width:].astype(bf16)
        toep[g, :, :width] = jnp.where(t_id >= s_id, turned[:, :width], 0.0).astype(bf16)

    for r in order:
        fix_copy(r).wait_recv()
    for h in range(own // 128):
        gathered = jnp.concatenate([fix_in[j, 2 * h : 2 * h + 2, :] for j in range(n)], axis=0)
        gathered = jnp.concatenate([gathered, jnp.zeros((width - 2 * n, 128), f32)], axis=0).T
        for j in range(n):
            near = gathered if j == 0 else pltpu.roll(gathered, width - 2 * j, 1)
            fix_col[j, h * 128 : (h + 1) * 128, :] = near
    head = lax.broadcasted_iota(jnp.int32, (n * per_group, width), 1) < 2

    for q in range(n_chunks):
        for r in order:
            prod_copy(q, r).wait_recv()
        per_chunk = rows // per_group

        @pl.loop(0, per_chunk, unroll=True)
        def _(k):
            place = pl.ds(pl.multiple_of(q * rows + k * per_group, per_group), per_group)
            block = recv[:, place, :].reshape(n * per_group, width).astype(f32)
            fixed = fix_col[:, place, :].reshape(n * per_group, width)
            block = jnp.where(head, fixed, block).astype(bf16)
            full = jnp.dot(block, toep[q * per_chunk + k], preferred_element_type=f32)
            for i in range(n):
                total = full[:per_group, i * width : (i + 1) * width]
                for j in range(1, i + 1):
                    total = total + full[
                        j * per_group : (j + 1) * per_group, (i - j) * width : (i - j + 1) * width
                    ]
                res[i, place, :] = total.astype(bf16)

        for r in order:
            res_copy(q, r).start()
        part = slice(q * rows, (q + 1) * rows)
        back[me, part, :] = res[me, part, :]

    local_col[...] = fix_row[...].T.reshape(local_col.shape)
    head = lax.broadcasted_iota(jnp.int32, (n * rows, width), 1) < 2
    for q in range(n_chunks):
        part = slice(q * rows, (q + 1) * rows)
        skip = coef_col[:, part, :].reshape(n * rows, coef_col.shape[2])[:, 3 * taps : 3 * taps + 1]
        fixed = local_col[:, part, :].reshape(n * rows, width)
        value = prod[:, part, :].reshape(n * rows, width).astype(f32)
        direct[:, part, :] = (skip * jnp.where(head, fixed, value)).reshape(n, rows, width)
        fixed = pltpu.roll(fixed, width - 2, 1)
        value = query[:, part, :].reshape(n * rows, width).astype(f32)
        query[:, part, :] = jnp.where(head, fixed, value).astype(bf16).reshape(n, rows, width)

    squares = jnp.zeros((8, width), f32)
    for q in range(n_chunks):
        part = slice(q * rows, (q + 1) * rows)
        for r in order:
            res_copy(q, r).wait_recv()
        far = back[:, part, :].astype(f32)
        gated = (query[:, part, :].astype(f32) * (far + direct[:, part, :])).astype(bf16)
        gated_vmem[:, part, :] = gated
        gated = gated.astype(f32)
        squares = squares + jnp.sum((gated * gated).reshape(n * rows // 8, 8, width), axis=0)
    sq_out[...] = squares

    def sq_copy(r):
        return pltpu.make_async_remote_copy(
            src_ref=sq_out,
            dst_ref=sq_in.at[tp],
            send_sem=sq_send.at[r],
            recv_sem=sq_recv.at[r],
            device_id=(me, lax.rem(tp + r, nt)),
            device_id_type=MESH,
        )

    for r in range(1, nt):
        sq_copy(r).start()
    gated_copy = pltpu.make_async_copy(gated_vmem, gated_ref, load_sem.at[3])
    gated_copy.start()
    sq_in[tp] = squares
    for r in order:
        filt_copy(r).wait_send()
        fix_copy(r).wait_send()
        for q in range(n_chunks):
            prod_copy(q, r).wait_send()
            res_copy(q, r).wait_send()

    @pl.when(me < n - 1)
    def _():
        edge_copy.wait_send()

    for r in range(1, nt):
        sq_copy(r).wait_recv()
    total = jnp.sum(jnp.sum(sq_in[...], axis=0), axis=0, keepdims=True)
    rms_ref[...] = jnp.sqrt(total / (chan * nt) + 1e-05)
    gated_copy.wait()
    for r in range(1, nt):
        sq_copy(r).wait_send()


def fused_shards(streams, short_weight, filters, skip_gain, norm_gain):
    n = lax.axis_size("ctx")
    nt = lax.axis_size("tp")
    chan, width = streams.shape[1:]
    own = chan // n
    owned_groups = filters.shape[0] // n
    n_chunks = 4
    bf16, f32 = jnp.bfloat16, jnp.float32
    vmem = pl.BlockSpec(memory_space=pltpu.VMEM)
    dma = pltpu.SemaphoreType.DMA
    slab = pltpu.VMEM((n, own, width), bf16)
    wide_slab = pltpu.VMEM((n, own, width), f32)
    gated, rms = pl.pallas_call(
        functools.partial(kernel, n, nt, n_chunks),
        out_shape=(
            jax.ShapeDtypeStruct((n, own, width), bf16),
            jax.ShapeDtypeStruct((1, width), f32),
        ),
        in_specs=[pl.BlockSpec(memory_space=pltpu.HBM)] * 4,
        out_specs=(pl.BlockSpec(memory_space=pltpu.HBM), vmem),
        scratch_shapes=[
            pltpu.VMEM((3, n, own, width), bf16),
            pltpu.VMEM(short_weight.shape, f32),
            pltpu.VMEM(filters.shape, f32),
            pltpu.VMEM((1, chan), f32),
            pltpu.VMEM((16, chan), bf16),
            pltpu.VMEM((16, chan), bf16),
            pltpu.VMEM((n, 8, 128), f32),
            pltpu.VMEM((n, 8, 128), f32),
            pltpu.VMEM((128, chan), f32),
            wide_slab,
            wide_slab,
            wide_slab,
            slab,
            pltpu.VMEM((16, chan), f32),
            pltpu.VMEM((n, own, 16), f32),
            pltpu.VMEM((filters.shape[0], width), bf16),
            pltpu.VMEM((n, owned_groups, width), bf16),
            pltpu.VMEM((n, owned_groups, width), f32),
            pltpu.VMEM((owned_groups, width, n * width), bf16),
            slab,
            slab,
            slab,
            slab,
            slab,
            pltpu.VMEM((8, width), f32),
            pltpu.VMEM((nt, 8, width), f32),
            dma((4 + n_chunks,)),
            dma,
            dma,
            dma((n,)),
            dma((n,)),
            dma((n,)),
            dma((n,)),
            dma((n_chunks, n)),
            dma((n_chunks, n)),
            dma((n_chunks, n)),
            dma((n_chunks, n)),
            dma((nt,)),
            dma((nt,)),
        ],
        compiler_params=pltpu.CompilerParams(
            collective_id=0, has_side_effects=True, vmem_limit_bytes=63 * 1024 * 1024
        ),
        name="hyena",
    )(
        streams.reshape(3, n, own, width),
        short_weight,
        filters,
        skip_gain.reshape(1, chan),
    )
    wide = gated.reshape(chan, width).astype(f32)
    return (wide * norm_gain[:, None] / rms).astype(bf16)


def solution(mesh):
    in_specs = (P(None, "tp", "ctx"), P(None, None, "tp"), P("tp", "ctx"), P("tp"), P("tp"))
    out_specs = P("tp", "ctx")
    body = fused_shards if mesh.shape["ctx"] <= 16 else shards
    return jax.shard_map(body, mesh=mesh, in_specs=in_specs, out_specs=out_specs, check_vma=False)
```

```python
import functools
import math

import jax
import jax.numpy as jnp
from jax import lax
from jax.experimental import pallas as pl
from jax.experimental.pallas import tpu as pltpu
from jax.sharding import PartitionSpec as P

highest = lax.Precision.HIGHEST
MESH = pl.DeviceIdType.MESH


def causal_short(padded, weights, length):
    taps = weights.shape[0]
    total = jnp.zeros(padded.shape[:2] + (length,), jnp.float32)
    for offset in range(taps):
        start = taps - 1 - offset
        total = total + weights[offset][:, :, None] * padded[:, :, start : start + length]
    return total


def trig_tables(half_count, row_count):
    periods = 2 * half_count
    total_len = periods * row_count
    freq = lax.iota(jnp.int32, periods)[:, None]
    place = lax.iota(jnp.int32, half_count)[None, :]
    angle_one = (freq * place % periods).astype(jnp.float32) * (2.0 * math.pi / periods)
    cols = lax.iota(jnp.int32, row_count)
    angle_two = (cols[:, None] * cols[None, :] % row_count).astype(jnp.float32) * (
        2.0 * math.pi / row_count
    )
    angle_twist = (freq * cols[None, :] % total_len).astype(jnp.float32) * (
        2.0 * math.pi / total_len
    )
    return (
        jnp.cos(angle_one),
        jnp.sin(angle_one),
        jnp.cos(angle_two),
        jnp.sin(angle_two),
        jnp.cos(angle_twist),
        jnp.sin(angle_twist),
    )


def forward_dft(signal, tables):
    cos_one, sin_one, cos_two, sin_two, cos_tw, sin_tw = tables
    first_re = jnp.einsum("ka,cab->ckb", cos_one, signal, precision=highest)
    first_im = -jnp.einsum("ka,cab->ckb", sin_one, signal, precision=highest)
    turned_re = first_re * cos_tw + first_im * sin_tw
    turned_im = first_im * cos_tw - first_re * sin_tw
    out_re = jnp.einsum("ckb,bq->ckq", turned_re, cos_two, precision=highest) + jnp.einsum(
        "ckb,bq->ckq", turned_im, sin_two, precision=highest
    )
    out_im = jnp.einsum("ckb,bq->ckq", turned_im, cos_two, precision=highest) - jnp.einsum(
        "ckb,bq->ckq", turned_re, sin_two, precision=highest
    )
    return (out_re, out_im)


def inverse_dft(spec_re, spec_im, tables):
    cos_one, sin_one, cos_two, sin_two, cos_tw, sin_tw = tables
    back_re = jnp.einsum("ckq,qb->ckb", spec_re, cos_two, precision=highest) - jnp.einsum(
        "ckq,qb->ckb", spec_im, sin_two, precision=highest
    )
    back_im = jnp.einsum("ckq,qb->ckb", spec_re, sin_two, precision=highest) + jnp.einsum(
        "ckq,qb->ckb", spec_im, cos_two, precision=highest
    )
    turned_re = back_re * cos_tw - back_im * sin_tw
    turned_im = back_re * sin_tw + back_im * cos_tw
    result = jnp.einsum("ka,ckb->cab", cos_one, turned_re, precision=highest) - jnp.einsum(
        "ka,ckb->cab", sin_one, turned_im, precision=highest
    )
    total_len = 2 * cos_one.shape[1] * cos_two.shape[0]
    return result / total_len


def shards(streams, short_weight, filters, skip_gain, norm_gain):
    n_ctx = lax.axis_size("ctx")
    n_width = lax.axis_size("tp")
    tok_rows = streams.shape[2]
    local_chan = streams.shape[1]
    owned = local_chan // n_ctx
    owned_groups = filters.shape[0] // n_ctx
    per_group = owned // owned_groups
    seq_len = tok_rows * n_ctx
    taps = short_weight.shape[0]
    owner_start = lax.axis_index("ctx") * owned
    skip_own = lax.dynamic_slice_in_dim(skip_gain, owner_start, owned, 0)
    filter_own = lax.all_to_all(filters, "ctx", split_axis=0, concat_axis=1, tiled=True)
    raw_own = lax.all_to_all(streams, "ctx", split_axis=1, concat_axis=2, tiled=True)
    weight_own = lax.dynamic_slice_in_dim(short_weight, owner_start, owned, 2)
    padded = jnp.pad(raw_own.astype(jnp.float32), ((0, 0), (0, 0), (taps - 1, 0)))
    conv_own = causal_short(padded, weight_own, seq_len)
    query_own = lax.optimization_barrier(conv_own[0].astype(jnp.bfloat16)).astype(jnp.float32)
    value_own = lax.optimization_barrier((conv_own[1] * conv_own[2]).astype(jnp.bfloat16)).astype(
        jnp.float32
    )
    tables = trig_tables(n_ctx, tok_rows)
    value_re, value_im = forward_dft(value_own.reshape(owned, n_ctx, tok_rows), tables)
    filt_re, filt_im = forward_dft(filter_own.reshape(owned_groups, n_ctx, tok_rows), tables)
    spec_shape = (owned_groups, per_group) + value_re.shape[1:]
    value_re = value_re.reshape(spec_shape)
    value_im = value_im.reshape(spec_shape)
    filt_re = filt_re[:, None]
    filt_im = filt_im[:, None]
    spec_re = (value_re * filt_re - value_im * filt_im).reshape((owned,) + spec_shape[2:])
    spec_im = (value_re * filt_im + value_im * filt_re).reshape((owned,) + spec_shape[2:])
    long_conv = inverse_dft(spec_re, spec_im, tables).reshape(owned, seq_len)
    gated = (query_own * (long_conv + skip_own[:, None] * value_own)).astype(jnp.bfloat16)
    gated_rows = lax.all_to_all(gated, "ctx", split_axis=1, concat_axis=0, tiled=True)
    gated_wide = gated_rows.astype(jnp.float32)
    squares = lax.psum(jnp.sum(gated_wide * gated_wide, axis=0), "tp")
    rms = jnp.sqrt(squares / (local_chan * n_width) + 1e-05)
    return (gated_wide * norm_gain[:, None] / rms[None, :]).astype(jnp.bfloat16)


def rolled_order(n):
    return sorted(range(1, n), key=lambda r: (abs(2 * r - n), r))


def kernel(
    n,
    nt,
    n_chunks,
    st_hbm,
    sw_hbm,
    filt_hbm,
    skip_hbm,
    gated_ref,
    rms_ref,
    st,
    sw_ref,
    filt_ref,
    skip_ref,
    edge_out,
    edge_in,
    fix_out,
    fix_in,
    fix_row,
    fix_col,
    local_col,
    direct,
    gated_vmem,
    coef_row,
    coef_col,
    filt_out,
    filt_in,
    filt_f32,
    toep,
    prod,
    query,
    recv,
    res,
    back,
    sq_out,
    sq_in,
    load_sem,
    edge_send,
    edge_recv,
    fix_send,
    fix_recv,
    filt_send,
    filt_recv,
    prod_send,
    prod_recv,
    res_send,
    res_recv,
    sq_send,
    sq_recv,
):
    bf16, f32 = jnp.bfloat16, jnp.float32
    me = lax.axis_index("ctx")
    tp = lax.axis_index("tp")
    taps = sw_ref.shape[0]
    own, width = st.shape[2], st.shape[3]
    chan = n * own
    owned_groups = filt_in.shape[1]
    per_group = own // owned_groups
    rows = own // n_chunks
    order = rolled_order(n)
    depth = 2

    small = [
        pltpu.make_async_copy(sw_hbm, sw_ref, load_sem.at[0]),
        pltpu.make_async_copy(skip_hbm, skip_ref, load_sem.at[1]),
        pltpu.make_async_copy(filt_hbm, filt_ref, load_sem.at[2]),
    ]
    loads = []
    for q in range(n_chunks):
        part = pl.ds(q * rows, rows)
        loads.append(
            pltpu.make_async_copy(
                st_hbm.at[:, :, part], st.at[:, :, part], load_sem.at[4 + q]
            )
        )
    for load in small + loads:
        load.start()

    barrier = pltpu.get_barrier_semaphore()
    for r in range(1, n):
        pl.semaphore_signal(
            barrier, inc=1, device_id=(lax.rem(me + r, n), tp), device_id_type=MESH
        )
    for r in range(1, nt):
        pl.semaphore_signal(
            barrier, inc=1, device_id=(me, lax.rem(tp + r, nt)), device_id_type=MESH
        )
    for load in small:
        load.wait()
    coef_row[...] = jnp.zeros_like(coef_row)
    fix_out[...] = jnp.zeros_like(fix_out)
    for j in range(taps):
        for s in range(3):
            coef_row[3 * j + s : 3 * j + s + 1, :] = sw_ref[j, s : s + 1, :]
    coef_row[3 * taps : 3 * taps + 1, :] = skip_ref[...]
    coef_col[...] = coef_row[...].T.reshape(coef_col.shape)
    filt_out[...] = filt_ref[...].astype(bf16)

    def filt_copy(r):
        to = lax.rem(me + r, n)
        return pltpu.make_async_remote_copy(
            src_ref=filt_out.at[pl.ds(pl.multiple_of(to * owned_groups, owned_groups), owned_groups)],
            dst_ref=filt_in.at[me],
            send_sem=filt_send.at[r],
            recv_sem=filt_recv.at[r],
            device_id=(to, tp),
            device_id_type=MESH,
        )

    def prod_copy(q, r):
        to = lax.rem(me + r, n)
        part = pl.ds(q * rows, rows)
        return pltpu.make_async_remote_copy(
            src_ref=prod.at[to, part],
            dst_ref=recv.at[me, part],
            send_sem=prod_send.at[q, r],
            recv_sem=prod_recv.at[q, r],
            device_id=(to, tp),
            device_id_type=MESH,
        )

    def res_copy(q, r):
        to = lax.rem(me + r, n)
        part = pl.ds(q * rows, rows)
        return pltpu.make_async_remote_copy(
            src_ref=res.at[to, part],
            dst_ref=back.at[me, part],
            send_sem=res_send.at[q, r],
            recv_sem=res_recv.at[q, r],
            device_id=(to, tp),
            device_id_type=MESH,
        )

    def fix_copy(r):
        to = lax.rem(me + r, n)
        return pltpu.make_async_remote_copy(
            src_ref=fix_out.at[to],
            dst_ref=fix_in.at[me],
            send_sem=fix_send.at[r],
            recv_sem=fix_recv.at[r],
            device_id=(to, tp),
            device_id_type=MESH,
        )

    edge_copy = pltpu.make_async_remote_copy(
        src_ref=edge_out,
        dst_ref=edge_in,
        send_sem=edge_send,
        recv_sem=edge_recv,
        device_id=(lax.rem(me + 1, n), tp),
        device_id_type=MESH,
    )

    def pick_edges():
        edge = jnp.zeros((16, chan), f32)
        row_id = lax.broadcasted_iota(jnp.int32, (16, width), 0)
        lane_id = lax.broadcasted_iota(jnp.int32, (16, width), 1)
        slot = jnp.where(lane_id < 2, lane_id, lane_id - width + 4)
        at_edge = (lane_id < 2) | (lane_id >= width - 2)
        for s in range(3):
            pick = at_edge & (row_id == 4 * s + slot)
            edge = edge + lax.dot_general(
                pick.astype(f32).astype(bf16),
                st[s].reshape(chan, width),
                (((1,), (1,)), ((), ())),
                preferred_element_type=f32,
            )
        edge_out[...] = edge.astype(bf16)

        @pl.when(me < n - 1)
        def _():
            edge_copy.start()

    def fix_edges():
        fix_row[...] = jnp.zeros_like(fix_row)

        @pl.when(me == 0)
        def _():
            edge_in[...] = jnp.zeros_like(edge_in)

        @pl.when(me > 0)
        def _():
            edge_copy.wait_recv()

        here = edge_out[...].astype(f32)
        left = edge_in[...].astype(f32)
        coef = coef_row[...]
        first, second = [], []
        for s in range(3):
            now, later = here[4 * s : 4 * s + 1], here[4 * s + 1 : 4 * s + 2]
            two, one = left[4 * s + 2 : 4 * s + 3], left[4 * s + 3 : 4 * s + 4]
            w0, w1, w2 = (coef[3 * j + s : 3 * j + s + 1] for j in range(3))
            first.append(w0 * now + w1 * one + w2 * two)
            second.append(w0 * later + w1 * now + w2 * one)
        lines = [
            first[1] * first[2],
            second[1] * second[2],
            first[0],
            second[0],
        ]
        lines = [line.astype(bf16).astype(f32) for line in lines]
        for o in range(n):
            for h in range(own // 128):
                at = o * own + h * 128
                for p in range(2):
                    fix_out[o, 2 * h + p : 2 * h + p + 1, :] = lines[p][:, at : at + 128]
        for i in range(4):
            fix_row[i : i + 1, :] = lines[i]

    t_id = lax.broadcasted_iota(jnp.int32, (width, width), 1)
    s_id = lax.broadcasted_iota(jnp.int32, (width, width), 0)

    def build_blocks(start, stop):
        @pl.loop(start, stop)
        def _(g):
            line = jnp.concatenate([filt_f32[j, pl.ds(g, 1), :] for j in range(n)], axis=1)
            line = jnp.broadcast_to(line, (width, n * width))
            turned = pltpu.roll(line, 0, 1, stride=1, stride_axis=0)
            toep[g, :, width:] = turned[:, width:].astype(bf16)
            toep[g, :, :width] = jnp.where(t_id >= s_id, turned[:, :width], 0.0).astype(bf16)

    k_id = lax.broadcasted_iota(jnp.int32, (width, 2 * width), 0)
    m_id = lax.broadcasted_iota(jnp.int32, (width, 2 * width), 1)
    source = jnp.where(m_id < width, m_id - 1, m_id - width - 2)
    mover = (k_id == source).astype(f32).astype(bf16)
    for q in range(n_chunks):
        if q == 0:
            loads[0].wait()
        part = slice(q * rows, (q + 1) * rows)
        coef = coef_col[:, part, :].reshape(n * rows, coef_col.shape[2])
        conv = []
        for s in range(3):
            now = st[s, :, part, :].reshape(n * rows, width)
            moved = jnp.dot(now, mover, preferred_element_type=f32)
            conv.append(
                coef[:, s : s + 1] * now.astype(f32)
                + coef[:, 3 + s : 4 + s] * moved[:, :width]
                + coef[:, 6 + s : 7 + s] * moved[:, width:]
            )
        query[:, part, :] = conv[0].astype(bf16).reshape(n, rows, width)
        prod[:, part, :] = (conv[1] * conv[2]).astype(bf16).reshape(n, rows, width)
        if q == 0:
            pl.semaphore_wait(barrier, n - 1 + nt - 1)
            for r in order:
                filt_copy(r).start()
        if q >= depth:
            for r in order:
                prod_copy(q - depth, r).wait_send()
        for r in order:
            prod_copy(q, r).start()
        if q == 0:
            filt_in[me] = filt_out[
                pl.ds(pl.multiple_of(me * owned_groups, owned_groups), owned_groups), :
            ]
            for load in loads[1:]:
                load.wait()
            pick_edges()
        recv[me, part, :] = prod[me, part, :]
        if q == n_chunks // 2 - 1:
            fix_edges()
            for r in order:
                fix_copy(r).start()
            fix_in[me] = fix_out[me]
        if q >= depth:
            if q == depth:
                for r in order:
                    filt_copy(r).wait_recv()
                filt_f32[...] = filt_in[...].astype(f32)
            span = n_chunks - depth
            build_blocks(
                (q - depth) * owned_groups // span, (q + 1 - depth) * owned_groups // span
            )

    for r in order:
        fix_copy(r).wait_recv()
    for h in range(own // 128):
        gathered = jnp.concatenate([fix_in[j, 2 * h : 2 * h + 2, :] for j in range(n)], axis=0)
        gathered = jnp.concatenate([gathered, jnp.zeros((width - 2 * n, 128), f32)], axis=0).T
        for j in range(n):
            near = gathered if j == 0 else pltpu.roll(gathered, width - 2 * j, 1)
            fix_col[j, h * 128 : (h + 1) * 128, :] = near
    head = lax.broadcasted_iota(jnp.int32, (n * per_group, width), 1) < 2

    for q in range(n_chunks):
        for r in order:
            prod_copy(q, r).wait_recv()
        per_chunk = rows // per_group

        @pl.loop(0, per_chunk, unroll=True)
        def _(k):
            place = pl.ds(pl.multiple_of(q * rows + k * per_group, per_group), per_group)
            block = recv[:, place, :].reshape(n * per_group, width).astype(f32)
            fixed = fix_col[:, place, :].reshape(n * per_group, width)
            block = jnp.where(head, fixed, block).astype(bf16)
            full = jnp.dot(block, toep[q * per_chunk + k], preferred_element_type=f32)
            for i in range(n):
                total = full[:per_group, i * width : (i + 1) * width]
                for j in range(1, i + 1):
                    total = total + full[
                        j * per_group : (j + 1) * per_group, (i - j) * width : (i - j + 1) * width
                    ]
                res[i, place, :] = total.astype(bf16)

        for r in order:
            res_copy(q, r).start()
        part = slice(q * rows, (q + 1) * rows)
        back[me, part, :] = res[me, part, :]

    local_col[...] = fix_row[...].T.reshape(local_col.shape)
    head = lax.broadcasted_iota(jnp.int32, (n * rows, width), 1) < 2
    for q in range(n_chunks):
        part = slice(q * rows, (q + 1) * rows)
        skip = coef_col[:, part, :].reshape(n * rows, coef_col.shape[2])[:, 3 * taps : 3 * taps + 1]
        fixed = local_col[:, part, :].reshape(n * rows, width)
        value = prod[:, part, :].reshape(n * rows, width).astype(f32)
        direct[:, part, :] = (skip * jnp.where(head, fixed, value)).reshape(n, rows, width)
        fixed = pltpu.roll(fixed, width - 2, 1)
        value = query[:, part, :].reshape(n * rows, width).astype(f32)
        query[:, part, :] = jnp.where(head, fixed, value).astype(bf16).reshape(n, rows, width)

    squares = jnp.zeros((8, width), f32)
    for q in range(n_chunks):
        part = slice(q * rows, (q + 1) * rows)
        for r in order:
            res_copy(q, r).wait_recv()
        far = back[:, part, :].astype(f32)
        gated = (query[:, part, :].astype(f32) * (far + direct[:, part, :])).astype(bf16)
        gated_vmem[:, part, :] = gated
        gated = gated.astype(f32)
        squares = squares + jnp.sum((gated * gated).reshape(n * rows // 8, 8, width), axis=0)
    sq_out[...] = squares

    def sq_copy(r):
        return pltpu.make_async_remote_copy(
            src_ref=sq_out,
            dst_ref=sq_in.at[tp],
            send_sem=sq_send.at[r],
            recv_sem=sq_recv.at[r],
            device_id=(me, lax.rem(tp + r, nt)),
            device_id_type=MESH,
        )

    for r in range(1, nt):
        sq_copy(r).start()
    gated_copy = pltpu.make_async_copy(gated_vmem, gated_ref, load_sem.at[3])
    gated_copy.start()
    sq_in[tp] = squares
    for r in order:
        filt_copy(r).wait_send()
        fix_copy(r).wait_send()
        for q in range(n_chunks):
            if q >= n_chunks - depth:
                prod_copy(q, r).wait_send()
            res_copy(q, r).wait_send()

    @pl.when(me < n - 1)
    def _():
        edge_copy.wait_send()

    for r in range(1, nt):
        sq_copy(r).wait_recv()
    total = jnp.sum(jnp.sum(sq_in[...], axis=0), axis=0, keepdims=True)
    rms_ref[...] = jnp.sqrt(total / (chan * nt) + 1e-05)
    gated_copy.wait()
    for r in range(1, nt):
        sq_copy(r).wait_send()


def fused_shards(streams, short_weight, filters, skip_gain, norm_gain):
    n = lax.axis_size("ctx")
    nt = lax.axis_size("tp")
    chan, width = streams.shape[1:]
    own = chan // n
    owned_groups = filters.shape[0] // n
    n_chunks = 4
    bf16, f32 = jnp.bfloat16, jnp.float32
    vmem = pl.BlockSpec(memory_space=pltpu.VMEM)
    dma = pltpu.SemaphoreType.DMA
    slab = pltpu.VMEM((n, own, width), bf16)
    wide_slab = pltpu.VMEM((n, own, width), f32)
    gated, rms = pl.pallas_call(
        functools.partial(kernel, n, nt, n_chunks),
        out_shape=(
            jax.ShapeDtypeStruct((n, own, width), bf16),
            jax.ShapeDtypeStruct((1, width), f32),
        ),
        in_specs=[pl.BlockSpec(memory_space=pltpu.HBM)] * 4,
        out_specs=(pl.BlockSpec(memory_space=pltpu.HBM), vmem),
        scratch_shapes=[
            pltpu.VMEM((3, n, own, width), bf16),
            pltpu.VMEM(short_weight.shape, f32),
            pltpu.VMEM(filters.shape, f32),
            pltpu.VMEM((1, chan), f32),
            pltpu.VMEM((16, chan), bf16),
            pltpu.VMEM((16, chan), bf16),
            pltpu.VMEM((n, 8, 128), f32),
            pltpu.VMEM((n, 8, 128), f32),
            pltpu.VMEM((128, chan), f32),
            wide_slab,
            wide_slab,
            wide_slab,
            slab,
            pltpu.VMEM((16, chan), f32),
            pltpu.VMEM((n, own, 16), f32),
            pltpu.VMEM((filters.shape[0], width), bf16),
            pltpu.VMEM((n, owned_groups, width), bf16),
            pltpu.VMEM((n, owned_groups, width), f32),
            pltpu.VMEM((owned_groups, width, n * width), bf16),
            slab,
            slab,
            slab,
            slab,
            slab,
            pltpu.VMEM((8, width), f32),
            pltpu.VMEM((nt, 8, width), f32),
            dma((4 + n_chunks,)),
            dma,
            dma,
            dma((n,)),
            dma((n,)),
            dma((n,)),
            dma((n,)),
            dma((n_chunks, n)),
            dma((n_chunks, n)),
            dma((n_chunks, n)),
            dma((n_chunks, n)),
            dma((nt,)),
            dma((nt,)),
        ],
        compiler_params=pltpu.CompilerParams(
            collective_id=0, has_side_effects=True, vmem_limit_bytes=63 * 1024 * 1024
        ),
        name="hyena",
    )(
        streams.reshape(3, n, own, width),
        short_weight,
        filters,
        skip_gain.reshape(1, chan),
    )
    wide = gated.reshape(chan, width).astype(f32)
    return (wide * norm_gain[:, None] / rms).astype(bf16)


def solution(mesh):
    in_specs = (P(None, "tp", "ctx"), P(None, None, "tp"), P("tp", "ctx"), P("tp"), P("tp"))
    out_specs = P("tp", "ctx")
    body = fused_shards if mesh.shape["ctx"] <= 16 else shards
    return jax.shard_map(body, mesh=mesh, in_specs=in_specs, out_specs=out_specs, check_vma=False)
```

```python
import functools
import math

import jax
import jax.numpy as jnp
from jax import lax
from jax.experimental import pallas as pl
from jax.experimental.pallas import tpu as pltpu
from jax.sharding import PartitionSpec as P

highest = lax.Precision.HIGHEST
MESH = pl.DeviceIdType.MESH


def causal_short(padded, weights, length):
    taps = weights.shape[0]
    total = jnp.zeros(padded.shape[:2] + (length,), jnp.float32)
    for offset in range(taps):
        start = taps - 1 - offset
        total = total + weights[offset][:, :, None] * padded[:, :, start : start + length]
    return total


def trig_tables(half_count, row_count):
    periods = 2 * half_count
    total_len = periods * row_count
    freq = lax.iota(jnp.int32, periods)[:, None]
    place = lax.iota(jnp.int32, half_count)[None, :]
    angle_one = (freq * place % periods).astype(jnp.float32) * (2.0 * math.pi / periods)
    cols = lax.iota(jnp.int32, row_count)
    angle_two = (cols[:, None] * cols[None, :] % row_count).astype(jnp.float32) * (
        2.0 * math.pi / row_count
    )
    angle_twist = (freq * cols[None, :] % total_len).astype(jnp.float32) * (
        2.0 * math.pi / total_len
    )
    return (
        jnp.cos(angle_one),
        jnp.sin(angle_one),
        jnp.cos(angle_two),
        jnp.sin(angle_two),
        jnp.cos(angle_twist),
        jnp.sin(angle_twist),
    )


def forward_dft(signal, tables):
    cos_one, sin_one, cos_two, sin_two, cos_tw, sin_tw = tables
    first_re = jnp.einsum("ka,cab->ckb", cos_one, signal, precision=highest)
    first_im = -jnp.einsum("ka,cab->ckb", sin_one, signal, precision=highest)
    turned_re = first_re * cos_tw + first_im * sin_tw
    turned_im = first_im * cos_tw - first_re * sin_tw
    out_re = jnp.einsum("ckb,bq->ckq", turned_re, cos_two, precision=highest) + jnp.einsum(
        "ckb,bq->ckq", turned_im, sin_two, precision=highest
    )
    out_im = jnp.einsum("ckb,bq->ckq", turned_im, cos_two, precision=highest) - jnp.einsum(
        "ckb,bq->ckq", turned_re, sin_two, precision=highest
    )
    return (out_re, out_im)


def inverse_dft(spec_re, spec_im, tables):
    cos_one, sin_one, cos_two, sin_two, cos_tw, sin_tw = tables
    back_re = jnp.einsum("ckq,qb->ckb", spec_re, cos_two, precision=highest) - jnp.einsum(
        "ckq,qb->ckb", spec_im, sin_two, precision=highest
    )
    back_im = jnp.einsum("ckq,qb->ckb", spec_re, sin_two, precision=highest) + jnp.einsum(
        "ckq,qb->ckb", spec_im, cos_two, precision=highest
    )
    turned_re = back_re * cos_tw - back_im * sin_tw
    turned_im = back_re * sin_tw + back_im * cos_tw
    result = jnp.einsum("ka,ckb->cab", cos_one, turned_re, precision=highest) - jnp.einsum(
        "ka,ckb->cab", sin_one, turned_im, precision=highest
    )
    total_len = 2 * cos_one.shape[1] * cos_two.shape[0]
    return result / total_len


def shards(streams, short_weight, filters, skip_gain, norm_gain):
    n_ctx = lax.axis_size("ctx")
    n_width = lax.axis_size("tp")
    tok_rows = streams.shape[2]
    local_chan = streams.shape[1]
    owned = local_chan // n_ctx
    owned_groups = filters.shape[0] // n_ctx
    per_group = owned // owned_groups
    seq_len = tok_rows * n_ctx
    taps = short_weight.shape[0]
    owner_start = lax.axis_index("ctx") * owned
    skip_own = lax.dynamic_slice_in_dim(skip_gain, owner_start, owned, 0)
    filter_own = lax.all_to_all(filters, "ctx", split_axis=0, concat_axis=1, tiled=True)
    raw_own = lax.all_to_all(streams, "ctx", split_axis=1, concat_axis=2, tiled=True)
    weight_own = lax.dynamic_slice_in_dim(short_weight, owner_start, owned, 2)
    padded = jnp.pad(raw_own.astype(jnp.float32), ((0, 0), (0, 0), (taps - 1, 0)))
    conv_own = causal_short(padded, weight_own, seq_len)
    query_own = lax.optimization_barrier(conv_own[0].astype(jnp.bfloat16)).astype(jnp.float32)
    value_own = lax.optimization_barrier((conv_own[1] * conv_own[2]).astype(jnp.bfloat16)).astype(
        jnp.float32
    )
    tables = trig_tables(n_ctx, tok_rows)
    value_re, value_im = forward_dft(value_own.reshape(owned, n_ctx, tok_rows), tables)
    filt_re, filt_im = forward_dft(filter_own.reshape(owned_groups, n_ctx, tok_rows), tables)
    spec_shape = (owned_groups, per_group) + value_re.shape[1:]
    value_re = value_re.reshape(spec_shape)
    value_im = value_im.reshape(spec_shape)
    filt_re = filt_re[:, None]
    filt_im = filt_im[:, None]
    spec_re = (value_re * filt_re - value_im * filt_im).reshape((owned,) + spec_shape[2:])
    spec_im = (value_re * filt_im + value_im * filt_re).reshape((owned,) + spec_shape[2:])
    long_conv = inverse_dft(spec_re, spec_im, tables).reshape(owned, seq_len)
    gated = (query_own * (long_conv + skip_own[:, None] * value_own)).astype(jnp.bfloat16)
    gated_rows = lax.all_to_all(gated, "ctx", split_axis=1, concat_axis=0, tiled=True)
    gated_wide = gated_rows.astype(jnp.float32)
    squares = lax.psum(jnp.sum(gated_wide * gated_wide, axis=0), "tp")
    rms = jnp.sqrt(squares / (local_chan * n_width) + 1e-05)
    return (gated_wide * norm_gain[:, None] / rms[None, :]).astype(jnp.bfloat16)


def rolled_order(n):
    return sorted(range(1, n), key=lambda r: (abs(2 * r - n), r))


def kernel(
    n,
    nt,
    n_chunks,
    st_hbm,
    sw_hbm,
    filt_hbm,
    skip_hbm,
    gated_ref,
    rms_ref,
    st,
    sw_ref,
    filt_ref,
    skip_ref,
    edge_out,
    edge_in,
    fix_out,
    fix_in,
    fix_row,
    fix_col,
    local_col,
    direct,
    gated_vmem,
    coef_row,
    coef_col,
    filt_out,
    filt_in,
    filt_f32,
    toep,
    prod,
    query,
    recv,
    res,
    back,
    sq_out,
    sq_in,
    load_sem,
    edge_send,
    edge_recv,
    fix_send,
    fix_recv,
    filt_send,
    filt_recv,
    prod_send,
    prod_recv,
    res_send,
    res_recv,
    sq_send,
    sq_recv,
):
    bf16, f32 = jnp.bfloat16, jnp.float32
    me = lax.axis_index("ctx")
    tp = lax.axis_index("tp")
    taps = sw_ref.shape[0]
    own, width = st.shape[2], st.shape[3]
    chan = n * own
    owned_groups = filt_in.shape[1]
    per_group = own // owned_groups
    rows = own // n_chunks
    order = rolled_order(n)
    depth = 2

    small = [
        pltpu.make_async_copy(sw_hbm, sw_ref, load_sem.at[0]),
        pltpu.make_async_copy(skip_hbm, skip_ref, load_sem.at[1]),
        pltpu.make_async_copy(filt_hbm, filt_ref, load_sem.at[2]),
    ]
    loads = []
    for q in range(n_chunks):
        part = pl.ds(q * rows, rows)
        loads.append(
            pltpu.make_async_copy(
                st_hbm.at[:, :, part], st.at[:, :, part], load_sem.at[4 + q]
            )
        )
    for load in small + loads:
        load.start()

    barrier = pltpu.get_barrier_semaphore()
    for r in range(1, n):
        pl.semaphore_signal(
            barrier, inc=1, device_id=(lax.rem(me + r, n), tp), device_id_type=MESH
        )
    for r in range(1, nt):
        pl.semaphore_signal(
            barrier, inc=1, device_id=(me, lax.rem(tp + r, nt)), device_id_type=MESH
        )
    for load in small:
        load.wait()
    coef_row[...] = jnp.zeros_like(coef_row)
    fix_out[...] = jnp.zeros_like(fix_out)
    for j in range(taps):
        for s in range(3):
            coef_row[3 * j + s : 3 * j + s + 1, :] = sw_ref[j, s : s + 1, :]
    coef_row[3 * taps : 3 * taps + 1, :] = skip_ref[...]
    coef_col[...] = coef_row[...].T.reshape(coef_col.shape)
    filt_out[...] = filt_ref[...].astype(bf16)

    def filt_copy(r):
        to = lax.rem(me + r, n)
        return pltpu.make_async_remote_copy(
            src_ref=filt_out.at[pl.ds(pl.multiple_of(to * owned_groups, owned_groups), owned_groups)],
            dst_ref=filt_in.at[me],
            send_sem=filt_send.at[r],
            recv_sem=filt_recv.at[r],
            device_id=(to, tp),
            device_id_type=MESH,
        )

    def prod_copy(q, r):
        to = lax.rem(me + r, n)
        part = pl.ds(q * rows, rows)
        return pltpu.make_async_remote_copy(
            src_ref=prod.at[to, part],
            dst_ref=recv.at[me, part],
            send_sem=prod_send.at[q, r],
            recv_sem=prod_recv.at[q, r],
            device_id=(to, tp),
            device_id_type=MESH,
        )

    def res_copy(q, r):
        to = lax.rem(me + r, n)
        part = pl.ds(q * rows, rows)
        return pltpu.make_async_remote_copy(
            src_ref=res.at[to, part],
            dst_ref=back.at[me, part],
            send_sem=res_send.at[q, r],
            recv_sem=res_recv.at[q, r],
            device_id=(to, tp),
            device_id_type=MESH,
        )

    def fix_copy(r):
        to = lax.rem(me + r, n)
        return pltpu.make_async_remote_copy(
            src_ref=fix_out.at[to],
            dst_ref=fix_in.at[me],
            send_sem=fix_send.at[r],
            recv_sem=fix_recv.at[r],
            device_id=(to, tp),
            device_id_type=MESH,
        )

    edge_copy = pltpu.make_async_remote_copy(
        src_ref=edge_out,
        dst_ref=edge_in,
        send_sem=edge_send,
        recv_sem=edge_recv,
        device_id=(lax.rem(me + 1, n), tp),
        device_id_type=MESH,
    )

    def pick_edges():
        edge = jnp.zeros((16, chan), f32)
        row_id = lax.broadcasted_iota(jnp.int32, (16, width), 0)
        lane_id = lax.broadcasted_iota(jnp.int32, (16, width), 1)
        slot = jnp.where(lane_id < 2, lane_id, lane_id - width + 4)
        at_edge = (lane_id < 2) | (lane_id >= width - 2)
        for s in range(3):
            pick = at_edge & (row_id == 4 * s + slot)
            edge = edge + lax.dot_general(
                pick.astype(f32).astype(bf16),
                st[s].reshape(chan, width),
                (((1,), (1,)), ((), ())),
                preferred_element_type=f32,
            )
        edge_out[...] = edge.astype(bf16)

        @pl.when(me < n - 1)
        def _():
            edge_copy.start()

    def fix_edges():
        fix_row[...] = jnp.zeros_like(fix_row)

        @pl.when(me == 0)
        def _():
            edge_in[...] = jnp.zeros_like(edge_in)

        @pl.when(me > 0)
        def _():
            edge_copy.wait_recv()

        here = edge_out[...].astype(f32)
        left = edge_in[...].astype(f32)
        coef = coef_row[...]
        first, second = [], []
        for s in range(3):
            now, later = here[4 * s : 4 * s + 1], here[4 * s + 1 : 4 * s + 2]
            two, one = left[4 * s + 2 : 4 * s + 3], left[4 * s + 3 : 4 * s + 4]
            w0, w1, w2 = (coef[3 * j + s : 3 * j + s + 1] for j in range(3))
            first.append(w0 * now + w1 * one + w2 * two)
            second.append(w0 * later + w1 * now + w2 * one)
        lines = [
            first[1] * first[2],
            second[1] * second[2],
            first[0],
            second[0],
        ]
        lines = [line.astype(bf16).astype(f32) for line in lines]
        for o in range(n):
            for h in range(own // 128):
                at = o * own + h * 128
                for p in range(2):
                    fix_out[o, 2 * h + p : 2 * h + p + 1, :] = lines[p][:, at : at + 128]
        for i in range(4):
            fix_row[i : i + 1, :] = lines[i]

    def build_blocks(start, stop):
        @pl.loop(start, stop)
        def _(g):
            line = jnp.concatenate(
                [jnp.zeros((1, width), f32)] + [filt_f32[j, pl.ds(g, 1), :] for j in range(n)],
                axis=1,
            )
            line = jnp.broadcast_to(line, (16, (n + 1) * width))
            base = pltpu.roll(line, 0, 1, stride=1, stride_axis=0).astype(bf16)
            for a in range(width // 16):
                moved = base if a == 0 else pltpu.roll(base, 16 * a, 1)
                toep[g, 16 * a : 16 * (a + 1), :] = moved[:, width:]

    k_id = lax.broadcasted_iota(jnp.int32, (width, 2 * width), 0)
    m_id = lax.broadcasted_iota(jnp.int32, (width, 2 * width), 1)
    source = jnp.where(m_id < width, m_id - 1, m_id - width - 2)
    mover = (k_id == source).astype(f32).astype(bf16)
    for q in range(n_chunks):
        if q == 0:
            loads[0].wait()
        part = slice(q * rows, (q + 1) * rows)
        coef = coef_col[:, part, :].reshape(n * rows, coef_col.shape[2])
        conv = []
        for s in range(3):
            now = st[s, :, part, :].reshape(n * rows, width)
            moved = jnp.dot(now, mover, preferred_element_type=f32)
            conv.append(
                coef[:, s : s + 1] * now.astype(f32)
                + coef[:, 3 + s : 4 + s] * moved[:, :width]
                + coef[:, 6 + s : 7 + s] * moved[:, width:]
            )
        query[:, part, :] = conv[0].astype(bf16).reshape(n, rows, width)
        prod[:, part, :] = (conv[1] * conv[2]).astype(bf16).reshape(n, rows, width)
        if q == 0:
            pl.semaphore_wait(barrier, n - 1 + nt - 1)
            for r in order:
                filt_copy(r).start()
        if q >= depth:
            for r in order:
                prod_copy(q - depth, r).wait_send()
        for r in order:
            prod_copy(q, r).start()
        if q == 0:
            filt_in[me] = filt_out[
                pl.ds(pl.multiple_of(me * owned_groups, owned_groups), owned_groups), :
            ]
            for load in loads[1:]:
                load.wait()
            pick_edges()
        recv[me, part, :] = prod[me, part, :]
        if q == n_chunks // 2 - 1:
            fix_edges()
            for r in order:
                fix_copy(r).start()
            fix_in[me] = fix_out[me]
        if q >= depth:
            if q == depth:
                for r in order:
                    filt_copy(r).wait_recv()
                filt_f32[...] = filt_in[...].astype(f32)
            span = n_chunks - depth
            build_blocks(
                (q - depth) * owned_groups // span, (q + 1 - depth) * owned_groups // span
            )

    for r in order:
        fix_copy(r).wait_recv()
    for h in range(own // 128):
        gathered = jnp.concatenate([fix_in[j, 2 * h : 2 * h + 2, :] for j in range(n)], axis=0)
        gathered = jnp.concatenate([gathered, jnp.zeros((width - 2 * n, 128), f32)], axis=0).T
        for j in range(n):
            near = gathered if j == 0 else pltpu.roll(gathered, width - 2 * j, 1)
            fix_col[j, h * 128 : (h + 1) * 128, :] = near
    head = lax.broadcasted_iota(jnp.int32, (n * per_group, width), 1) < 2

    for q in range(n_chunks):
        for r in order:
            prod_copy(q, r).wait_recv()
        per_chunk = rows // per_group

        @pl.loop(0, per_chunk, unroll=True)
        def _(k):
            place = pl.ds(pl.multiple_of(q * rows + k * per_group, per_group), per_group)
            block = recv[:, place, :].reshape(n * per_group, width).astype(f32)
            fixed = fix_col[:, place, :].reshape(n * per_group, width)
            block = jnp.where(head, fixed, block).astype(bf16)
            half = n // 2
            taps_of = toep[q * per_chunk + k]
            near = jnp.dot(block, taps_of[:, : half * width], preferred_element_type=f32)
            far = jnp.dot(
                block[: half * per_group], taps_of[:, half * width :], preferred_element_type=f32
            )

            def term(j, d):
                full, at = (near, d) if d < half else (far, d - half)
                return full[
                    j * per_group : (j + 1) * per_group, at * width : (at + 1) * width
                ]

            for i in range(n):
                total = term(0, i)
                for j in range(1, i + 1):
                    total = total + term(j, i - j)
                res[i, place, :] = total.astype(bf16)

        for r in order:
            res_copy(q, r).start()
        part = slice(q * rows, (q + 1) * rows)
        back[me, part, :] = res[me, part, :]

    local_col[...] = fix_row[...].T.reshape(local_col.shape)
    head = lax.broadcasted_iota(jnp.int32, (n * rows, width), 1) < 2
    for q in range(n_chunks):
        part = slice(q * rows, (q + 1) * rows)
        skip = coef_col[:, part, :].reshape(n * rows, coef_col.shape[2])[:, 3 * taps : 3 * taps + 1]
        fixed = local_col[:, part, :].reshape(n * rows, width)
        value = prod[:, part, :].reshape(n * rows, width).astype(f32)
        direct[:, part, :] = (skip * jnp.where(head, fixed, value)).reshape(n, rows, width)
        fixed = pltpu.roll(fixed, width - 2, 1)
        value = query[:, part, :].reshape(n * rows, width).astype(f32)
        query[:, part, :] = jnp.where(head, fixed, value).astype(bf16).reshape(n, rows, width)

    squares = jnp.zeros((8, width), f32)
    for q in range(n_chunks):
        part = slice(q * rows, (q + 1) * rows)
        for r in order:
            res_copy(q, r).wait_recv()
        far = back[:, part, :].astype(f32)
        gated = (query[:, part, :].astype(f32) * (far + direct[:, part, :])).astype(bf16)
        gated_vmem[:, part, :] = gated
        gated = gated.astype(f32)
        squares = squares + jnp.sum((gated * gated).reshape(n * rows // 8, 8, width), axis=0)
    sq_out[...] = squares

    def sq_copy(r):
        return pltpu.make_async_remote_copy(
            src_ref=sq_out,
            dst_ref=sq_in.at[tp],
            send_sem=sq_send.at[r],
            recv_sem=sq_recv.at[r],
            device_id=(me, lax.rem(tp + r, nt)),
            device_id_type=MESH,
        )

    for r in range(1, nt):
        sq_copy(r).start()
    gated_copy = pltpu.make_async_copy(gated_vmem, gated_ref, load_sem.at[3])
    gated_copy.start()
    sq_in[tp] = squares
    for r in order:
        filt_copy(r).wait_send()
        fix_copy(r).wait_send()
        for q in range(n_chunks):
            if q >= n_chunks - depth:
                prod_copy(q, r).wait_send()
            res_copy(q, r).wait_send()

    @pl.when(me < n - 1)
    def _():
        edge_copy.wait_send()

    for r in range(1, nt):
        sq_copy(r).wait_recv()
    total = jnp.sum(jnp.sum(sq_in[...], axis=0), axis=0, keepdims=True)
    rms_ref[...] = jnp.sqrt(total / (chan * nt) + 1e-05)
    gated_copy.wait()
    for r in range(1, nt):
        sq_copy(r).wait_send()


def fused_shards(streams, short_weight, filters, skip_gain, norm_gain):
    n = lax.axis_size("ctx")
    nt = lax.axis_size("tp")
    chan, width = streams.shape[1:]
    own = chan // n
    owned_groups = filters.shape[0] // n
    n_chunks = 4
    bf16, f32 = jnp.bfloat16, jnp.float32
    vmem = pl.BlockSpec(memory_space=pltpu.VMEM)
    dma = pltpu.SemaphoreType.DMA
    slab = pltpu.VMEM((n, own, width), bf16)
    wide_slab = pltpu.VMEM((n, own, width), f32)
    gated, rms = pl.pallas_call(
        functools.partial(kernel, n, nt, n_chunks),
        out_shape=(
            jax.ShapeDtypeStruct((n, own, width), bf16),
            jax.ShapeDtypeStruct((1, width), f32),
        ),
        in_specs=[pl.BlockSpec(memory_space=pltpu.HBM)] * 4,
        out_specs=(pl.BlockSpec(memory_space=pltpu.HBM), vmem),
        scratch_shapes=[
            pltpu.VMEM((3, n, own, width), bf16),
            pltpu.VMEM(short_weight.shape, f32),
            pltpu.VMEM(filters.shape, f32),
            pltpu.VMEM((1, chan), f32),
            pltpu.VMEM((16, chan), bf16),
            pltpu.VMEM((16, chan), bf16),
            pltpu.VMEM((n, 8, 128), f32),
            pltpu.VMEM((n, 8, 128), f32),
            pltpu.VMEM((128, chan), f32),
            wide_slab,
            wide_slab,
            wide_slab,
            slab,
            pltpu.VMEM((16, chan), f32),
            pltpu.VMEM((n, own, 16), f32),
            pltpu.VMEM((filters.shape[0], width), bf16),
            pltpu.VMEM((n, owned_groups, width), bf16),
            pltpu.VMEM((n, owned_groups, width), f32),
            pltpu.VMEM((owned_groups, width, n * width), bf16),
            slab,
            slab,
            slab,
            slab,
            slab,
            pltpu.VMEM((8, width), f32),
            pltpu.VMEM((nt, 8, width), f32),
            dma((4 + n_chunks,)),
            dma,
            dma,
            dma((n,)),
            dma((n,)),
            dma((n,)),
            dma((n,)),
            dma((n_chunks, n)),
            dma((n_chunks, n)),
            dma((n_chunks, n)),
            dma((n_chunks, n)),
            dma((nt,)),
            dma((nt,)),
        ],
        compiler_params=pltpu.CompilerParams(
            collective_id=0, has_side_effects=True, vmem_limit_bytes=63 * 1024 * 1024
        ),
        name="hyena",
    )(
        streams.reshape(3, n, own, width),
        short_weight,
        filters,
        skip_gain.reshape(1, chan),
    )
    wide = gated.reshape(chan, width).astype(f32)
    return (wide * norm_gain[:, None] / rms).astype(bf16)


def solution(mesh):
    in_specs = (P(None, "tp", "ctx"), P(None, None, "tp"), P("tp", "ctx"), P("tp"), P("tp"))
    out_specs = P("tp", "ctx")
    body = fused_shards if mesh.shape["ctx"] <= 16 else shards
    return jax.shard_map(body, mesh=mesh, in_specs=in_specs, out_specs=out_specs, check_vma=False)
```

```python
import functools
import math

import jax
import jax.numpy as jnp
from jax import lax
from jax.experimental import pallas as pl
from jax.experimental.pallas import tpu as pltpu
from jax.sharding import PartitionSpec as P

highest = lax.Precision.HIGHEST
MESH = pl.DeviceIdType.MESH


def causal_short(padded, weights, length):
    taps = weights.shape[0]
    total = jnp.zeros(padded.shape[:2] + (length,), jnp.float32)
    for offset in range(taps):
        start = taps - 1 - offset
        total = total + weights[offset][:, :, None] * padded[:, :, start : start + length]
    return total


def trig_tables(half_count, row_count):
    periods = 2 * half_count
    total_len = periods * row_count
    freq = lax.iota(jnp.int32, periods)[:, None]
    place = lax.iota(jnp.int32, half_count)[None, :]
    angle_one = (freq * place % periods).astype(jnp.float32) * (2.0 * math.pi / periods)
    cols = lax.iota(jnp.int32, row_count)
    angle_two = (cols[:, None] * cols[None, :] % row_count).astype(jnp.float32) * (
        2.0 * math.pi / row_count
    )
    angle_twist = (freq * cols[None, :] % total_len).astype(jnp.float32) * (
        2.0 * math.pi / total_len
    )
    return (
        jnp.cos(angle_one),
        jnp.sin(angle_one),
        jnp.cos(angle_two),
        jnp.sin(angle_two),
        jnp.cos(angle_twist),
        jnp.sin(angle_twist),
    )


def forward_dft(signal, tables):
    cos_one, sin_one, cos_two, sin_two, cos_tw, sin_tw = tables
    first_re = jnp.einsum("ka,cab->ckb", cos_one, signal, precision=highest)
    first_im = -jnp.einsum("ka,cab->ckb", sin_one, signal, precision=highest)
    turned_re = first_re * cos_tw + first_im * sin_tw
    turned_im = first_im * cos_tw - first_re * sin_tw
    out_re = jnp.einsum("ckb,bq->ckq", turned_re, cos_two, precision=highest) + jnp.einsum(
        "ckb,bq->ckq", turned_im, sin_two, precision=highest
    )
    out_im = jnp.einsum("ckb,bq->ckq", turned_im, cos_two, precision=highest) - jnp.einsum(
        "ckb,bq->ckq", turned_re, sin_two, precision=highest
    )
    return (out_re, out_im)


def inverse_dft(spec_re, spec_im, tables):
    cos_one, sin_one, cos_two, sin_two, cos_tw, sin_tw = tables
    back_re = jnp.einsum("ckq,qb->ckb", spec_re, cos_two, precision=highest) - jnp.einsum(
        "ckq,qb->ckb", spec_im, sin_two, precision=highest
    )
    back_im = jnp.einsum("ckq,qb->ckb", spec_re, sin_two, precision=highest) + jnp.einsum(
        "ckq,qb->ckb", spec_im, cos_two, precision=highest
    )
    turned_re = back_re * cos_tw - back_im * sin_tw
    turned_im = back_re * sin_tw + back_im * cos_tw
    result = jnp.einsum("ka,ckb->cab", cos_one, turned_re, precision=highest) - jnp.einsum(
        "ka,ckb->cab", sin_one, turned_im, precision=highest
    )
    total_len = 2 * cos_one.shape[1] * cos_two.shape[0]
    return result / total_len


def shards(streams, short_weight, filters, skip_gain, norm_gain):
    n_ctx = lax.axis_size("ctx")
    n_width = lax.axis_size("tp")
    tok_rows = streams.shape[2]
    local_chan = streams.shape[1]
    owned = local_chan // n_ctx
    owned_groups = filters.shape[0] // n_ctx
    per_group = owned // owned_groups
    seq_len = tok_rows * n_ctx
    taps = short_weight.shape[0]
    owner_start = lax.axis_index("ctx") * owned
    skip_own = lax.dynamic_slice_in_dim(skip_gain, owner_start, owned, 0)
    filter_own = lax.all_to_all(filters, "ctx", split_axis=0, concat_axis=1, tiled=True)
    raw_own = lax.all_to_all(streams, "ctx", split_axis=1, concat_axis=2, tiled=True)
    weight_own = lax.dynamic_slice_in_dim(short_weight, owner_start, owned, 2)
    padded = jnp.pad(raw_own.astype(jnp.float32), ((0, 0), (0, 0), (taps - 1, 0)))
    conv_own = causal_short(padded, weight_own, seq_len)
    query_own = lax.optimization_barrier(conv_own[0].astype(jnp.bfloat16)).astype(jnp.float32)
    value_own = lax.optimization_barrier((conv_own[1] * conv_own[2]).astype(jnp.bfloat16)).astype(
        jnp.float32
    )
    tables = trig_tables(n_ctx, tok_rows)
    value_re, value_im = forward_dft(value_own.reshape(owned, n_ctx, tok_rows), tables)
    filt_re, filt_im = forward_dft(filter_own.reshape(owned_groups, n_ctx, tok_rows), tables)
    spec_shape = (owned_groups, per_group) + value_re.shape[1:]
    value_re = value_re.reshape(spec_shape)
    value_im = value_im.reshape(spec_shape)
    filt_re = filt_re[:, None]
    filt_im = filt_im[:, None]
    spec_re = (value_re * filt_re - value_im * filt_im).reshape((owned,) + spec_shape[2:])
    spec_im = (value_re * filt_im + value_im * filt_re).reshape((owned,) + spec_shape[2:])
    long_conv = inverse_dft(spec_re, spec_im, tables).reshape(owned, seq_len)
    gated = (query_own * (long_conv + skip_own[:, None] * value_own)).astype(jnp.bfloat16)
    gated_rows = lax.all_to_all(gated, "ctx", split_axis=1, concat_axis=0, tiled=True)
    gated_wide = gated_rows.astype(jnp.float32)
    squares = lax.psum(jnp.sum(gated_wide * gated_wide, axis=0), "tp")
    rms = jnp.sqrt(squares / (local_chan * n_width) + 1e-05)
    return (gated_wide * norm_gain[:, None] / rms[None, :]).astype(jnp.bfloat16)


def rolled_order(n):
    return sorted(range(1, n), key=lambda r: (abs(2 * r - n), r))


def kernel(
    n,
    nt,
    n_chunks,
    st_hbm,
    sw_hbm,
    filt_hbm,
    skip_hbm,
    gain_hbm,
    out_ref,
    st,
    sw_ref,
    filt_ref,
    skip_ref,
    gain_ref,
    edge_row,
    edge_out,
    edge_in,
    fix_out,
    fix_in,
    fix_row,
    fix_col,
    local_col,
    direct,
    out_vmem,
    coef_row,
    coef_col,
    filt_out,
    filt_in,
    filt_f32,
    toep,
    prod,
    query,
    recv,
    res,
    back,
    sq_out,
    sq_in,
    load_sem,
    store_sem,
    edge_send,
    edge_recv,
    fix_send,
    fix_recv,
    filt_send,
    filt_recv,
    prod_send,
    prod_recv,
    res_send,
    res_recv,
    sq_send,
    sq_recv,
):
    bf16, f32 = jnp.bfloat16, jnp.float32
    me = lax.axis_index("ctx")
    tp = lax.axis_index("tp")
    taps = sw_ref.shape[0]
    own, width = st.shape[2], st.shape[3]
    chan = n * own
    owned_groups = filt_in.shape[1]
    per_group = own // owned_groups
    rows = own // n_chunks
    order = rolled_order(n)
    depth = 2

    small = [
        pltpu.make_async_copy(sw_hbm, sw_ref, load_sem.at[0]),
        pltpu.make_async_copy(skip_hbm, skip_ref, load_sem.at[1]),
        pltpu.make_async_copy(filt_hbm, filt_ref, load_sem.at[2]),
        pltpu.make_async_copy(gain_hbm, gain_ref, load_sem.at[3]),
    ]
    loads = []
    for q in range(n_chunks):
        part = pl.ds(q * rows, rows)
        loads.append(
            pltpu.make_async_copy(
                st_hbm.at[:, :, part], st.at[:, :, part], load_sem.at[4 + q]
            )
        )
    for load in small + loads:
        load.start()

    barrier = pltpu.get_barrier_semaphore()
    for r in range(1, n):
        pl.semaphore_signal(
            barrier, inc=1, device_id=(lax.rem(me + r, n), tp), device_id_type=MESH
        )
    for r in range(1, nt):
        pl.semaphore_signal(
            barrier, inc=1, device_id=(me, lax.rem(tp + r, nt)), device_id_type=MESH
        )
    for load in small:
        load.wait()
    coef_row[...] = jnp.zeros_like(coef_row)
    for j in range(taps):
        for s in range(3):
            coef_row[3 * j + s : 3 * j + s + 1, :] = sw_ref[j, s : s + 1, :]
    coef_row[3 * taps : 3 * taps + 1, :] = skip_ref[...]
    coef_row[3 * taps + 1 : 3 * taps + 2, :] = gain_ref[...]
    coef_col[...] = coef_row[...].T.reshape(coef_col.shape)
    filt_out[...] = filt_ref[...].astype(bf16)

    def filt_copy(r):
        to = lax.rem(me + r, n)
        return pltpu.make_async_remote_copy(
            src_ref=filt_out.at[pl.ds(pl.multiple_of(to * owned_groups, owned_groups), owned_groups)],
            dst_ref=filt_in.at[me],
            send_sem=filt_send.at[r],
            recv_sem=filt_recv.at[r],
            device_id=(to, tp),
            device_id_type=MESH,
        )

    def prod_copy(q, r):
        to = lax.rem(me + r, n)
        part = pl.ds(q * rows, rows)
        return pltpu.make_async_remote_copy(
            src_ref=prod.at[to, part],
            dst_ref=recv.at[me, part],
            send_sem=prod_send.at[q, r],
            recv_sem=prod_recv.at[q, r],
            device_id=(to, tp),
            device_id_type=MESH,
        )

    def res_copy(q, r):
        to = lax.rem(me + r, n)
        part = pl.ds(q * rows, rows)
        return pltpu.make_async_remote_copy(
            src_ref=res.at[to, part],
            dst_ref=back.at[me, part],
            send_sem=res_send.at[q, r],
            recv_sem=res_recv.at[q, r],
            device_id=(to, tp),
            device_id_type=MESH,
        )

    def fix_copy(r):
        to = lax.rem(me + r, n)
        return pltpu.make_async_remote_copy(
            src_ref=fix_out.at[to],
            dst_ref=fix_in.at[me],
            send_sem=fix_send.at[r],
            recv_sem=fix_recv.at[r],
            device_id=(to, tp),
            device_id_type=MESH,
        )

    edge_copy = pltpu.make_async_remote_copy(
        src_ref=edge_out,
        dst_ref=edge_in,
        send_sem=edge_send,
        recv_sem=edge_recv,
        device_id=(lax.rem(me + 1, n), tp),
        device_id_type=MESH,
    )

    def pick_edges():
        edge = jnp.zeros((16, chan), f32)
        row_id = lax.broadcasted_iota(jnp.int32, (16, width), 0)
        lane_id = lax.broadcasted_iota(jnp.int32, (16, width), 1)
        slot = jnp.where(lane_id < 2, lane_id + 8, lane_id - width + 2)
        at_edge = (lane_id < 2) | (lane_id >= width - 2)
        for s in range(3):
            pick = at_edge & (row_id == 2 * s + slot)
            edge = edge + lax.dot_general(
                pick.astype(f32).astype(bf16),
                st[s].reshape(chan, width),
                (((1,), (1,)), ((), ())),
                preferred_element_type=f32,
            )
        edge_row[...] = edge
        edge_out[...] = jnp.concatenate(
            [edge[:8, : chan // 2], edge[:8, chan // 2 :]], axis=0
        ).astype(bf16)

        @pl.when(me < n - 1)
        def _():
            edge_copy.start()

    def fix_edges():
        fix_row[...] = jnp.zeros_like(fix_row)

        @pl.when(me == 0)
        def _():
            edge_in[...] = jnp.zeros_like(edge_in)

        @pl.when(me > 0)
        def _():
            edge_copy.wait_recv()

        here = edge_row[8:, :]
        left = edge_in[...].astype(f32)
        left = jnp.concatenate([left[:8], left[8:]], axis=1)
        coef = coef_row[...]
        first, second = [], []
        for s in range(3):
            now, later = here[2 * s : 2 * s + 1], here[2 * s + 1 : 2 * s + 2]
            two, one = left[2 * s : 2 * s + 1], left[2 * s + 1 : 2 * s + 2]
            w0, w1, w2 = (coef[3 * j + s : 3 * j + s + 1] for j in range(3))
            first.append(w0 * now + w1 * one + w2 * two)
            second.append(w0 * later + w1 * now + w2 * one)
        lines = [
            first[1] * first[2],
            second[1] * second[2],
            first[0],
            second[0],
        ]
        lines = [line.astype(bf16).astype(f32) for line in lines]
        for o in range(n):
            for h in range(own // 128):
                at = o * own + h * 128
                for p in range(2):
                    fix_out[o, 2 * h + p : 2 * h + p + 1, :] = lines[p][:, at : at + 128]
        for i in range(4):
            fix_row[i : i + 1, :] = lines[i]

    def build_blocks(start, stop):
        @pl.loop(start, stop)
        def _(g):
            line = jnp.concatenate(
                [jnp.zeros((1, width), f32)] + [filt_f32[j, pl.ds(g, 1), :] for j in range(n)],
                axis=1,
            )
            line = jnp.broadcast_to(line, (16, (n + 1) * width))
            base = pltpu.roll(line, 0, 1, stride=1, stride_axis=0).astype(bf16)
            for a in range(width // 16):
                moved = base if a == 0 else pltpu.roll(base, 16 * a, 1)
                toep[g, 16 * a : 16 * (a + 1), :] = moved[:, width:]

    k_id = lax.broadcasted_iota(jnp.int32, (width, 2 * width), 0)
    m_id = lax.broadcasted_iota(jnp.int32, (width, 2 * width), 1)
    source = jnp.where(m_id < width, m_id - 1, m_id - width - 2)
    mover = (k_id == source).astype(f32).astype(bf16)
    for q in range(n_chunks):
        if q == 0:
            loads[0].wait()
        part = slice(q * rows, (q + 1) * rows)
        coef = coef_col[:, part, :].reshape(n * rows, coef_col.shape[2])
        conv = []
        for s in range(3):
            now = st[s, :, part, :].reshape(n * rows, width)
            moved = jnp.dot(now, mover, preferred_element_type=f32)
            conv.append(
                coef[:, s : s + 1] * now.astype(f32)
                + coef[:, 3 + s : 4 + s] * moved[:, :width]
                + coef[:, 6 + s : 7 + s] * moved[:, width:]
            )
        query[:, part, :] = conv[0].astype(bf16).reshape(n, rows, width)
        prod[:, part, :] = (conv[1] * conv[2]).astype(bf16).reshape(n, rows, width)
        if q == 0:
            pl.semaphore_wait(barrier, n - 1 + nt - 1)
            for r in order:
                filt_copy(r).start()
        if q >= depth:
            for r in order:
                prod_copy(q - depth, r).wait_send()
        for r in order:
            prod_copy(q, r).start()
        if q == 0:
            filt_in[me] = filt_out[
                pl.ds(pl.multiple_of(me * owned_groups, owned_groups), owned_groups), :
            ]
            for load in loads[1:]:
                load.wait()
            pick_edges()
        recv[me, part, :] = prod[me, part, :]
        if q == n_chunks // 2 - 1:
            fix_edges()
            for r in order:
                fix_copy(r).start()
            fix_in[me] = fix_out[me]
        if q >= depth:
            if q == depth:
                for r in order:
                    filt_copy(r).wait_recv()
                filt_f32[...] = filt_in[...].astype(f32)
            span = n_chunks - depth
            build_blocks(
                (q - depth) * owned_groups // span, (q + 1 - depth) * owned_groups // span
            )

    for r in order:
        fix_copy(r).wait_recv()
    for h in range(own // 128):
        gathered = jnp.concatenate([fix_in[j, 2 * h : 2 * h + 2, :] for j in range(n)], axis=0)
        gathered = jnp.concatenate([gathered, jnp.zeros((width - 2 * n, 128), f32)], axis=0).T
        for j in range(n):
            near = gathered if j == 0 else pltpu.roll(gathered, width - 2 * j, 1)
            fix_col[j, h * 128 : (h + 1) * 128, :] = near
    head = lax.broadcasted_iota(jnp.int32, (n * per_group, width), 1) < 2

    for q in range(n_chunks):
        for r in order:
            prod_copy(q, r).wait_recv()
        per_chunk = rows // per_group

        @pl.loop(0, per_chunk, unroll=True)
        def _(k):
            place = pl.ds(pl.multiple_of(q * rows + k * per_group, per_group), per_group)
            block = recv[:, place, :].reshape(n * per_group, width).astype(f32)
            fixed = fix_col[:, place, :].reshape(n * per_group, width)
            block = jnp.where(head, fixed, block).astype(bf16)
            half = n // 2
            taps_of = toep[q * per_chunk + k]
            near = jnp.dot(block, taps_of[:, : half * width], preferred_element_type=f32)
            far = jnp.dot(
                block[: half * per_group], taps_of[:, half * width :], preferred_element_type=f32
            )

            def term(j, d):
                full, at = (near, d) if d < half else (far, d - half)
                return full[
                    j * per_group : (j + 1) * per_group, at * width : (at + 1) * width
                ]

            for i in range(n):
                total = term(0, i)
                for j in range(1, i + 1):
                    total = total + term(j, i - j)
                res[i, place, :] = total.astype(bf16)

        for r in order:
            res_copy(q, r).start()
        part = slice(q * rows, (q + 1) * rows)
        back[me, part, :] = res[me, part, :]

    local_col[...] = fix_row[...].T.reshape(local_col.shape)
    head = lax.broadcasted_iota(jnp.int32, (n * rows, width), 1) < 2
    for q in range(n_chunks):
        part = slice(q * rows, (q + 1) * rows)
        skip = coef_col[:, part, :].reshape(n * rows, coef_col.shape[2])[:, 3 * taps : 3 * taps + 1]
        fixed = local_col[:, part, :].reshape(n * rows, width)
        value = prod[:, part, :].reshape(n * rows, width).astype(f32)
        direct[:, part, :] = (skip * jnp.where(head, fixed, value)).reshape(n, rows, width)
        fixed = pltpu.roll(fixed, width - 2, 1)
        value = query[:, part, :].reshape(n * rows, width).astype(f32)
        query[:, part, :] = jnp.where(head, fixed, value).astype(bf16).reshape(n, rows, width)

    squares = jnp.zeros((8, width), f32)
    for q in range(n_chunks):
        part = slice(q * rows, (q + 1) * rows)
        for r in order:
            res_copy(q, r).wait_recv()
        far = back[:, part, :].astype(f32)
        gated = (query[:, part, :].astype(f32) * (far + direct[:, part, :])).astype(bf16)
        gated = gated.astype(f32)
        gain = coef_col[:, part, :][:, :, 3 * taps + 1 : 3 * taps + 2]
        direct[:, part, :] = gated * gain
        squares = squares + jnp.sum((gated * gated).reshape(n * rows // 8, 8, width), axis=0)
    sq_out[...] = squares

    def sq_copy(r):
        return pltpu.make_async_remote_copy(
            src_ref=sq_out,
            dst_ref=sq_in.at[tp],
            send_sem=sq_send.at[r],
            recv_sem=sq_recv.at[r],
            device_id=(me, lax.rem(tp + r, nt)),
            device_id_type=MESH,
        )

    for r in range(1, nt):
        sq_copy(r).start()
    sq_in[tp] = squares
    for r in order:
        filt_copy(r).wait_send()
        fix_copy(r).wait_send()
        for q in range(n_chunks):
            if q >= n_chunks - depth:
                prod_copy(q, r).wait_send()
            res_copy(q, r).wait_send()

    @pl.when(me < n - 1)
    def _():
        edge_copy.wait_send()

    for r in range(1, nt):
        sq_copy(r).wait_recv()
    total = jnp.sum(jnp.sum(sq_in[...], axis=0), axis=0, keepdims=True)
    inverse = 1.0 / jnp.sqrt(total / (chan * nt) + 1e-05)
    stores = []
    for part in range(4):
        some = pl.ds(part * n // 4, n // 4)
        out_vmem[some] = (direct[some] * inverse).astype(bf16)
        stores.append(
            pltpu.make_async_copy(out_vmem.at[some], out_ref.at[some], store_sem.at[part])
        )
        stores[-1].start()
    for store in stores:
        store.wait()
    for r in range(1, nt):
        sq_copy(r).wait_send()


def fused_shards(streams, short_weight, filters, skip_gain, norm_gain):
    n = lax.axis_size("ctx")
    nt = lax.axis_size("tp")
    chan, width = streams.shape[1:]
    own = chan // n
    owned_groups = filters.shape[0] // n
    n_chunks = 4
    bf16, f32 = jnp.bfloat16, jnp.float32
    dma = pltpu.SemaphoreType.DMA
    slab = pltpu.VMEM((n, own, width), bf16)
    wide_slab = pltpu.VMEM((n, own, width), f32)
    result = pl.pallas_call(
        functools.partial(kernel, n, nt, n_chunks),
        out_shape=jax.ShapeDtypeStruct((n, own, width), bf16),
        in_specs=[pl.BlockSpec(memory_space=pltpu.HBM)] * 5,
        out_specs=pl.BlockSpec(memory_space=pltpu.HBM),
        scratch_shapes=[
            pltpu.VMEM((3, n, own, width), bf16),
            pltpu.VMEM(short_weight.shape, f32),
            pltpu.VMEM(filters.shape, f32),
            pltpu.VMEM((1, chan), f32),
            pltpu.VMEM((1, chan), f32),
            pltpu.VMEM((16, chan), f32),
            pltpu.VMEM((16, chan // 2), bf16),
            pltpu.VMEM((16, chan // 2), bf16),
            pltpu.VMEM((n, own // 64, 128), f32),
            pltpu.VMEM((n, own // 64, 128), f32),
            pltpu.VMEM((128, chan), f32),
            wide_slab,
            wide_slab,
            wide_slab,
            slab,
            pltpu.VMEM((16, chan), f32),
            pltpu.VMEM((n, own, 16), f32),
            pltpu.VMEM((filters.shape[0], width), bf16),
            pltpu.VMEM((n, owned_groups, width), bf16),
            pltpu.VMEM((n, owned_groups, width), f32),
            pltpu.VMEM((owned_groups, width, n * width), bf16),
            slab,
            slab,
            slab,
            slab,
            slab,
            pltpu.VMEM((8, width), f32),
            pltpu.VMEM((nt, 8, width), f32),
            dma((4 + n_chunks,)),
            dma((4,)),
            dma,
            dma,
            dma((n,)),
            dma((n,)),
            dma((n,)),
            dma((n,)),
            dma((n_chunks, n)),
            dma((n_chunks, n)),
            dma((n_chunks, n)),
            dma((n_chunks, n)),
            dma((nt,)),
            dma((nt,)),
        ],
        compiler_params=pltpu.CompilerParams(
            collective_id=0, has_side_effects=True, vmem_limit_bytes=63 * 1024 * 1024
        ),
        name="hyena",
    )(
        streams.reshape(3, n, own, width),
        short_weight,
        filters,
        skip_gain.reshape(1, chan),
        norm_gain.reshape(1, chan),
    )
    return result.reshape(chan, width)


def solution(mesh):
    in_specs = (P(None, "tp", "ctx"), P(None, None, "tp"), P("tp", "ctx"), P("tp"), P("tp"))
    out_specs = P("tp", "ctx")
    body = fused_shards if mesh.shape["ctx"] <= 16 else shards
    return jax.shard_map(body, mesh=mesh, in_specs=in_specs, out_specs=out_specs, check_vma=False)
```

```python
import functools
import math

import jax
import jax.numpy as jnp
from jax import lax
from jax.experimental import pallas as pl
from jax.experimental.pallas import tpu as pltpu
from jax.sharding import PartitionSpec as P

highest = lax.Precision.HIGHEST
MESH = pl.DeviceIdType.MESH


def causal_short(padded, weights, length):
    taps = weights.shape[0]
    total = jnp.zeros(padded.shape[:2] + (length,), jnp.float32)
    for offset in range(taps):
        start = taps - 1 - offset
        total = total + weights[offset][:, :, None] * padded[:, :, start : start + length]
    return total


def trig_tables(half_count, row_count):
    periods = 2 * half_count
    total_len = periods * row_count
    freq = lax.iota(jnp.int32, periods)[:, None]
    place = lax.iota(jnp.int32, half_count)[None, :]
    angle_one = (freq * place % periods).astype(jnp.float32) * (2.0 * math.pi / periods)
    cols = lax.iota(jnp.int32, row_count)
    angle_two = (cols[:, None] * cols[None, :] % row_count).astype(jnp.float32) * (
        2.0 * math.pi / row_count
    )
    angle_twist = (freq * cols[None, :] % total_len).astype(jnp.float32) * (
        2.0 * math.pi / total_len
    )
    return (
        jnp.cos(angle_one),
        jnp.sin(angle_one),
        jnp.cos(angle_two),
        jnp.sin(angle_two),
        jnp.cos(angle_twist),
        jnp.sin(angle_twist),
    )


def forward_dft(signal, tables):
    cos_one, sin_one, cos_two, sin_two, cos_tw, sin_tw = tables
    first_re = jnp.einsum("ka,cab->ckb", cos_one, signal, precision=highest)
    first_im = -jnp.einsum("ka,cab->ckb", sin_one, signal, precision=highest)
    turned_re = first_re * cos_tw + first_im * sin_tw
    turned_im = first_im * cos_tw - first_re * sin_tw
    out_re = jnp.einsum("ckb,bq->ckq", turned_re, cos_two, precision=highest) + jnp.einsum(
        "ckb,bq->ckq", turned_im, sin_two, precision=highest
    )
    out_im = jnp.einsum("ckb,bq->ckq", turned_im, cos_two, precision=highest) - jnp.einsum(
        "ckb,bq->ckq", turned_re, sin_two, precision=highest
    )
    return (out_re, out_im)


def inverse_dft(spec_re, spec_im, tables):
    cos_one, sin_one, cos_two, sin_two, cos_tw, sin_tw = tables
    back_re = jnp.einsum("ckq,qb->ckb", spec_re, cos_two, precision=highest) - jnp.einsum(
        "ckq,qb->ckb", spec_im, sin_two, precision=highest
    )
    back_im = jnp.einsum("ckq,qb->ckb", spec_re, sin_two, precision=highest) + jnp.einsum(
        "ckq,qb->ckb", spec_im, cos_two, precision=highest
    )
    turned_re = back_re * cos_tw - back_im * sin_tw
    turned_im = back_re * sin_tw + back_im * cos_tw
    result = jnp.einsum("ka,ckb->cab", cos_one, turned_re, precision=highest) - jnp.einsum(
        "ka,ckb->cab", sin_one, turned_im, precision=highest
    )
    total_len = 2 * cos_one.shape[1] * cos_two.shape[0]
    return result / total_len


def shards(streams, short_weight, filters, skip_gain, norm_gain):
    n_ctx = lax.axis_size("ctx")
    n_width = lax.axis_size("tp")
    tok_rows = streams.shape[2]
    local_chan = streams.shape[1]
    owned = local_chan // n_ctx
    owned_groups = filters.shape[0] // n_ctx
    per_group = owned // owned_groups
    seq_len = tok_rows * n_ctx
    taps = short_weight.shape[0]
    owner_start = lax.axis_index("ctx") * owned
    skip_own = lax.dynamic_slice_in_dim(skip_gain, owner_start, owned, 0)
    filter_own = lax.all_to_all(filters, "ctx", split_axis=0, concat_axis=1, tiled=True)
    raw_own = lax.all_to_all(streams, "ctx", split_axis=1, concat_axis=2, tiled=True)
    weight_own = lax.dynamic_slice_in_dim(short_weight, owner_start, owned, 2)
    padded = jnp.pad(raw_own.astype(jnp.float32), ((0, 0), (0, 0), (taps - 1, 0)))
    conv_own = causal_short(padded, weight_own, seq_len)
    query_own = lax.optimization_barrier(conv_own[0].astype(jnp.bfloat16)).astype(jnp.float32)
    value_own = lax.optimization_barrier((conv_own[1] * conv_own[2]).astype(jnp.bfloat16)).astype(
        jnp.float32
    )
    tables = trig_tables(n_ctx, tok_rows)
    value_re, value_im = forward_dft(value_own.reshape(owned, n_ctx, tok_rows), tables)
    filt_re, filt_im = forward_dft(filter_own.reshape(owned_groups, n_ctx, tok_rows), tables)
    spec_shape = (owned_groups, per_group) + value_re.shape[1:]
    value_re = value_re.reshape(spec_shape)
    value_im = value_im.reshape(spec_shape)
    filt_re = filt_re[:, None]
    filt_im = filt_im[:, None]
    spec_re = (value_re * filt_re - value_im * filt_im).reshape((owned,) + spec_shape[2:])
    spec_im = (value_re * filt_im + value_im * filt_re).reshape((owned,) + spec_shape[2:])
    long_conv = inverse_dft(spec_re, spec_im, tables).reshape(owned, seq_len)
    gated = (query_own * (long_conv + skip_own[:, None] * value_own)).astype(jnp.bfloat16)
    gated_rows = lax.all_to_all(gated, "ctx", split_axis=1, concat_axis=0, tiled=True)
    gated_wide = gated_rows.astype(jnp.float32)
    squares = lax.psum(jnp.sum(gated_wide * gated_wide, axis=0), "tp")
    rms = jnp.sqrt(squares / (local_chan * n_width) + 1e-05)
    return (gated_wide * norm_gain[:, None] / rms[None, :]).astype(jnp.bfloat16)


def rolled_order(n):
    return sorted(range(1, n), key=lambda r: (abs(2 * r - n), r))


def kernel(
    n,
    nt,
    n_chunks,
    st_hbm,
    sw_hbm,
    filt_hbm,
    skip_hbm,
    gain_hbm,
    out_ref,
    st,
    sw_ref,
    filt_ref,
    skip_ref,
    gain_ref,
    edge_row,
    edge_out,
    edge_in,
    fix_out,
    fix_in,
    fix_row,
    fix_col,
    local_col,
    direct,
    out_vmem,
    coef_row,
    coef_col,
    filt_out,
    filt_in,
    filt_f32,
    toep,
    prod,
    query,
    recv,
    res,
    back,
    sq_out,
    sq_in,
    load_sem,
    store_sem,
    edge_send,
    edge_recv,
    fix_send,
    fix_recv,
    filt_send,
    filt_recv,
    prod_send,
    prod_recv,
    res_send,
    res_recv,
    sq_send,
    sq_recv,
):
    bf16, f32 = jnp.bfloat16, jnp.float32
    me = lax.axis_index("ctx")
    tp = lax.axis_index("tp")
    taps = sw_ref.shape[0]
    own, width = st.shape[2], st.shape[3]
    chan = n * own
    owned_groups = filt_in.shape[1]
    per_group = own // owned_groups
    rows = own // n_chunks
    order = rolled_order(n)
    depth = 4

    small = [
        pltpu.make_async_copy(sw_hbm, sw_ref, load_sem.at[0]),
        pltpu.make_async_copy(skip_hbm, skip_ref, load_sem.at[1]),
        pltpu.make_async_copy(filt_hbm, filt_ref, load_sem.at[2]),
        pltpu.make_async_copy(gain_hbm, gain_ref, load_sem.at[3]),
    ]
    loads = []
    for q in range(n_chunks):
        part = pl.ds(q * rows, rows)
        loads.append(
            pltpu.make_async_copy(
                st_hbm.at[:, :, part], st.at[:, :, part], load_sem.at[4 + q]
            )
        )
    for load in small + loads:
        load.start()

    barrier = pltpu.get_barrier_semaphore()
    for r in range(1, n):
        pl.semaphore_signal(
            barrier, inc=1, device_id=(lax.rem(me + r, n), tp), device_id_type=MESH
        )
    for r in range(1, nt):
        pl.semaphore_signal(
            barrier, inc=1, device_id=(me, lax.rem(tp + r, nt)), device_id_type=MESH
        )
    for load in small:
        load.wait()
    coef_row[...] = jnp.zeros_like(coef_row)
    for j in range(taps):
        for s in range(3):
            coef_row[3 * j + s : 3 * j + s + 1, :] = sw_ref[j, s : s + 1, :]
    coef_row[3 * taps : 3 * taps + 1, :] = skip_ref[...]
    coef_row[3 * taps + 1 : 3 * taps + 2, :] = gain_ref[...]
    coef_col[...] = coef_row[...].T.reshape(coef_col.shape)
    filt_out[...] = filt_ref[...].astype(bf16)

    def filt_copy(r):
        to = lax.rem(me + r, n)
        return pltpu.make_async_remote_copy(
            src_ref=filt_out.at[pl.ds(pl.multiple_of(to * owned_groups, owned_groups), owned_groups)],
            dst_ref=filt_in.at[me],
            send_sem=filt_send.at[r],
            recv_sem=filt_recv.at[r],
            device_id=(to, tp),
            device_id_type=MESH,
        )

    def prod_copy(q, r):
        to = lax.rem(me + r, n)
        part = pl.ds(q * rows, rows)
        return pltpu.make_async_remote_copy(
            src_ref=prod.at[to, part],
            dst_ref=recv.at[me, part],
            send_sem=prod_send.at[q, r],
            recv_sem=prod_recv.at[q, r],
            device_id=(to, tp),
            device_id_type=MESH,
        )

    def res_copy(q, r):
        to = lax.rem(me + r, n)
        part = pl.ds(q * rows, rows)
        return pltpu.make_async_remote_copy(
            src_ref=res.at[to, part],
            dst_ref=back.at[me, part],
            send_sem=res_send.at[q, r],
            recv_sem=res_recv.at[q, r],
            device_id=(to, tp),
            device_id_type=MESH,
        )

    def fix_copy(r):
        to = lax.rem(me + r, n)
        return pltpu.make_async_remote_copy(
            src_ref=fix_out.at[to],
            dst_ref=fix_in.at[me],
            send_sem=fix_send.at[r],
            recv_sem=fix_recv.at[r],
            device_id=(to, tp),
            device_id_type=MESH,
        )

    edge_copy = pltpu.make_async_remote_copy(
        src_ref=edge_out,
        dst_ref=edge_in,
        send_sem=edge_send,
        recv_sem=edge_recv,
        device_id=(lax.rem(me + 1, n), tp),
        device_id_type=MESH,
    )

    def pick_edges():
        edge = jnp.zeros((16, chan), f32)
        row_id = lax.broadcasted_iota(jnp.int32, (16, width), 0)
        lane_id = lax.broadcasted_iota(jnp.int32, (16, width), 1)
        slot = jnp.where(lane_id < 2, lane_id + 8, lane_id - width + 2)
        at_edge = (lane_id < 2) | (lane_id >= width - 2)
        for s in range(3):
            pick = at_edge & (row_id == 2 * s + slot)
            edge = edge + lax.dot_general(
                pick.astype(f32).astype(bf16),
                st[s].reshape(chan, width),
                (((1,), (1,)), ((), ())),
                preferred_element_type=f32,
            )
        edge_row[...] = edge
        edge_out[...] = jnp.concatenate(
            [edge[:8, : chan // 2], edge[:8, chan // 2 :]], axis=0
        ).astype(bf16)

        @pl.when(me < n - 1)
        def _():
            edge_copy.start()

    def fix_edges():
        fix_row[...] = jnp.zeros_like(fix_row)

        @pl.when(me == 0)
        def _():
            edge_in[...] = jnp.zeros_like(edge_in)

        @pl.when(me > 0)
        def _():
            edge_copy.wait_recv()

        here = edge_row[8:, :]
        left = edge_in[...].astype(f32)
        left = jnp.concatenate([left[:8], left[8:]], axis=1)
        coef = coef_row[...]
        first, second = [], []
        for s in range(3):
            now, later = here[2 * s : 2 * s + 1], here[2 * s + 1 : 2 * s + 2]
            two, one = left[2 * s : 2 * s + 1], left[2 * s + 1 : 2 * s + 2]
            w0, w1, w2 = (coef[3 * j + s : 3 * j + s + 1] for j in range(3))
            first.append(w0 * now + w1 * one + w2 * two)
            second.append(w0 * later + w1 * now + w2 * one)
        lines = [
            first[1] * first[2],
            second[1] * second[2],
            first[0],
            second[0],
        ]
        lines = [line.astype(bf16).astype(f32) for line in lines]
        for o in range(n):
            for h in range(own // 128):
                at = o * own + h * 128
                for p in range(2):
                    fix_out[o, 2 * h + p : 2 * h + p + 1, :] = lines[p][:, at : at + 128]
        for i in range(4):
            fix_row[i : i + 1, :] = lines[i]

    def build_blocks(start, stop):
        @pl.loop(start, stop)
        def _(g):
            line = jnp.concatenate(
                [jnp.zeros((1, width), f32)] + [filt_f32[j, pl.ds(g, 1), :] for j in range(n)],
                axis=1,
            )
            line = jnp.broadcast_to(line, (16, (n + 1) * width))
            base = pltpu.roll(line, 0, 1, stride=1, stride_axis=0).astype(bf16)
            for a in range(width // 16):
                moved = base if a == 0 else pltpu.roll(base, 16 * a, 1)
                toep[g, 16 * a : 16 * (a + 1), :] = moved[:, width:]

    k_id = lax.broadcasted_iota(jnp.int32, (width, 2 * width), 0)
    m_id = lax.broadcasted_iota(jnp.int32, (width, 2 * width), 1)
    source = jnp.where(m_id < width, m_id - 1, m_id - width - 2)
    mover = (k_id == source).astype(f32).astype(bf16)
    for q in range(n_chunks):
        if q == 0:
            loads[0].wait()
        part = slice(q * rows, (q + 1) * rows)
        coef = coef_col[:, part, :].reshape(n * rows, coef_col.shape[2])
        conv = []
        for s in range(3):
            now = st[s, :, part, :].reshape(n * rows, width)
            moved = jnp.dot(now, mover, preferred_element_type=f32)
            conv.append(
                coef[:, s : s + 1] * now.astype(f32)
                + coef[:, 3 + s : 4 + s] * moved[:, :width]
                + coef[:, 6 + s : 7 + s] * moved[:, width:]
            )
        query[:, part, :] = conv[0].astype(bf16).reshape(n, rows, width)
        prod[:, part, :] = (conv[1] * conv[2]).astype(bf16).reshape(n, rows, width)
        if q == 0:
            pl.semaphore_wait(barrier, n - 1 + nt - 1)
            for r in order:
                filt_copy(r).start()
        if q >= depth:
            for r in order:
                prod_copy(q - depth, r).wait_send()
        for r in order:
            prod_copy(q, r).start()
        if q == 0:
            filt_in[me] = filt_out[
                pl.ds(pl.multiple_of(me * owned_groups, owned_groups), owned_groups), :
            ]
            for load in loads[1:]:
                load.wait()
            pick_edges()
        recv[me, part, :] = prod[me, part, :]
        if q == n_chunks // 4:
            fix_edges()
            for r in order:
                fix_copy(r).start()
            fix_in[me] = fix_out[me]
        if q >= depth:
            if q == depth:
                for r in order:
                    filt_copy(r).wait_recv()
                filt_f32[...] = filt_in[...].astype(f32)
            span = n_chunks - depth
            build_blocks(
                (q - depth) * owned_groups // span, (q + 1 - depth) * owned_groups // span
            )

    for r in order:
        fix_copy(r).wait_recv()
    for h in range(own // 128):
        gathered = jnp.concatenate([fix_in[j, 2 * h : 2 * h + 2, :] for j in range(n)], axis=0)
        gathered = jnp.concatenate([gathered, jnp.zeros((width - 2 * n, 128), f32)], axis=0).T
        for j in range(n):
            near = gathered if j == 0 else pltpu.roll(gathered, width - 2 * j, 1)
            fix_col[j, h * 128 : (h + 1) * 128, :] = near
    head = lax.broadcasted_iota(jnp.int32, (n * per_group, width), 1) < 2

    for q in range(n_chunks):
        for r in order:
            prod_copy(q, r).wait_recv()
        per_chunk = rows // per_group

        @pl.loop(0, per_chunk, unroll=True)
        def _(k):
            place = pl.ds(pl.multiple_of(q * rows + k * per_group, per_group), per_group)
            block = recv[:, place, :].reshape(n * per_group, width).astype(f32)
            fixed = fix_col[:, place, :].reshape(n * per_group, width)
            block = jnp.where(head, fixed, block).astype(bf16)
            half = n // 2
            taps_of = toep[q * per_chunk + k]
            near = jnp.dot(block, taps_of[:, : half * width], preferred_element_type=f32)
            far = jnp.dot(
                block[: half * per_group], taps_of[:, half * width :], preferred_element_type=f32
            )

            def term(j, d):
                full, at = (near, d) if d < half else (far, d - half)
                return full[
                    j * per_group : (j + 1) * per_group, at * width : (at + 1) * width
                ]

            for i in range(n):
                total = term(0, i)
                for j in range(1, i + 1):
                    total = total + term(j, i - j)
                res[i, place, :] = total.astype(bf16)

        for r in order:
            res_copy(q, r).start()
        part = slice(q * rows, (q + 1) * rows)
        back[me, part, :] = res[me, part, :]

    local_col[...] = fix_row[...].T.reshape(local_col.shape)
    head = lax.broadcasted_iota(jnp.int32, (n * rows, width), 1) < 2
    for q in range(n_chunks):
        part = slice(q * rows, (q + 1) * rows)
        skip = coef_col[:, part, :].reshape(n * rows, coef_col.shape[2])[:, 3 * taps : 3 * taps + 1]
        fixed = local_col[:, part, :].reshape(n * rows, width)
        value = prod[:, part, :].reshape(n * rows, width).astype(f32)
        direct[:, part, :] = (skip * jnp.where(head, fixed, value)).reshape(n, rows, width)
        fixed = pltpu.roll(fixed, width - 2, 1)
        value = query[:, part, :].reshape(n * rows, width).astype(f32)
        query[:, part, :] = jnp.where(head, fixed, value).astype(bf16).reshape(n, rows, width)

    squares = jnp.zeros((8, width), f32)
    for q in range(n_chunks):
        part = slice(q * rows, (q + 1) * rows)
        for r in order:
            res_copy(q, r).wait_recv()
        far = back[:, part, :].astype(f32)
        gated = (query[:, part, :].astype(f32) * (far + direct[:, part, :])).astype(bf16)
        gated = gated.astype(f32)
        gain = coef_col[:, part, :][:, :, 3 * taps + 1 : 3 * taps + 2]
        direct[:, part, :] = gated * gain
        squares = squares + jnp.sum((gated * gated).reshape(n * rows // 8, 8, width), axis=0)
    sq_out[...] = squares

    def sq_copy(r):
        return pltpu.make_async_remote_copy(
            src_ref=sq_out,
            dst_ref=sq_in.at[tp],
            send_sem=sq_send.at[r],
            recv_sem=sq_recv.at[r],
            device_id=(me, lax.rem(tp + r, nt)),
            device_id_type=MESH,
        )

    for r in range(1, nt):
        sq_copy(r).start()
    sq_in[tp] = squares
    for r in order:
        filt_copy(r).wait_send()
        fix_copy(r).wait_send()
        for q in range(n_chunks):
            if q >= n_chunks - depth:
                prod_copy(q, r).wait_send()
            res_copy(q, r).wait_send()

    @pl.when(me < n - 1)
    def _():
        edge_copy.wait_send()

    for r in range(1, nt):
        sq_copy(r).wait_recv()
    total = jnp.sum(jnp.sum(sq_in[...], axis=0), axis=0, keepdims=True)
    inverse = 1.0 / jnp.sqrt(total / (chan * nt) + 1e-05)
    stores = []
    for part in range(4):
        some = pl.ds(part * n // 4, n // 4)
        out_vmem[some] = (direct[some] * inverse).astype(bf16)
        stores.append(
            pltpu.make_async_copy(out_vmem.at[some], out_ref.at[some], store_sem.at[part])
        )
        stores[-1].start()
    for store in stores:
        store.wait()
    for r in range(1, nt):
        sq_copy(r).wait_send()


def fused_shards(streams, short_weight, filters, skip_gain, norm_gain):
    n = lax.axis_size("ctx")
    nt = lax.axis_size("tp")
    chan, width = streams.shape[1:]
    own = chan // n
    owned_groups = filters.shape[0] // n
    n_chunks = 8
    bf16, f32 = jnp.bfloat16, jnp.float32
    dma = pltpu.SemaphoreType.DMA
    slab = pltpu.VMEM((n, own, width), bf16)
    wide_slab = pltpu.VMEM((n, own, width), f32)
    result = pl.pallas_call(
        functools.partial(kernel, n, nt, n_chunks),
        out_shape=jax.ShapeDtypeStruct((n, own, width), bf16),
        in_specs=[pl.BlockSpec(memory_space=pltpu.HBM)] * 5,
        out_specs=pl.BlockSpec(memory_space=pltpu.HBM),
        scratch_shapes=[
            pltpu.VMEM((3, n, own, width), bf16),
            pltpu.VMEM(short_weight.shape, f32),
            pltpu.VMEM(filters.shape, f32),
            pltpu.VMEM((1, chan), f32),
            pltpu.VMEM((1, chan), f32),
            pltpu.VMEM((16, chan), f32),
            pltpu.VMEM((16, chan // 2), bf16),
            pltpu.VMEM((16, chan // 2), bf16),
            pltpu.VMEM((n, own // 64, 128), f32),
            pltpu.VMEM((n, own // 64, 128), f32),
            pltpu.VMEM((128, chan), f32),
            wide_slab,
            wide_slab,
            wide_slab,
            slab,
            pltpu.VMEM((16, chan), f32),
            pltpu.VMEM((n, own, 16), f32),
            pltpu.VMEM((filters.shape[0], width), bf16),
            pltpu.VMEM((n, owned_groups, width), bf16),
            pltpu.VMEM((n, owned_groups, width), f32),
            pltpu.VMEM((owned_groups, width, n * width), bf16),
            slab,
            slab,
            slab,
            slab,
            slab,
            pltpu.VMEM((8, width), f32),
            pltpu.VMEM((nt, 8, width), f32),
            dma((4 + n_chunks,)),
            dma((4,)),
            dma,
            dma,
            dma((n,)),
            dma((n,)),
            dma((n,)),
            dma((n,)),
            dma((n_chunks, n)),
            dma((n_chunks, n)),
            dma((n_chunks, n)),
            dma((n_chunks, n)),
            dma((nt,)),
            dma((nt,)),
        ],
        compiler_params=pltpu.CompilerParams(
            collective_id=0, has_side_effects=True, vmem_limit_bytes=63 * 1024 * 1024
        ),
        name="hyena",
    )(
        streams.reshape(3, n, own, width),
        short_weight,
        filters,
        skip_gain.reshape(1, chan),
        norm_gain.reshape(1, chan),
    )
    return result.reshape(chan, width)


def solution(mesh):
    in_specs = (P(None, "tp", "ctx"), P(None, None, "tp"), P("tp", "ctx"), P("tp"), P("tp"))
    out_specs = P("tp", "ctx")
    body = fused_shards if mesh.shape["ctx"] <= 16 else shards
    return jax.shard_map(body, mesh=mesh, in_specs=in_specs, out_specs=out_specs, check_vma=False)
```

```python
import functools
import math

import jax
import jax.numpy as jnp
from jax import lax
from jax.experimental import pallas as pl
from jax.experimental.pallas import tpu as pltpu
from jax.sharding import PartitionSpec as P

highest = lax.Precision.HIGHEST
MESH = pl.DeviceIdType.MESH


def causal_short(padded, weights, length):
    taps = weights.shape[0]
    total = jnp.zeros(padded.shape[:2] + (length,), jnp.float32)
    for offset in range(taps):
        start = taps - 1 - offset
        total = total + weights[offset][:, :, None] * padded[:, :, start : start + length]
    return total


def trig_tables(half_count, row_count):
    periods = 2 * half_count
    total_len = periods * row_count
    freq = lax.iota(jnp.int32, periods)[:, None]
    place = lax.iota(jnp.int32, half_count)[None, :]
    angle_one = (freq * place % periods).astype(jnp.float32) * (2.0 * math.pi / periods)
    cols = lax.iota(jnp.int32, row_count)
    angle_two = (cols[:, None] * cols[None, :] % row_count).astype(jnp.float32) * (
        2.0 * math.pi / row_count
    )
    angle_twist = (freq * cols[None, :] % total_len).astype(jnp.float32) * (
        2.0 * math.pi / total_len
    )
    return (
        jnp.cos(angle_one),
        jnp.sin(angle_one),
        jnp.cos(angle_two),
        jnp.sin(angle_two),
        jnp.cos(angle_twist),
        jnp.sin(angle_twist),
    )


def forward_dft(signal, tables):
    cos_one, sin_one, cos_two, sin_two, cos_tw, sin_tw = tables
    first_re = jnp.einsum("ka,cab->ckb", cos_one, signal, precision=highest)
    first_im = -jnp.einsum("ka,cab->ckb", sin_one, signal, precision=highest)
    turned_re = first_re * cos_tw + first_im * sin_tw
    turned_im = first_im * cos_tw - first_re * sin_tw
    out_re = jnp.einsum("ckb,bq->ckq", turned_re, cos_two, precision=highest) + jnp.einsum(
        "ckb,bq->ckq", turned_im, sin_two, precision=highest
    )
    out_im = jnp.einsum("ckb,bq->ckq", turned_im, cos_two, precision=highest) - jnp.einsum(
        "ckb,bq->ckq", turned_re, sin_two, precision=highest
    )
    return (out_re, out_im)


def inverse_dft(spec_re, spec_im, tables):
    cos_one, sin_one, cos_two, sin_two, cos_tw, sin_tw = tables
    back_re = jnp.einsum("ckq,qb->ckb", spec_re, cos_two, precision=highest) - jnp.einsum(
        "ckq,qb->ckb", spec_im, sin_two, precision=highest
    )
    back_im = jnp.einsum("ckq,qb->ckb", spec_re, sin_two, precision=highest) + jnp.einsum(
        "ckq,qb->ckb", spec_im, cos_two, precision=highest
    )
    turned_re = back_re * cos_tw - back_im * sin_tw
    turned_im = back_re * sin_tw + back_im * cos_tw
    result = jnp.einsum("ka,ckb->cab", cos_one, turned_re, precision=highest) - jnp.einsum(
        "ka,ckb->cab", sin_one, turned_im, precision=highest
    )
    total_len = 2 * cos_one.shape[1] * cos_two.shape[0]
    return result / total_len


def shards(streams, short_weight, filters, skip_gain, norm_gain):
    n_ctx = lax.axis_size("ctx")
    n_width = lax.axis_size("tp")
    tok_rows = streams.shape[2]
    local_chan = streams.shape[1]
    owned = local_chan // n_ctx
    owned_groups = filters.shape[0] // n_ctx
    per_group = owned // owned_groups
    seq_len = tok_rows * n_ctx
    taps = short_weight.shape[0]
    owner_start = lax.axis_index("ctx") * owned
    skip_own = lax.dynamic_slice_in_dim(skip_gain, owner_start, owned, 0)
    filter_own = lax.all_to_all(filters, "ctx", split_axis=0, concat_axis=1, tiled=True)
    raw_own = lax.all_to_all(streams, "ctx", split_axis=1, concat_axis=2, tiled=True)
    weight_own = lax.dynamic_slice_in_dim(short_weight, owner_start, owned, 2)
    padded = jnp.pad(raw_own.astype(jnp.float32), ((0, 0), (0, 0), (taps - 1, 0)))
    conv_own = causal_short(padded, weight_own, seq_len)
    query_own = lax.optimization_barrier(conv_own[0].astype(jnp.bfloat16)).astype(jnp.float32)
    value_own = lax.optimization_barrier((conv_own[1] * conv_own[2]).astype(jnp.bfloat16)).astype(
        jnp.float32
    )
    tables = trig_tables(n_ctx, tok_rows)
    value_re, value_im = forward_dft(value_own.reshape(owned, n_ctx, tok_rows), tables)
    filt_re, filt_im = forward_dft(filter_own.reshape(owned_groups, n_ctx, tok_rows), tables)
    spec_shape = (owned_groups, per_group) + value_re.shape[1:]
    value_re = value_re.reshape(spec_shape)
    value_im = value_im.reshape(spec_shape)
    filt_re = filt_re[:, None]
    filt_im = filt_im[:, None]
    spec_re = (value_re * filt_re - value_im * filt_im).reshape((owned,) + spec_shape[2:])
    spec_im = (value_re * filt_im + value_im * filt_re).reshape((owned,) + spec_shape[2:])
    long_conv = inverse_dft(spec_re, spec_im, tables).reshape(owned, seq_len)
    gated = (query_own * (long_conv + skip_own[:, None] * value_own)).astype(jnp.bfloat16)
    gated_rows = lax.all_to_all(gated, "ctx", split_axis=1, concat_axis=0, tiled=True)
    gated_wide = gated_rows.astype(jnp.float32)
    squares = lax.psum(jnp.sum(gated_wide * gated_wide, axis=0), "tp")
    rms = jnp.sqrt(squares / (local_chan * n_width) + 1e-05)
    return (gated_wide * norm_gain[:, None] / rms[None, :]).astype(jnp.bfloat16)


def rolled_order(n):
    return sorted(range(1, n), key=lambda r: (abs(2 * r - n), r))


def kernel(
    n,
    nt,
    n_chunks,
    st_hbm,
    sw_hbm,
    filt_hbm,
    skip_hbm,
    gain_hbm,
    out_ref,
    st,
    sw_ref,
    filt_ref,
    skip_ref,
    gain_ref,
    edge_row,
    edge_out,
    edge_in,
    fix_out,
    fix_in,
    fix_row,
    fix_col,
    local_col,
    direct,
    out_vmem,
    coef_row,
    coef_col,
    filt_out,
    filt_in,
    filt_f32,
    toep,
    prod,
    query,
    recv,
    res,
    back,
    sq_out,
    sq_in,
    load_sem,
    store_sem,
    edge_send,
    edge_recv,
    fix_send,
    fix_recv,
    filt_send,
    filt_recv,
    prod_send,
    prod_recv,
    res_send,
    res_recv,
    sq_send,
    sq_recv,
):
    bf16, f32 = jnp.bfloat16, jnp.float32
    me = lax.axis_index("ctx")
    tp = lax.axis_index("tp")
    taps = sw_ref.shape[0]
    own, width = st.shape[2], st.shape[3]
    chan = n * own
    owned_groups = filt_in.shape[1]
    per_group = own // owned_groups
    rows = own // n_chunks
    order = rolled_order(n)
    depth = 1

    small = [
        pltpu.make_async_copy(sw_hbm, sw_ref, load_sem.at[0]),
        pltpu.make_async_copy(skip_hbm, skip_ref, load_sem.at[1]),
        pltpu.make_async_copy(filt_hbm, filt_ref, load_sem.at[2]),
        pltpu.make_async_copy(gain_hbm, gain_ref, load_sem.at[3]),
    ]
    loads = []
    for q in range(n_chunks):
        part = pl.ds(q * rows, rows)
        loads.append(
            pltpu.make_async_copy(
                st_hbm.at[:, :, part], st.at[:, :, part], load_sem.at[4 + q]
            )
        )
    for load in small + loads:
        load.start()

    barrier = pltpu.get_barrier_semaphore()
    for r in range(1, n):
        pl.semaphore_signal(
            barrier, inc=1, device_id=(lax.rem(me + r, n), tp), device_id_type=MESH
        )
    for r in range(1, nt):
        pl.semaphore_signal(
            barrier, inc=1, device_id=(me, lax.rem(tp + r, nt)), device_id_type=MESH
        )
    for load in small:
        load.wait()
    coef_row[...] = jnp.zeros_like(coef_row)
    for j in range(taps):
        for s in range(3):
            coef_row[3 * j + s : 3 * j + s + 1, :] = sw_ref[j, s : s + 1, :]
    coef_row[3 * taps : 3 * taps + 1, :] = skip_ref[...]
    coef_row[3 * taps + 1 : 3 * taps + 2, :] = gain_ref[...]
    coef_col[...] = coef_row[...].T.reshape(coef_col.shape)
    filt_out[...] = filt_ref[...].astype(bf16)

    def filt_copy(r):
        to = lax.rem(me + r, n)
        return pltpu.make_async_remote_copy(
            src_ref=filt_out.at[pl.ds(pl.multiple_of(to * owned_groups, owned_groups), owned_groups)],
            dst_ref=filt_in.at[me],
            send_sem=filt_send.at[r],
            recv_sem=filt_recv.at[r],
            device_id=(to, tp),
            device_id_type=MESH,
        )

    def prod_copy(q, r):
        to = lax.rem(me + r, n)
        part = pl.ds(q * rows, rows)
        return pltpu.make_async_remote_copy(
            src_ref=prod.at[to, part],
            dst_ref=recv.at[me, part],
            send_sem=prod_send.at[q, r],
            recv_sem=prod_recv.at[q, r],
            device_id=(to, tp),
            device_id_type=MESH,
        )

    def res_copy(q, r):
        to = lax.rem(me + r, n)
        part = pl.ds(q * rows, rows)
        return pltpu.make_async_remote_copy(
            src_ref=res.at[to, part],
            dst_ref=back.at[me, part],
            send_sem=res_send.at[q, r],
            recv_sem=res_recv.at[q, r],
            device_id=(to, tp),
            device_id_type=MESH,
        )

    def fix_copy(r):
        to = lax.rem(me + r, n)
        return pltpu.make_async_remote_copy(
            src_ref=fix_out.at[to],
            dst_ref=fix_in.at[me],
            send_sem=fix_send.at[r],
            recv_sem=fix_recv.at[r],
            device_id=(to, tp),
            device_id_type=MESH,
        )

    edge_copy = pltpu.make_async_remote_copy(
        src_ref=edge_out,
        dst_ref=edge_in,
        send_sem=edge_send,
        recv_sem=edge_recv,
        device_id=(lax.rem(me + 1, n), tp),
        device_id_type=MESH,
    )

    def pick_edges():
        edge = jnp.zeros((16, chan), f32)
        row_id = lax.broadcasted_iota(jnp.int32, (16, width), 0)
        lane_id = lax.broadcasted_iota(jnp.int32, (16, width), 1)
        slot = jnp.where(lane_id < 2, lane_id + 8, lane_id - width + 2)
        at_edge = (lane_id < 2) | (lane_id >= width - 2)
        for s in range(3):
            pick = at_edge & (row_id == 2 * s + slot)
            edge = edge + lax.dot_general(
                pick.astype(f32).astype(bf16),
                st[s].reshape(chan, width),
                (((1,), (1,)), ((), ())),
                preferred_element_type=f32,
            )
        edge_row[...] = edge
        edge_out[...] = jnp.concatenate(
            [edge[:8, : chan // 2], edge[:8, chan // 2 :]], axis=0
        ).astype(bf16)

        @pl.when(me < n - 1)
        def _():
            edge_copy.start()

    def fix_edges():
        fix_row[...] = jnp.zeros_like(fix_row)

        @pl.when(me == 0)
        def _():
            edge_in[...] = jnp.zeros_like(edge_in)

        @pl.when(me > 0)
        def _():
            edge_copy.wait_recv()

        here = edge_row[8:, :]
        left = edge_in[...].astype(f32)
        left = jnp.concatenate([left[:8], left[8:]], axis=1)
        coef = coef_row[...]
        first, second = [], []
        for s in range(3):
            now, later = here[2 * s : 2 * s + 1], here[2 * s + 1 : 2 * s + 2]
            two, one = left[2 * s : 2 * s + 1], left[2 * s + 1 : 2 * s + 2]
            w0, w1, w2 = (coef[3 * j + s : 3 * j + s + 1] for j in range(3))
            first.append(w0 * now + w1 * one + w2 * two)
            second.append(w0 * later + w1 * now + w2 * one)
        lines = [
            first[1] * first[2],
            second[1] * second[2],
            first[0],
            second[0],
        ]
        lines = [line.astype(bf16).astype(f32) for line in lines]
        for o in range(n):
            for h in range(own // 128):
                at = o * own + h * 128
                for p in range(2):
                    fix_out[o, 2 * h + p : 2 * h + p + 1, :] = lines[p][:, at : at + 128]
        for i in range(4):
            fix_row[i : i + 1, :] = lines[i]

    def build_blocks(start, stop):
        @pl.loop(start, stop)
        def _(g):
            line = jnp.concatenate(
                [jnp.zeros((1, width), f32)] + [filt_f32[j, pl.ds(g, 1), :] for j in range(n)],
                axis=1,
            )
            line = jnp.broadcast_to(line, (16, (n + 1) * width))
            base = pltpu.roll(line, 0, 1, stride=1, stride_axis=0).astype(bf16)
            for a in range(width // 16):
                moved = base if a == 0 else pltpu.roll(base, 16 * a, 1)
                toep[g, 16 * a : 16 * (a + 1), :] = moved[:, width:]

    k_id = lax.broadcasted_iota(jnp.int32, (width, 2 * width), 0)
    m_id = lax.broadcasted_iota(jnp.int32, (width, 2 * width), 1)
    source = jnp.where(m_id < width, m_id - 1, m_id - width - 2)
    mover = (k_id == source).astype(f32).astype(bf16)
    for q in range(n_chunks):
        if q == 0:
            loads[0].wait()
        part = slice(q * rows, (q + 1) * rows)
        coef = coef_col[:, part, :].reshape(n * rows, coef_col.shape[2])
        conv = []
        for s in range(3):
            now = st[s, :, part, :].reshape(n * rows, width)
            moved = jnp.dot(now, mover, preferred_element_type=f32)
            conv.append(
                coef[:, s : s + 1] * now.astype(f32)
                + coef[:, 3 + s : 4 + s] * moved[:, :width]
                + coef[:, 6 + s : 7 + s] * moved[:, width:]
            )
        query[:, part, :] = conv[0].astype(bf16).reshape(n, rows, width)
        prod[:, part, :] = (conv[1] * conv[2]).astype(bf16).reshape(n, rows, width)
        if q == 0:
            pl.semaphore_wait(barrier, n - 1 + nt - 1)
            for r in order:
                filt_copy(r).start()
        if q >= depth:
            for r in order:
                prod_copy(q - depth, r).wait_send()
        for r in order:
            prod_copy(q, r).start()
        if q == 0:
            filt_in[me] = filt_out[
                pl.ds(pl.multiple_of(me * owned_groups, owned_groups), owned_groups), :
            ]
            for load in loads[1:]:
                load.wait()
            pick_edges()
        recv[me, part, :] = prod[me, part, :]
        if q == n_chunks // 2 - 1:
            fix_edges()
            for r in order:
                fix_copy(r).start()
            fix_in[me] = fix_out[me]
        if q >= depth:
            if q == depth:
                for r in order:
                    filt_copy(r).wait_recv()
                filt_f32[...] = filt_in[...].astype(f32)
            span = n_chunks - depth
            build_blocks(
                (q - depth) * owned_groups // span, (q + 1 - depth) * owned_groups // span
            )

    for r in order:
        fix_copy(r).wait_recv()
    for h in range(own // 128):
        gathered = jnp.concatenate([fix_in[j, 2 * h : 2 * h + 2, :] for j in range(n)], axis=0)
        gathered = jnp.concatenate([gathered, jnp.zeros((width - 2 * n, 128), f32)], axis=0).T
        for j in range(n):
            near = gathered if j == 0 else pltpu.roll(gathered, width - 2 * j, 1)
            fix_col[j, h * 128 : (h + 1) * 128, :] = near
    head = lax.broadcasted_iota(jnp.int32, (n * per_group, width), 1) < 2

    for q in range(n_chunks):
        for r in order:
            prod_copy(q, r).wait_recv()
        per_chunk = rows // per_group

        @pl.loop(0, per_chunk, unroll=True)
        def _(k):
            place = pl.ds(pl.multiple_of(q * rows + k * per_group, per_group), per_group)
            block = recv[:, place, :].reshape(n * per_group, width).astype(f32)
            fixed = fix_col[:, place, :].reshape(n * per_group, width)
            block = jnp.where(head, fixed, block).astype(bf16)
            half = n // 2
            taps_of = toep[q * per_chunk + k]
            near = jnp.dot(block, taps_of[:, : half * width], preferred_element_type=f32)
            far = jnp.dot(
                block[: half * per_group], taps_of[:, half * width :], preferred_element_type=f32
            )

            def term(j, d):
                full, at = (near, d) if d < half else (far, d - half)
                return full[
                    j * per_group : (j + 1) * per_group, at * width : (at + 1) * width
                ]

            for i in range(n):
                total = term(0, i)
                for j in range(1, i + 1):
                    total = total + term(j, i - j)
                res[i, place, :] = total.astype(bf16)

        for r in order:
            res_copy(q, r).start()
        part = slice(q * rows, (q + 1) * rows)
        back[me, part, :] = res[me, part, :]

    local_col[...] = fix_row[...].T.reshape(local_col.shape)
    head = lax.broadcasted_iota(jnp.int32, (n * rows, width), 1) < 2
    for q in range(n_chunks):
        part = slice(q * rows, (q + 1) * rows)
        skip = coef_col[:, part, :].reshape(n * rows, coef_col.shape[2])[:, 3 * taps : 3 * taps + 1]
        fixed = local_col[:, part, :].reshape(n * rows, width)
        value = prod[:, part, :].reshape(n * rows, width).astype(f32)
        direct[:, part, :] = (skip * jnp.where(head, fixed, value)).reshape(n, rows, width)
        fixed = pltpu.roll(fixed, width - 2, 1)
        value = query[:, part, :].reshape(n * rows, width).astype(f32)
        query[:, part, :] = jnp.where(head, fixed, value).astype(bf16).reshape(n, rows, width)

    squares = jnp.zeros((8, width), f32)
    for q in range(n_chunks):
        part = slice(q * rows, (q + 1) * rows)
        for r in order:
            res_copy(q, r).wait_recv()
        far = back[:, part, :].astype(f32)
        gated = (query[:, part, :].astype(f32) * (far + direct[:, part, :])).astype(bf16)
        gated = gated.astype(f32)
        gain = coef_col[:, part, :][:, :, 3 * taps + 1 : 3 * taps + 2]
        direct[:, part, :] = gated * gain
        squares = squares + jnp.sum((gated * gated).reshape(n * rows // 8, 8, width), axis=0)
    sq_out[...] = squares

    def sq_copy(r):
        return pltpu.make_async_remote_copy(
            src_ref=sq_out,
            dst_ref=sq_in.at[tp],
            send_sem=sq_send.at[r],
            recv_sem=sq_recv.at[r],
            device_id=(me, lax.rem(tp + r, nt)),
            device_id_type=MESH,
        )

    for r in range(1, nt):
        sq_copy(r).start()
    sq_in[tp] = squares
    for r in order:
        filt_copy(r).wait_send()
        fix_copy(r).wait_send()
        for q in range(n_chunks):
            if q >= n_chunks - depth:
                prod_copy(q, r).wait_send()
            res_copy(q, r).wait_send()

    @pl.when(me < n - 1)
    def _():
        edge_copy.wait_send()

    for r in range(1, nt):
        sq_copy(r).wait_recv()
    total = jnp.sum(jnp.sum(sq_in[...], axis=0), axis=0, keepdims=True)
    inverse = 1.0 / jnp.sqrt(total / (chan * nt) + 1e-05)
    stores = []
    for part in range(4):
        some = pl.ds(part * n // 4, n // 4)
        out_vmem[some] = (direct[some] * inverse).astype(bf16)
        stores.append(
            pltpu.make_async_copy(out_vmem.at[some], out_ref.at[some], store_sem.at[part])
        )
        stores[-1].start()
    for store in stores:
        store.wait()
    for r in range(1, nt):
        sq_copy(r).wait_send()


def fused_shards(streams, short_weight, filters, skip_gain, norm_gain):
    n = lax.axis_size("ctx")
    nt = lax.axis_size("tp")
    chan, width = streams.shape[1:]
    own = chan // n
    owned_groups = filters.shape[0] // n
    n_chunks = 2
    bf16, f32 = jnp.bfloat16, jnp.float32
    dma = pltpu.SemaphoreType.DMA
    slab = pltpu.VMEM((n, own, width), bf16)
    wide_slab = pltpu.VMEM((n, own, width), f32)
    result = pl.pallas_call(
        functools.partial(kernel, n, nt, n_chunks),
        out_shape=jax.ShapeDtypeStruct((n, own, width), bf16),
        in_specs=[pl.BlockSpec(memory_space=pltpu.HBM)] * 5,
        out_specs=pl.BlockSpec(memory_space=pltpu.HBM),
        scratch_shapes=[
            pltpu.VMEM((3, n, own, width), bf16),
            pltpu.VMEM(short_weight.shape, f32),
            pltpu.VMEM(filters.shape, f32),
            pltpu.VMEM((1, chan), f32),
            pltpu.VMEM((1, chan), f32),
            pltpu.VMEM((16, chan), f32),
            pltpu.VMEM((16, chan // 2), bf16),
            pltpu.VMEM((16, chan // 2), bf16),
            pltpu.VMEM((n, own // 64, 128), f32),
            pltpu.VMEM((n, own // 64, 128), f32),
            pltpu.VMEM((128, chan), f32),
            wide_slab,
            wide_slab,
            wide_slab,
            slab,
            pltpu.VMEM((16, chan), f32),
            pltpu.VMEM((n, own, 16), f32),
            pltpu.VMEM((filters.shape[0], width), bf16),
            pltpu.VMEM((n, owned_groups, width), bf16),
            pltpu.VMEM((n, owned_groups, width), f32),
            pltpu.VMEM((owned_groups, width, n * width), bf16),
            slab,
            slab,
            slab,
            slab,
            slab,
            pltpu.VMEM((8, width), f32),
            pltpu.VMEM((nt, 8, width), f32),
            dma((4 + n_chunks,)),
            dma((4,)),
            dma,
            dma,
            dma((n,)),
            dma((n,)),
            dma((n,)),
            dma((n,)),
            dma((n_chunks, n)),
            dma((n_chunks, n)),
            dma((n_chunks, n)),
            dma((n_chunks, n)),
            dma((nt,)),
            dma((nt,)),
        ],
        compiler_params=pltpu.CompilerParams(
            collective_id=0, has_side_effects=True, vmem_limit_bytes=63 * 1024 * 1024
        ),
        name="hyena",
    )(
        streams.reshape(3, n, own, width),
        short_weight,
        filters,
        skip_gain.reshape(1, chan),
        norm_gain.reshape(1, chan),
    )
    return result.reshape(chan, width)


def solution(mesh):
    in_specs = (P(None, "tp", "ctx"), P(None, None, "tp"), P("tp", "ctx"), P("tp"), P("tp"))
    out_specs = P("tp", "ctx")
    body = fused_shards if mesh.shape["ctx"] <= 16 else shards
    return jax.shard_map(body, mesh=mesh, in_specs=in_specs, out_specs=out_specs, check_vma=False)
```

```python
import functools
import math

import jax
import jax.numpy as jnp
from jax import lax
from jax.experimental import pallas as pl
from jax.experimental.pallas import tpu as pltpu
from jax.sharding import PartitionSpec as P

highest = lax.Precision.HIGHEST
MESH = pl.DeviceIdType.MESH


def causal_short(padded, weights, length):
    taps = weights.shape[0]
    total = jnp.zeros(padded.shape[:2] + (length,), jnp.float32)
    for offset in range(taps):
        start = taps - 1 - offset
        total = total + weights[offset][:, :, None] * padded[:, :, start : start + length]
    return total


def trig_tables(half_count, row_count):
    periods = 2 * half_count
    total_len = periods * row_count
    freq = lax.iota(jnp.int32, periods)[:, None]
    place = lax.iota(jnp.int32, half_count)[None, :]
    angle_one = (freq * place % periods).astype(jnp.float32) * (2.0 * math.pi / periods)
    cols = lax.iota(jnp.int32, row_count)
    angle_two = (cols[:, None] * cols[None, :] % row_count).astype(jnp.float32) * (
        2.0 * math.pi / row_count
    )
    angle_twist = (freq * cols[None, :] % total_len).astype(jnp.float32) * (
        2.0 * math.pi / total_len
    )
    return (
        jnp.cos(angle_one),
        jnp.sin(angle_one),
        jnp.cos(angle_two),
        jnp.sin(angle_two),
        jnp.cos(angle_twist),
        jnp.sin(angle_twist),
    )


def forward_dft(signal, tables):
    cos_one, sin_one, cos_two, sin_two, cos_tw, sin_tw = tables
    first_re = jnp.einsum("ka,cab->ckb", cos_one, signal, precision=highest)
    first_im = -jnp.einsum("ka,cab->ckb", sin_one, signal, precision=highest)
    turned_re = first_re * cos_tw + first_im * sin_tw
    turned_im = first_im * cos_tw - first_re * sin_tw
    out_re = jnp.einsum("ckb,bq->ckq", turned_re, cos_two, precision=highest) + jnp.einsum(
        "ckb,bq->ckq", turned_im, sin_two, precision=highest
    )
    out_im = jnp.einsum("ckb,bq->ckq", turned_im, cos_two, precision=highest) - jnp.einsum(
        "ckb,bq->ckq", turned_re, sin_two, precision=highest
    )
    return (out_re, out_im)


def inverse_dft(spec_re, spec_im, tables):
    cos_one, sin_one, cos_two, sin_two, cos_tw, sin_tw = tables
    back_re = jnp.einsum("ckq,qb->ckb", spec_re, cos_two, precision=highest) - jnp.einsum(
        "ckq,qb->ckb", spec_im, sin_two, precision=highest
    )
    back_im = jnp.einsum("ckq,qb->ckb", spec_re, sin_two, precision=highest) + jnp.einsum(
        "ckq,qb->ckb", spec_im, cos_two, precision=highest
    )
    turned_re = back_re * cos_tw - back_im * sin_tw
    turned_im = back_re * sin_tw + back_im * cos_tw
    result = jnp.einsum("ka,ckb->cab", cos_one, turned_re, precision=highest) - jnp.einsum(
        "ka,ckb->cab", sin_one, turned_im, precision=highest
    )
    total_len = 2 * cos_one.shape[1] * cos_two.shape[0]
    return result / total_len


def shards(streams, short_weight, filters, skip_gain, norm_gain):
    n_ctx = lax.axis_size("ctx")
    n_width = lax.axis_size("tp")
    tok_rows = streams.shape[2]
    local_chan = streams.shape[1]
    owned = local_chan // n_ctx
    owned_groups = filters.shape[0] // n_ctx
    per_group = owned // owned_groups
    seq_len = tok_rows * n_ctx
    taps = short_weight.shape[0]
    owner_start = lax.axis_index("ctx") * owned
    skip_own = lax.dynamic_slice_in_dim(skip_gain, owner_start, owned, 0)
    filter_own = lax.all_to_all(filters, "ctx", split_axis=0, concat_axis=1, tiled=True)
    raw_own = lax.all_to_all(streams, "ctx", split_axis=1, concat_axis=2, tiled=True)
    weight_own = lax.dynamic_slice_in_dim(short_weight, owner_start, owned, 2)
    padded = jnp.pad(raw_own.astype(jnp.float32), ((0, 0), (0, 0), (taps - 1, 0)))
    conv_own = causal_short(padded, weight_own, seq_len)
    query_own = lax.optimization_barrier(conv_own[0].astype(jnp.bfloat16)).astype(jnp.float32)
    value_own = lax.optimization_barrier((conv_own[1] * conv_own[2]).astype(jnp.bfloat16)).astype(
        jnp.float32
    )
    tables = trig_tables(n_ctx, tok_rows)
    value_re, value_im = forward_dft(value_own.reshape(owned, n_ctx, tok_rows), tables)
    filt_re, filt_im = forward_dft(filter_own.reshape(owned_groups, n_ctx, tok_rows), tables)
    spec_shape = (owned_groups, per_group) + value_re.shape[1:]
    value_re = value_re.reshape(spec_shape)
    value_im = value_im.reshape(spec_shape)
    filt_re = filt_re[:, None]
    filt_im = filt_im[:, None]
    spec_re = (value_re * filt_re - value_im * filt_im).reshape((owned,) + spec_shape[2:])
    spec_im = (value_re * filt_im + value_im * filt_re).reshape((owned,) + spec_shape[2:])
    long_conv = inverse_dft(spec_re, spec_im, tables).reshape(owned, seq_len)
    gated = (query_own * (long_conv + skip_own[:, None] * value_own)).astype(jnp.bfloat16)
    gated_rows = lax.all_to_all(gated, "ctx", split_axis=1, concat_axis=0, tiled=True)
    gated_wide = gated_rows.astype(jnp.float32)
    squares = lax.psum(jnp.sum(gated_wide * gated_wide, axis=0), "tp")
    rms = jnp.sqrt(squares / (local_chan * n_width) + 1e-05)
    return (gated_wide * norm_gain[:, None] / rms[None, :]).astype(jnp.bfloat16)


def rolled_order(n):
    far_first = sorted(range(1, n), key=lambda r: (abs(2 * r - n), r))
    half = n // 2
    mixed = []
    for i in range(half):
        mixed += far_first[i : i + 1] + far_first[half + i : half + i + 1]
    return mixed


def kernel(
    n,
    nt,
    n_chunks,
    st_hbm,
    sw_hbm,
    filt_hbm,
    skip_hbm,
    gain_hbm,
    out_ref,
    st,
    sw_ref,
    filt_ref,
    skip_ref,
    gain_ref,
    edge_row,
    edge_out,
    edge_in,
    fix_out,
    fix_in,
    fix_row,
    fix_col,
    local_col,
    direct,
    out_vmem,
    coef_row,
    coef_col,
    filt_out,
    filt_in,
    filt_f32,
    toep,
    prod,
    query,
    recv,
    res,
    back,
    sq_out,
    sq_in,
    load_sem,
    store_sem,
    edge_send,
    edge_recv,
    fix_send,
    fix_recv,
    filt_send,
    filt_recv,
    prod_send,
    prod_recv,
    res_send,
    res_recv,
    sq_send,
    sq_recv,
):
    bf16, f32 = jnp.bfloat16, jnp.float32
    me = lax.axis_index("ctx")
    tp = lax.axis_index("tp")
    taps = sw_ref.shape[0]
    own, width = st.shape[2], st.shape[3]
    chan = n * own
    owned_groups = filt_in.shape[1]
    per_group = own // owned_groups
    rows = own // n_chunks
    order = rolled_order(n)
    depth = 2

    small = [
        pltpu.make_async_copy(sw_hbm, sw_ref, load_sem.at[0]),
        pltpu.make_async_copy(skip_hbm, skip_ref, load_sem.at[1]),
        pltpu.make_async_copy(filt_hbm, filt_ref, load_sem.at[2]),
        pltpu.make_async_copy(gain_hbm, gain_ref, load_sem.at[3]),
    ]
    loads = []
    for q in range(n_chunks):
        part = pl.ds(q * rows, rows)
        loads.append(
            pltpu.make_async_copy(
                st_hbm.at[:, :, part], st.at[:, :, part], load_sem.at[4 + q]
            )
        )
    for load in small + loads:
        load.start()

    barrier = pltpu.get_barrier_semaphore()
    for r in range(1, n):
        pl.semaphore_signal(
            barrier, inc=1, device_id=(lax.rem(me + r, n), tp), device_id_type=MESH
        )
    for r in range(1, nt):
        pl.semaphore_signal(
            barrier, inc=1, device_id=(me, lax.rem(tp + r, nt)), device_id_type=MESH
        )
    for load in small:
        load.wait()
    coef_row[...] = jnp.zeros_like(coef_row)
    for j in range(taps):
        for s in range(3):
            coef_row[3 * j + s : 3 * j + s + 1, :] = sw_ref[j, s : s + 1, :]
    coef_row[3 * taps : 3 * taps + 1, :] = skip_ref[...]
    coef_row[3 * taps + 1 : 3 * taps + 2, :] = gain_ref[...]
    coef_col[...] = coef_row[...].T.reshape(coef_col.shape)
    filt_out[...] = filt_ref[...].astype(bf16)

    def filt_copy(r):
        to = lax.rem(me + r, n)
        return pltpu.make_async_remote_copy(
            src_ref=filt_out.at[pl.ds(pl.multiple_of(to * owned_groups, owned_groups), owned_groups)],
            dst_ref=filt_in.at[me],
            send_sem=filt_send.at[r],
            recv_sem=filt_recv.at[r],
            device_id=(to, tp),
            device_id_type=MESH,
        )

    def prod_copy(q, r):
        to = lax.rem(me + r, n)
        part = pl.ds(q * rows, rows)
        return pltpu.make_async_remote_copy(
            src_ref=prod.at[to, part],
            dst_ref=recv.at[me, part],
            send_sem=prod_send.at[q, r],
            recv_sem=prod_recv.at[q, r],
            device_id=(to, tp),
            device_id_type=MESH,
        )

    def res_copy(q, r):
        to = lax.rem(me + r, n)
        part = pl.ds(q * rows, rows)
        return pltpu.make_async_remote_copy(
            src_ref=res.at[to, part],
            dst_ref=back.at[me, part],
            send_sem=res_send.at[q, r],
            recv_sem=res_recv.at[q, r],
            device_id=(to, tp),
            device_id_type=MESH,
        )

    def fix_copy(r):
        to = lax.rem(me + r, n)
        return pltpu.make_async_remote_copy(
            src_ref=fix_out.at[to],
            dst_ref=fix_in.at[me],
            send_sem=fix_send.at[r],
            recv_sem=fix_recv.at[r],
            device_id=(to, tp),
            device_id_type=MESH,
        )

    edge_copy = pltpu.make_async_remote_copy(
        src_ref=edge_out,
        dst_ref=edge_in,
        send_sem=edge_send,
        recv_sem=edge_recv,
        device_id=(lax.rem(me + 1, n), tp),
        device_id_type=MESH,
    )

    def pick_edges():
        edge = jnp.zeros((16, chan), f32)
        row_id = lax.broadcasted_iota(jnp.int32, (16, width), 0)
        lane_id = lax.broadcasted_iota(jnp.int32, (16, width), 1)
        slot = jnp.where(lane_id < 2, lane_id + 8, lane_id - width + 2)
        at_edge = (lane_id < 2) | (lane_id >= width - 2)
        for s in range(3):
            pick = at_edge & (row_id == 2 * s + slot)
            edge = edge + lax.dot_general(
                pick.astype(f32).astype(bf16),
                st[s].reshape(chan, width),
                (((1,), (1,)), ((), ())),
                preferred_element_type=f32,
            )
        edge_row[...] = edge
        edge_out[...] = jnp.concatenate(
            [edge[:8, : chan // 2], edge[:8, chan // 2 :]], axis=0
        ).astype(bf16)

        @pl.when(me < n - 1)
        def _():
            edge_copy.start()

    def fix_edges():
        fix_row[...] = jnp.zeros_like(fix_row)

        @pl.when(me == 0)
        def _():
            edge_in[...] = jnp.zeros_like(edge_in)

        @pl.when(me > 0)
        def _():
            edge_copy.wait_recv()

        here = edge_row[8:, :]
        left = edge_in[...].astype(f32)
        left = jnp.concatenate([left[:8], left[8:]], axis=1)
        coef = coef_row[...]
        first, second = [], []
        for s in range(3):
            now, later = here[2 * s : 2 * s + 1], here[2 * s + 1 : 2 * s + 2]
            two, one = left[2 * s : 2 * s + 1], left[2 * s + 1 : 2 * s + 2]
            w0, w1, w2 = (coef[3 * j + s : 3 * j + s + 1] for j in range(3))
            first.append(w0 * now + w1 * one + w2 * two)
            second.append(w0 * later + w1 * now + w2 * one)
        lines = [
            first[1] * first[2],
            second[1] * second[2],
            first[0],
            second[0],
        ]
        lines = [line.astype(bf16).astype(f32) for line in lines]
        for o in range(n):
            for h in range(own // 128):
                at = o * own + h * 128
                for p in range(2):
                    fix_out[o, 2 * h + p : 2 * h + p + 1, :] = lines[p][:, at : at + 128]
        for i in range(4):
            fix_row[i : i + 1, :] = lines[i]

    def build_blocks(start, stop):
        @pl.loop(start, stop)
        def _(g):
            line = jnp.concatenate(
                [jnp.zeros((1, width), f32)] + [filt_f32[j, pl.ds(g, 1), :] for j in range(n)],
                axis=1,
            )
            line = jnp.broadcast_to(line, (16, (n + 1) * width))
            base = pltpu.roll(line, 0, 1, stride=1, stride_axis=0).astype(bf16)
            for a in range(width // 16):
                moved = base if a == 0 else pltpu.roll(base, 16 * a, 1)
                toep[g, 16 * a : 16 * (a + 1), :] = moved[:, width:]

    k_id = lax.broadcasted_iota(jnp.int32, (width, 2 * width), 0)
    m_id = lax.broadcasted_iota(jnp.int32, (width, 2 * width), 1)
    source = jnp.where(m_id < width, m_id - 1, m_id - width - 2)
    mover = (k_id == source).astype(f32).astype(bf16)
    for q in range(n_chunks):
        if q == 0:
            loads[0].wait()
        part = slice(q * rows, (q + 1) * rows)
        coef = coef_col[:, part, :].reshape(n * rows, coef_col.shape[2])
        conv = []
        for s in range(3):
            now = st[s, :, part, :].reshape(n * rows, width)
            moved = jnp.dot(now, mover, preferred_element_type=f32)
            conv.append(
                coef[:, s : s + 1] * now.astype(f32)
                + coef[:, 3 + s : 4 + s] * moved[:, :width]
                + coef[:, 6 + s : 7 + s] * moved[:, width:]
            )
        query[:, part, :] = conv[0].astype(bf16).reshape(n, rows, width)
        prod[:, part, :] = (conv[1] * conv[2]).astype(bf16).reshape(n, rows, width)
        if q == 0:
            pl.semaphore_wait(barrier, n - 1 + nt - 1)
            for r in order:
                filt_copy(r).start()
        if q >= depth:
            for r in order:
                prod_copy(q - depth, r).wait_send()
        for r in order:
            prod_copy(q, r).start()
        if q == 0:
            filt_in[me] = filt_out[
                pl.ds(pl.multiple_of(me * owned_groups, owned_groups), owned_groups), :
            ]
            for load in loads[1:]:
                load.wait()
            pick_edges()
        recv[me, part, :] = prod[me, part, :]
        if q == n_chunks // 2 - 1:
            fix_edges()
            for r in order:
                fix_copy(r).start()
            fix_in[me] = fix_out[me]
        if q >= depth:
            if q == depth:
                for r in order:
                    filt_copy(r).wait_recv()
                filt_f32[...] = filt_in[...].astype(f32)
            span = n_chunks - depth
            build_blocks(
                (q - depth) * owned_groups // span, (q + 1 - depth) * owned_groups // span
            )

    for r in order:
        fix_copy(r).wait_recv()
    for h in range(own // 128):
        gathered = jnp.concatenate([fix_in[j, 2 * h : 2 * h + 2, :] for j in range(n)], axis=0)
        gathered = jnp.concatenate([gathered, jnp.zeros((width - 2 * n, 128), f32)], axis=0).T
        for j in range(n):
            near = gathered if j == 0 else pltpu.roll(gathered, width - 2 * j, 1)
            fix_col[j, h * 128 : (h + 1) * 128, :] = near
    head = lax.broadcasted_iota(jnp.int32, (n * per_group, width), 1) < 2

    for q in range(n_chunks):
        for r in order:
            prod_copy(q, r).wait_recv()
        per_chunk = rows // per_group

        @pl.loop(0, per_chunk, unroll=True)
        def _(k):
            place = pl.ds(pl.multiple_of(q * rows + k * per_group, per_group), per_group)
            block = recv[:, place, :].reshape(n * per_group, width).astype(f32)
            fixed = fix_col[:, place, :].reshape(n * per_group, width)
            block = jnp.where(head, fixed, block).astype(bf16)
            half = n // 2
            taps_of = toep[q * per_chunk + k]
            near = jnp.dot(block, taps_of[:, : half * width], preferred_element_type=f32)
            far = jnp.dot(
                block[: half * per_group], taps_of[:, half * width :], preferred_element_type=f32
            )

            def term(j, d):
                full, at = (near, d) if d < half else (far, d - half)
                return full[
                    j * per_group : (j + 1) * per_group, at * width : (at + 1) * width
                ]

            for i in range(n):
                total = term(0, i)
                for j in range(1, i + 1):
                    total = total + term(j, i - j)
                res[i, place, :] = total.astype(bf16)

        for r in order:
            res_copy(q, r).start()
        part = slice(q * rows, (q + 1) * rows)
        back[me, part, :] = res[me, part, :]

    local_col[...] = fix_row[...].T.reshape(local_col.shape)
    head = lax.broadcasted_iota(jnp.int32, (n * rows, width), 1) < 2
    for q in range(n_chunks):
        part = slice(q * rows, (q + 1) * rows)
        skip = coef_col[:, part, :].reshape(n * rows, coef_col.shape[2])[:, 3 * taps : 3 * taps + 1]
        fixed = local_col[:, part, :].reshape(n * rows, width)
        value = prod[:, part, :].reshape(n * rows, width).astype(f32)
        direct[:, part, :] = (skip * jnp.where(head, fixed, value)).reshape(n, rows, width)
        fixed = pltpu.roll(fixed, width - 2, 1)
        value = query[:, part, :].reshape(n * rows, width).astype(f32)
        query[:, part, :] = jnp.where(head, fixed, value).astype(bf16).reshape(n, rows, width)

    squares = jnp.zeros((8, width), f32)
    for q in range(n_chunks):
        part = slice(q * rows, (q + 1) * rows)
        for r in order:
            res_copy(q, r).wait_recv()
        far = back[:, part, :].astype(f32)
        gated = (query[:, part, :].astype(f32) * (far + direct[:, part, :])).astype(bf16)
        gated = gated.astype(f32)
        gain = coef_col[:, part, :][:, :, 3 * taps + 1 : 3 * taps + 2]
        direct[:, part, :] = gated * gain
        squares = squares + jnp.sum((gated * gated).reshape(n * rows // 8, 8, width), axis=0)
    sq_out[...] = squares

    def sq_copy(r):
        return pltpu.make_async_remote_copy(
            src_ref=sq_out,
            dst_ref=sq_in.at[tp],
            send_sem=sq_send.at[r],
            recv_sem=sq_recv.at[r],
            device_id=(me, lax.rem(tp + r, nt)),
            device_id_type=MESH,
        )

    for r in range(1, nt):
        sq_copy(r).start()
    sq_in[tp] = squares
    for r in order:
        filt_copy(r).wait_send()
        fix_copy(r).wait_send()
        for q in range(n_chunks):
            if q >= n_chunks - depth:
                prod_copy(q, r).wait_send()
            res_copy(q, r).wait_send()

    @pl.when(me < n - 1)
    def _():
        edge_copy.wait_send()

    for r in range(1, nt):
        sq_copy(r).wait_recv()
    total = jnp.sum(jnp.sum(sq_in[...], axis=0), axis=0, keepdims=True)
    inverse = 1.0 / jnp.sqrt(total / (chan * nt) + 1e-05)
    stores = []
    for part in range(4):
        some = pl.ds(part * n // 4, n // 4)
        out_vmem[some] = (direct[some] * inverse).astype(bf16)
        stores.append(
            pltpu.make_async_copy(out_vmem.at[some], out_ref.at[some], store_sem.at[part])
        )
        stores[-1].start()
    for store in stores:
        store.wait()
    for r in range(1, nt):
        sq_copy(r).wait_send()


def fused_shards(streams, short_weight, filters, skip_gain, norm_gain):
    n = lax.axis_size("ctx")
    nt = lax.axis_size("tp")
    chan, width = streams.shape[1:]
    own = chan // n
    owned_groups = filters.shape[0] // n
    n_chunks = 4
    bf16, f32 = jnp.bfloat16, jnp.float32
    dma = pltpu.SemaphoreType.DMA
    slab = pltpu.VMEM((n, own, width), bf16)
    wide_slab = pltpu.VMEM((n, own, width), f32)
    result = pl.pallas_call(
        functools.partial(kernel, n, nt, n_chunks),
        out_shape=jax.ShapeDtypeStruct((n, own, width), bf16),
        in_specs=[pl.BlockSpec(memory_space=pltpu.HBM)] * 5,
        out_specs=pl.BlockSpec(memory_space=pltpu.HBM),
        scratch_shapes=[
            pltpu.VMEM((3, n, own, width), bf16),
            pltpu.VMEM(short_weight.shape, f32),
            pltpu.VMEM(filters.shape, f32),
            pltpu.VMEM((1, chan), f32),
            pltpu.VMEM((1, chan), f32),
            pltpu.VMEM((16, chan), f32),
            pltpu.VMEM((16, chan // 2), bf16),
            pltpu.VMEM((16, chan // 2), bf16),
            pltpu.VMEM((n, own // 64, 128), f32),
            pltpu.VMEM((n, own // 64, 128), f32),
            pltpu.VMEM((128, chan), f32),
            wide_slab,
            wide_slab,
            wide_slab,
            slab,
            pltpu.VMEM((16, chan), f32),
            pltpu.VMEM((n, own, 16), f32),
            pltpu.VMEM((filters.shape[0], width), bf16),
            pltpu.VMEM((n, owned_groups, width), bf16),
            pltpu.VMEM((n, owned_groups, width), f32),
            pltpu.VMEM((owned_groups, width, n * width), bf16),
            slab,
            slab,
            slab,
            slab,
            slab,
            pltpu.VMEM((8, width), f32),
            pltpu.VMEM((nt, 8, width), f32),
            dma((4 + n_chunks,)),
            dma((4,)),
            dma,
            dma,
            dma((n,)),
            dma((n,)),
            dma((n,)),
            dma((n,)),
            dma((n_chunks, n)),
            dma((n_chunks, n)),
            dma((n_chunks, n)),
            dma((n_chunks, n)),
            dma((nt,)),
            dma((nt,)),
        ],
        compiler_params=pltpu.CompilerParams(
            collective_id=0, has_side_effects=True, vmem_limit_bytes=63 * 1024 * 1024
        ),
        name="hyena",
    )(
        streams.reshape(3, n, own, width),
        short_weight,
        filters,
        skip_gain.reshape(1, chan),
        norm_gain.reshape(1, chan),
    )
    return result.reshape(chan, width)


def solution(mesh):
    in_specs = (P(None, "tp", "ctx"), P(None, None, "tp"), P("tp", "ctx"), P("tp"), P("tp"))
    out_specs = P("tp", "ctx")
    body = fused_shards if mesh.shape["ctx"] <= 16 else shards
    return jax.shard_map(body, mesh=mesh, in_specs=in_specs, out_specs=out_specs, check_vma=False)
```
